32 devices in a mesh: expert: 16 (over z, y, x), tensor: 2 (over core).
Axes of the slice: x: 2, y: 2, z: 4, core: 2. Of those that a mesh axis runs over, the one named last changes fastest.
Arguments:
- tokens: bfloat16 [16384, 1024], P('expert'), may hold values from -6 to 6
- segment_ids: int32 [16384], P('expert'), may hold values from 0 to 7, as said below
- router_logits: float32 [16384, 16], P('expert'), may hold values from -3 to 3
- expert_ids: int32 [16384, 8], P('expert'), may hold values from 0 to 15, all different within a row; in each aligned block of 1024 rows (0 to 1023, 1024 to 2047, ...) at most 768 rows name the same one
- gain_attn: float32 [1024], replicated, may hold values from 0.1 to 1.9
- w_query: bfloat16 [1024, 1024], P(None, 'tensor'), may hold values from -0.1875 to 0.1875
- key_matrix: bfloat16 [1024, 512], P(None, 'tensor'), may hold values from -0.1875 to 0.1875
- value_matrix: bfloat16 [1024, 512], P(None, 'tensor'), may hold values from -0.1875 to 0.1875
- w_out: bfloat16 [1024, 1024], P('tensor'), may hold values from -0.75 to 0.75
- gain_mlp: float32 [1024], replicated, may hold values from 0.1 to 1.9
- w_gate: bfloat16 [16, 1024, 512], P('expert', None, 'tensor'), may hold values from -0.1875 to 0.1875
- w_up: bfloat16 [16, 1024, 512], P('expert', None, 'tensor'), may hold values from -0.1875 to 0.1875
- w_down: bfloat16 [16, 512, 1024], P('expert', 'tensor'), may hold values from -0.75 to 0.75
- out_grad: float32 [16384, 1024], P('expert', 'tensor'), may hold values from -6 to 6
Outputs:
- block_out: bfloat16 [16384, 1024], P('expert', 'tensor')
- grad_tokens: float32 [16384, 1024], P('expert', 'tensor')
- grad_logits: float32 [16384, 16], P('expert')
- grad_gain_attn: float32 [1024], P('tensor')
- grad_query: float32 [1024, 1024], P(None, 'tensor')
- grad_key: float32 [1024, 512], P(None, 'tensor')
- grad_value: float32 [1024, 512], P(None, 'tensor')
- grad_out: float32 [1024, 1024], P('tensor')
- grad_gain_mlp: float32 [1024], P('tensor')
- grad_gate: float32 [16, 1024, 512], P('expert', None, 'tensor')
- grad_up: float32 [16, 1024, 512], P('expert', None, 'tensor')
- grad_down: float32 [16, 512, 1024], P('expert', 'tensor')
The draws below stay inside these ranges and needn't reach their ends.
Inputs may be any that keep to these rules, and one draw needn't show every extreme that they name: `segment_ids`: within each block of 1024 rows the ids start at 0 and rise by 0 or 1 from row to row; a run of equal ids is one sequence; a block holds 1 to 8 sequences; some block holds a single sequence of 1024 tokens and some block holds eight. `expert_ids`: each row names 8 different experts; within the rows of one index of the expert axis no expert is named by more than 768 rows.
All inputs are finite; a program needn't handle non-finite values.
Results may differ from the reference program's by a relative error of at most 0.023.
Values may be sent and summed in bfloat16 or wider, within the bound.
No kernel may reach another device: no remote copies, remote signals or barrier semaphores. Data moves between devices by JAX's collectives and lax.ppermute only.
A program may use at most 448 MiB of HBM per device.

```python
import math
import jax
import jax.numpy as jnp
import numpy as np
from jax import lax

MODEL_DIM = 1024
QUERY_HEADS = 16
KEY_VALUE_HEADS = 8
HEAD_SIZE = 64
FFE = 512
TOP = 8
TOK_DEV = 1024
EXPERTS = 16
TOKEN_ROWS = 16384
CAP = 768
N_EXPERT = 16


def draw_segment_ids(key, part):
    key = jax.random.fold_in(key, 7)
    key_count, key_whole, key_place = jax.random.split(key, 3)
    block_index = jnp.arange(N_EXPERT, dtype=jnp.int32)
    cut_counts = jax.random.randint(key_count, (N_EXPERT,), 0, 8)
    whole_block = jax.random.randint(key_whole, (), 0, N_EXPERT)
    busy_block = (whole_block + 1) % N_EXPERT
    cut_counts = jnp.where(block_index == busy_block, 7, cut_counts)
    cut_counts = jnp.where(block_index == whole_block, 0, cut_counts)
    place_keys = jax.random.split(key_place, N_EXPERT)
    orders = jax.vmap(lambda one_key: jax.random.permutation(one_key, TOK_DEV - 1))(place_keys)
    cut_places = orders[:, :7].astype(jnp.int32) + 1
    used = (jnp.arange(7, dtype=jnp.int32)[None, :] < cut_counts[:, None]).astype(jnp.int32)
    row_index = jnp.arange(TOK_DEV, dtype=jnp.int32)
    marks = jnp.sum((cut_places[:, :, None] == row_index[None, None, :]).astype(jnp.int32) * used[:, :, None], axis=1)
    return jnp.cumsum(marks, axis=1).reshape(-1).astype(jnp.int32)


def level_of(rng, extent, pieces, smallest, top_value):
    level, own = 1.0, jax.random.fold_in(rng, 6)
    for axis_at, parts in pieces:
        heights = jnp.exp(jax.random.uniform(jax.random.fold_in(own, axis_at), (parts,), jnp.float32, smallest / len(pieces), top_value / len(pieces)))
        level = level * jnp.repeat(heights, extent[axis_at] // parts).reshape([-1 if axis == axis_at else 1 for axis in range(len(extent))])
    return level


def shared_out(rng, own, number, rows, number_of, top, most, slope):
    sequence = jax.random.permutation(rng, number_of)
    crowded, ordinary = shares(number_of, rows * top, most, slope, True), shares(number_of, rows * top, most, slope, False)
    places = jnp.arange(number_of)

    def named(lengths, rotation):
        used = int((lengths > 0).sum())
        fixed = max(1, used // 4)
        shifted = fixed + (places - fixed + rotation * (used - fixed)) % max(1, number_of - fixed)
        return jnp.zeros((number_of,), jnp.int32).at[sequence[jnp.where(places < fixed, places, shifted)]].set(jnp.asarray(lengths, jnp.int32))

    lengths = jnp.where(number % 4 == 0, named(crowded, number // 4), named(ordinary, number - number // 4 - 1))
    mixed = jax.random.permutation(jax.random.fold_in(own, 3), number_of)
    donor, taker = mixed[0:number_of // 2 * 2:2], mixed[1:number_of // 2 * 2:2]
    margin = jnp.minimum(lengths[donor] - 1, most - lengths[taker]) // 2
    margin = jnp.where((donor == sequence[0]) | (taker == sequence[0]) | (lengths[taker] == 0), 0, jnp.maximum(margin, 0))
    shifted = jax.random.randint(jax.random.fold_in(own, 4), (number_of // 2,), 0, 1 << 20) % (margin + 1)
    lengths = lengths.at[donor].add(-shifted).at[taker].add(shifted)
    labels = jnp.searchsorted(jnp.cumsum(lengths), jnp.arange(rows * top), side="right").astype(jnp.int32)
    grid = labels.reshape(top, rows).T
    grid = grid[jax.random.permutation(jax.random.fold_in(own, 1), rows)]
    rotation = jax.random.randint(jax.random.fold_in(own, 2), (rows, 1), 0, top)
    return jnp.take_along_axis(grid, (jnp.arange(top)[None, :] + rotation) % top, axis=1)


def shares(count, total, reach, lean, full):
    portions = [(1 << 20) // math.isqrt(standing ** lean) + 1 for standing in range(1, count + 1)]
    largest = reach if full else min(reach, max(-(-total // count), total * portions[0] // sum(portions)))
    least = 1 if total - largest >= count - 1 else 0
    holding, spare = [largest] + [least] * (count - 1), total - largest - least * (count - 1)
    while spare > 0:
        candidates = [i for i in range(1, count) if holding[i] < largest] or [i for i in range(1, count) if holding[i] < reach]
        mass, budget = sum([portions[i] for i in candidates]), spare
        for i in candidates:
            more = min(reach - holding[i], max(1, budget * portions[i] // mass), spare)
            holding[i] = holding[i] + more
            spare = spare - more
    return np.array(holding)


def gaussian(own_key, extent, deviation, most, cuts=(), held_as=jnp.bfloat16):
    entries = deviation * jax.random.normal(own_key, extent, jnp.float32)
    if cuts:
        entries = entries * level_of(own_key, extent, cuts, -0.22, 0.18)
    return jnp.clip(entries, -most, most).astype(held_as)


def setup_inputs(seed: int = 0) -> dict:
    streams_of = jax.random.split(jax.random.key(seed), 15)
    tokens = gaussian(streams_of[0], (TOKEN_ROWS, MODEL_DIM), 1.0, 6.0, ((0, 16),))
    segment_ids = draw_segment_ids(jax.random.fold_in(streams_of[14], 71), 0)
    router_logits = gaussian(streams_of[2], (TOKEN_ROWS, EXPERTS), 0.5, 3.0, ((0, 16),), jnp.float32)
    expert_ids_keys = jax.random.split(jax.random.fold_in(streams_of[3], 1), TOKEN_ROWS // TOK_DEV)
    expert_ids_turns = jax.random.permutation(jax.random.fold_in(streams_of[3], 3), TOKEN_ROWS // TOK_DEV)
    expert_ids = jax.vmap(lambda own, number: shared_out(jax.random.fold_in(streams_of[3], 2), own, number, TOK_DEV, EXPERTS, TOP, CAP, 2))(expert_ids_keys, expert_ids_turns).reshape((TOKEN_ROWS, TOP))
    gain_attn = jnp.clip(1.0 + 0.18 * jax.random.normal(streams_of[4], (MODEL_DIM,), jnp.float32), 0.1, 1.9)
    w_query = gaussian(streams_of[5], (MODEL_DIM, QUERY_HEADS * HEAD_SIZE), MODEL_DIM ** -0.5, 0.1875, ((1, 2),))
    key_matrix = gaussian(streams_of[6], (MODEL_DIM, KEY_VALUE_HEADS * HEAD_SIZE), MODEL_DIM ** -0.5, 0.1875, ((1, 2),))
    value_matrix = gaussian(streams_of[7], (MODEL_DIM, KEY_VALUE_HEADS * HEAD_SIZE), MODEL_DIM ** -0.5, 0.1875, ((1, 2),))
    w_out = gaussian(streams_of[8], (QUERY_HEADS * HEAD_SIZE, MODEL_DIM), (QUERY_HEADS * HEAD_SIZE // 16) ** -0.5, 0.75, ((0, 2),))
    gain_mlp = jnp.clip(1.0 + 0.18 * jax.random.normal(streams_of[9], (MODEL_DIM,), jnp.float32), 0.1, 1.9)
    w_gate = gaussian(streams_of[10], (EXPERTS, MODEL_DIM, FFE), MODEL_DIM ** -0.5, 0.1875, ((0, 16), (2, 2)))
    w_up = gaussian(streams_of[11], (EXPERTS, MODEL_DIM, FFE), MODEL_DIM ** -0.5, 0.1875, ((0, 16), (2, 2)))
    w_down = gaussian(streams_of[12], (EXPERTS, FFE, MODEL_DIM), (FFE // 8) ** -0.5, 0.75, ((0, 16), (1, 2)))
    out_grad = gaussian(streams_of[13], (TOKEN_ROWS, MODEL_DIM), 1.0, 6.0, ((0, 16), (1, 2)), jnp.float32)
    return {"tokens": tokens, "segment_ids": segment_ids, "router_logits": router_logits, "expert_ids": expert_ids, "gain_attn": gain_attn, "w_query": w_query, "key_matrix": key_matrix, "value_matrix": value_matrix, "w_out": w_out, "gain_mlp": gain_mlp, "w_gate": w_gate, "w_up": w_up, "w_down": w_down, "out_grad": out_grad}


EPS = 1e-06
THETA = 10000.0
NEG = -1e+30
HIGH = lax.Precision.HIGHEST

@jax.custom_vjp
def lower_half(v):
    return lax.optimization_barrier(v.astype(jnp.bfloat16)).astype(jnp.float32)

@jax.custom_vjp
def low_back(v):
    return v

def low_keep(v):
    return (lower_half(v), None)

def low_pass(kept, grad):
    return (grad,)

def back_keep(v):
    return (v, None)

def back_low(kept, grad):
    return (lower_half(grad),)
lower_half.defvjp(low_keep, low_pass)
low_back.defvjp(back_keep, back_low)

def positions(segment_row):
    row_index = jnp.arange(segment_row.shape[0], dtype=jnp.int32)
    before = jnp.concatenate([segment_row[:1] - 1, segment_row[:-1]])
    starts = lax.cummax(jnp.where(segment_row != before, row_index, 0), axis=0)
    return row_index - starts

def rope_tables(places, head_dim):
    half_dim = head_dim // 2
    freq_row = jnp.power(THETA, -2.0 * jnp.arange(half_dim, dtype=jnp.float32) / head_dim)
    angles = places.astype(jnp.float32)[:, None] * freq_row[None, :]
    return (jnp.cos(angles), jnp.sin(angles))

def rotate_pairs(value_rows, cosine_table, sine_table):
    half_dim = value_rows.shape[-1] // 2
    first = value_rows[..., :half_dim]
    second = value_rows[..., half_dim:]
    cos_b = cosine_table[:, None, :]
    sin_b = sine_table[:, None, :]
    return jnp.concatenate([first * cos_b - second * sin_b, second * cos_b + first * sin_b], axis=-1)

def rms(value_rows, gain):
    return value_rows * lax.rsqrt(lax.optimization_barrier(jnp.mean(value_rows * value_rows, axis=-1, keepdims=True)) + EPS) * gain

def slot_tables(expert_ids):
    pair_ids = expert_ids.reshape(N_EXPERT, TOK_DEV * TOP)
    onehot = (pair_ids[:, :, None] == jnp.arange(EXPERTS, dtype=jnp.int32)[None, None, :]).astype(jnp.int32)
    rank_run = jnp.cumsum(onehot, axis=1) - 1
    slot_in = lax.optimization_barrier(jnp.sum(rank_run * onehot, axis=2))
    group_base = (jnp.arange(N_EXPERT, dtype=jnp.int32) * CAP)[:, None]
    dest_slot = (pair_ids * (N_EXPERT * CAP) + group_base + slot_in).reshape(-1)
    pair_index = jnp.arange(TOKEN_ROWS * TOP, dtype=jnp.int32)
    slot_count = EXPERTS * N_EXPERT * CAP
    slot_pairs = jnp.zeros((slot_count,), jnp.int32).at[dest_slot].set(pair_index)
    slot_live = jnp.zeros((slot_count,), jnp.float32).at[dest_slot].set(1.0)
    return (slot_pairs.reshape(EXPERTS, N_EXPERT * CAP), slot_live.reshape(EXPERTS, N_EXPERT * CAP))

def attend(packed):
    q_group, k_group, v_group, seg_row = packed
    query_group_size = QUERY_HEADS // KEY_VALUE_HEADS
    keys_all = jnp.repeat(k_group, query_group_size, axis=1)
    vals_all = jnp.repeat(v_group, query_group_size, axis=1)
    raw = low_back(jnp.einsum('qhd,khd->hqk', q_group, keys_all, precision=HIGH))
    row_index = jnp.arange(TOK_DEV)
    allowed = (seg_row[:, None] == seg_row[None, :]) & (row_index[:, None] >= row_index[None, :])
    scores = jnp.where(allowed[None], raw * HEAD_SIZE ** (-0.5), NEG)
    probs = lower_half(jax.nn.softmax(scores, axis=-1))
    return jnp.einsum('hqk,khd->qhd', probs, vals_all, precision=HIGH)

def reference(tokens, segment_ids, router_logits, expert_ids, gain_attn, w_query, key_matrix, value_matrix, w_out, gain_mlp, w_gate, w_up, w_down, out_grad):
    seg_groups = segment_ids.reshape(N_EXPERT, TOK_DEV)
    places = jax.vmap(positions)(seg_groups).reshape(TOKEN_ROWS)
    cosine_table, sine_table = rope_tables(places, HEAD_SIZE)
    slot_pairs, slot_live = slot_tables(expert_ids)

    def grouped(array):
        return array.reshape((N_EXPERT, TOK_DEV) + array.shape[1:])

    def forward(x_in, g_attn, wq_in, wk_in, wv_in, wo_in, g_mlp, logits_in, wg_in, wu_in, wd_in):
        attn_in = lower_half(rms(x_in, g_attn))
        q_pre = low_back(jnp.dot(attn_in, wq_in, precision=HIGH))
        key_projected = low_back(jnp.dot(attn_in, wk_in, precision=HIGH))
        value_rows_used = lower_half(low_back(jnp.dot(attn_in, wv_in, precision=HIGH)))
        queries = lower_half(rotate_pairs(q_pre.reshape(TOKEN_ROWS, QUERY_HEADS, HEAD_SIZE), cosine_table, sine_table))
        rotated_keys = lower_half(rotate_pairs(key_projected.reshape(TOKEN_ROWS, KEY_VALUE_HEADS, HEAD_SIZE), cosine_table, sine_table))
        value_rows = value_rows_used.reshape(TOKEN_ROWS, KEY_VALUE_HEADS, HEAD_SIZE)
        attn_vals = lax.map(jax.checkpoint(attend), (grouped(queries), grouped(rotated_keys), grouped(value_rows), seg_groups))
        o_used = lower_half(low_back(attn_vals.reshape(TOKEN_ROWS, QUERY_HEADS * HEAD_SIZE)))
        mixed = x_in + low_back(jnp.dot(o_used, wo_in, precision=HIGH))
        mlp_in = lower_half(rms(mixed, g_mlp))
        chosen = jnp.take_along_axis(logits_in, expert_ids, axis=1)
        gates = jax.nn.softmax(chosen, axis=1).reshape(-1)

        def expert_step(total_out, packed):
            gate_w, up_w, down_w, pair_row, live_row = packed
            tok_index = pair_row // TOP
            slot_rows = low_back(mlp_in[tok_index]) * live_row[:, None]
            gate_pre = low_back(jnp.dot(slot_rows, gate_w, precision=HIGH))
            up_pre = low_back(jnp.dot(slot_rows, up_w, precision=HIGH))
            hidden_act = lower_half(jax.nn.silu(gate_pre) * up_pre)
            slot_out = lower_half(low_back(jnp.dot(hidden_act, down_w, precision=HIGH)))
            slot_weight = gates[pair_row] * live_row
            return (total_out.at[tok_index].add(slot_weight[:, None] * slot_out), None)
        expert_sum, _ = lax.scan(jax.checkpoint(expert_step), jnp.zeros((TOKEN_ROWS, MODEL_DIM), jnp.float32), (wg_in, wu_in, wd_in, slot_pairs, slot_live))
        return mixed + expert_sum
    inputs = (tokens.astype(jnp.float32), gain_attn, w_query.astype(jnp.float32), key_matrix.astype(jnp.float32), value_matrix.astype(jnp.float32), w_out.astype(jnp.float32), gain_mlp, router_logits, w_gate.astype(jnp.float32), w_up.astype(jnp.float32), w_down.astype(jnp.float32))
    result, pull = jax.vjp(forward, *inputs)
    grads = pull(out_grad)
    return (result.astype(jnp.bfloat16), grads[0], grads[7], grads[1], grads[2], grads[3], grads[4], grads[5], grads[6], grads[8], grads[9], grads[10])
```

```python
import functools

import jax
import jax.numpy as jnp
from jax import lax
from jax.experimental import pallas as pl
from jax.experimental.pallas import tpu as pltpu
from jax.sharding import PartitionSpec as P

HEAD_SIZE = 64
EPS = 1e-06
THETA = 10000.0
NEG = -1e30
PLANE = 4
F32 = jnp.float32
BF16 = jnp.bfloat16
NT = (((1,), (1,)), ((), ()))
TN = (((0,), (0,)), ((), ()))


def dot(a, b):
    return jnp.dot(a, b, preferred_element_type=F32)


def dot_nt(a, b):
    return lax.dot_general(a, b, NT, preferred_element_type=F32)


def dot_tn(a, b):
    return lax.dot_general(a, b, TN, preferred_element_type=F32)


def attn_mask(start, row_start, block, keys):
    first = start[:, row_start : row_start + block]
    first = jnp.concatenate([first, first], axis=1)
    key_at = lax.broadcasted_iota(jnp.int32, (keys, 2 * block), 0)
    lane = lax.broadcasted_iota(jnp.int32, (1, 2 * block), 1)
    row_at = row_start + jnp.where(lane >= block, lane - block, lane)
    return (key_at >= first) & (key_at <= row_at)


def rope(x, c, s):
    half = x.shape[0] // 2
    a, b = x[:half], x[half:]
    return jnp.concatenate([a * c - b * s, b * c + a * s], axis=0)


def attn_fwd_kernel(block, q_ref, k_ref, v_ref, cos_ref, sin_ref, start_ref, qo_ref, ko_ref, o_ref, lse_ref):
    hd = HEAD_SIZE
    n = k_ref.shape[1]
    c, s = cos_ref[...], sin_ref[...]
    k_rot = rope(k_ref[...], c, s)
    ko_ref[...] = k_rot.astype(BF16)
    keys = k_rot.T.astype(BF16)
    q0 = rope(q_ref[0:hd], c, s).astype(BF16)
    q1 = rope(q_ref[hd : 2 * hd], c, s).astype(BF16)
    qo_ref[0:hd] = q0
    qo_ref[hd : 2 * hd] = q1
    start = start_ref[...]
    for r0 in range(0, n, block):
        cn = r0 + block
        qb = jnp.concatenate([q0[:, r0:cn], q1[:, r0:cn]], axis=1) * jnp.asarray(hd**-0.5, BF16)
        scores = dot(keys[:cn], qb)
        scores = jnp.where(attn_mask(start, r0, block, cn), scores, NEG)
        peak = jnp.max(scores, axis=0, keepdims=True)
        p = jnp.exp(scores - peak)
        total = jnp.sum(p, axis=0, keepdims=True)
        o = dot(v_ref[:, :cn], p.astype(BF16)) / total
        o_ref[0:hd, r0:cn] = o[:, :block].astype(BF16)
        o_ref[hd : 2 * hd, r0:cn] = o[:, block:].astype(BF16)
        lse = peak + jnp.log(total)
        lse_ref[0, 0:1, r0:cn] = lse[:, :block]
        lse_ref[0, 1:2, r0:cn] = lse[:, block:]


def attn_bwd_kernel(
    block, q_ref, k_ref, v_ref, do_ref, lse_ref, cos_ref, sin_ref, start_ref, dq_ref, dk_ref, dv_ref, dk_acc, dv_acc
):
    hd = HEAD_SIZE
    n = k_ref.shape[1]
    c, s = cos_ref[...], sin_ref[...]
    keys = k_ref[...].astype(F32).T.astype(BF16)
    vals = v_ref[...].astype(F32).T.astype(BF16)
    start = start_ref[...]
    dk_acc[...] = jnp.zeros_like(dk_acc)
    dv_acc[...] = jnp.zeros_like(dv_acc)
    scale = hd**-0.5
    for r0 in range(0, n, block):
        cn = r0 + block
        qb = jnp.concatenate([q_ref[0:hd, r0:cn], q_ref[hd : 2 * hd, r0:cn]], axis=1)
        gb = jnp.concatenate([do_ref[0:hd, r0:cn], do_ref[hd : 2 * hd, r0:cn]], axis=1)
        lse = jnp.concatenate([lse_ref[0, 0:1, r0:cn], lse_ref[0, 1:2, r0:cn]], axis=1)
        scores = dot(keys[:cn], qb * jnp.asarray(scale, BF16))
        p = jnp.exp(jnp.where(attn_mask(start, r0, block, cn), scores, NEG) - lse)
        dv_acc[:, :cn] += dot_nt(gb, p.astype(BF16))
        dp = dot(vals[:cn], gb)
        delta = jnp.sum(p * dp, axis=0, keepdims=True)
        ds = (p * (dp - delta) * scale).astype(BF16)
        dq = dot(k_ref[:, :cn], ds)
        dk_acc[:, :cn] += dot_nt(qb, ds)
        cb, sb = c[:, r0:cn], -s[:, r0:cn]
        dq_ref[0:hd, r0:cn] = rope(dq[:, :block], cb, sb).astype(BF16)
        dq_ref[hd : 2 * hd, r0:cn] = rope(dq[:, block:], cb, sb).astype(BF16)
    dk_ref[...] = rope(dk_acc[...], c, -s).astype(BF16)
    dv_ref[...] = dv_acc[...].astype(BF16)


def attn_cost(heads, n, products):
    return pl.CostEstimate(
        flops=products * heads * n * n * HEAD_SIZE * 2, bytes_accessed=8 * heads * n * HEAD_SIZE, transcendentals=heads * n * n
    )


def attn_forward(q_t, k_t, v_t, cos_t, sin_t, start):
    n = q_t.shape[1]
    hd = HEAD_SIZE
    kv = k_t.shape[0] // hd
    block = min(256, n)
    pair = pl.BlockSpec((2 * hd, n), lambda h: (h, 0))
    one = pl.BlockSpec((hd, n), lambda h: (h, 0))
    table = pl.BlockSpec((hd // 2, n), lambda h: (0, 0))
    return pl.pallas_call(
        functools.partial(attn_fwd_kernel, block),
        grid=(kv,),
        in_specs=[pair, one, one, table, table, pl.BlockSpec((1, n), lambda h: (0, 0))],
        out_specs=[pair, one, pair, pl.BlockSpec((1, 2, n), lambda h: (h, 0, 0))],
        out_shape=[
            jax.ShapeDtypeStruct(q_t.shape, BF16),
            jax.ShapeDtypeStruct(k_t.shape, BF16),
            jax.ShapeDtypeStruct(q_t.shape, BF16),
            jax.ShapeDtypeStruct((kv, 2, n), F32),
        ],
        compiler_params=pltpu.CompilerParams(vmem_limit_bytes=48 * 2**20),
        cost_estimate=attn_cost(2 * kv, n, 4),
        name="attn_forward",
    )(q_t, k_t, v_t, cos_t, sin_t, start)


def attn_backward(q_t, k_t, v_t, do_t, lse, cos_t, sin_t, start):
    n = q_t.shape[1]
    hd = HEAD_SIZE
    kv = k_t.shape[0] // hd
    block = min(256, n)
    pair = pl.BlockSpec((2 * hd, n), lambda h: (h, 0))
    one = pl.BlockSpec((hd, n), lambda h: (h, 0))
    table = pl.BlockSpec((hd // 2, n), lambda h: (0, 0))
    return pl.pallas_call(
        functools.partial(attn_bwd_kernel, block),
        grid=(kv,),
        in_specs=[
            pair,
            one,
            one,
            pair,
            pl.BlockSpec((1, 2, n), lambda h: (h, 0, 0)),
            table,
            table,
            pl.BlockSpec((1, n), lambda h: (0, 0)),
        ],
        out_specs=[pair, one, one],
        out_shape=[
            jax.ShapeDtypeStruct(q_t.shape, BF16),
            jax.ShapeDtypeStruct(k_t.shape, BF16),
            jax.ShapeDtypeStruct(k_t.shape, BF16),
        ],
        scratch_shapes=[pltpu.VMEM((hd, n), F32), pltpu.VMEM((hd, n), F32)],
        compiler_params=pltpu.CompilerParams(vmem_limit_bytes=48 * 2**20),
        cost_estimate=attn_cost(2 * kv, n, 10),
        name="attn_backward",
    )(q_t, k_t, v_t, do_t, lse, cos_t, sin_t, start)


def moe_kernel(first, pieces, expert_ref, *refs):
    refs = list(refs)
    x_ref, g_ref, gates_ref = refs[:3]
    wg, wu, wd = refs[3 : 3 + pieces], refs[3 + pieces : 3 + 2 * pieces], refs[3 + 2 * pieces : 3 + 3 * pieces]
    refs = refs[3 + 3 * pieces :]
    if not first:
        out_in, dx_in, dgate_in = refs[:3]
        refs = refs[3:]
    out_ref, dx_ref, dgate_ref = refs[:3]
    refs = refs[3:]
    og, ou, od = refs[:pieces], refs[pieces : 2 * pieces], refs[2 * pieces : 3 * pieces]
    acc_g, acc_u, acc_d = refs[3 * pieces :]
    step, steps = pl.program_id(0), pl.num_programs(0)

    @pl.when(step == 0)
    def _():
        acc_g[...] = jnp.zeros_like(acc_g)
        acc_u[...] = jnp.zeros_like(acc_u)
        acc_d[...] = jnp.zeros_like(acc_d)

    x, g = x_ref[...], g_ref[...]
    here = lax.broadcasted_iota(jnp.int32, gates_ref.shape, 1) == expert_ref[0]
    gate = jnp.sum(jnp.where(here, gates_ref[...], 0.0), axis=1, keepdims=True)
    x_t = x.T
    row_sum = None
    for i in range(pieces):
        gate_pre = dot(x, wg[i][...])
        up_pre = dot(x, wu[i][...])
        d_hidden = dot_nt(g, wd[i][...])
        sig = jax.nn.sigmoid(gate_pre)
        silu = gate_pre * sig
        act = silu * up_pre
        part = jnp.sum(act * d_hidden, axis=1, keepdims=True)
        row_sum = part if row_sum is None else row_sum + part
        act_w = (act * gate).astype(BF16)
        d_hidden = d_hidden * gate
        d_up = (d_hidden * silu).astype(BF16)
        d_gate = (d_hidden * up_pre * sig * (1.0 + gate_pre * (1.0 - sig))).astype(BF16)
        out_term = dot(act_w, wd[i][...])
        dx_term = dot_nt(d_gate, wg[i][...]) + dot_nt(d_up, wu[i][...])
        if i == 0 and first:
            out_ref[...] = out_term
            dx_ref[...] = dx_term
        elif i == 0:
            out_ref[...] = out_in[...] + out_term
            dx_ref[...] = dx_in[...] + dx_term
        else:
            out_ref[...] += out_term
            dx_ref[...] += dx_term
        acc_g[i] += dot(x_t, d_gate)
        acc_u[i] += dot(x_t, d_up)
        acc_d[i] += dot_tn(act_w, g)
    dgate_term = jnp.where(here, row_sum, 0.0)
    dgate_ref[...] = dgate_term if first else dgate_in[...] + dgate_term

    @pl.when(step == steps - 1)
    def _():
        for i in range(pieces):
            og[i][...] = acc_g[i].astype(BF16)
            ou[i][...] = acc_u[i].astype(BF16)
            od[i][...] = acc_d[i].astype(BF16)


def moe_slot(expert, x, g, gates, wg, wu, wd, carry, tile):
    rows, width = x.shape
    experts = gates.shape[1]
    pieces = len(wg)
    hidden = wg[0].shape[1]
    first = carry is None
    wide = pl.BlockSpec((tile, width), lambda i: (i, 0))
    thin = pl.BlockSpec((tile, experts), lambda i: (i, 0))
    tall = pl.BlockSpec((width, hidden), lambda i: (0, 0))
    flat = pl.BlockSpec((hidden, width), lambda i: (0, 0))
    ins = [expert, x, g, gates, *wg, *wu, *wd]
    specs = [pl.BlockSpec(memory_space=pltpu.SMEM), wide, wide, thin] + [tall] * (2 * pieces) + [flat] * pieces
    if not first:
        ins += list(carry)
        specs += [wide, wide, thin]
    outs = pl.pallas_call(
        functools.partial(moe_kernel, first, pieces),
        grid=(rows // tile,),
        in_specs=specs,
        out_specs=[wide, wide, thin] + [tall] * (2 * pieces) + [flat] * pieces,
        out_shape=[
            jax.ShapeDtypeStruct((rows, width), F32),
            jax.ShapeDtypeStruct((rows, width), F32),
            jax.ShapeDtypeStruct((rows, experts), F32),
        ]
        + [jax.ShapeDtypeStruct((width, hidden), BF16)] * (2 * pieces)
        + [jax.ShapeDtypeStruct((hidden, width), BF16)] * pieces,
        scratch_shapes=[
            pltpu.VMEM((pieces, width, hidden), F32),
            pltpu.VMEM((pieces, width, hidden), F32),
            pltpu.VMEM((pieces, hidden, width), F32),
        ],
        compiler_params=pltpu.CompilerParams(vmem_limit_bytes=60 * 2**20),
        cost_estimate=pl.CostEstimate(
            flops=18 * rows * width * hidden * pieces,
            bytes_accessed=rows * width * 20 + width * hidden * pieces * 12,
            transcendentals=rows * hidden * pieces,
        ),
        name="moe_slot",
    )(*ins)
    grads = outs[3:]
    return (
        tuple(outs[:3]),
        [(grads[i], grads[pieces + i], grads[2 * pieces + i]) for i in range(pieces)],
    )


def body(
    tokens,
    segment_ids,
    router_logits,
    expert_ids,
    gain_attn,
    w_query,
    key_matrix,
    value_matrix,
    w_out,
    gain_mlp,
    w_gate,
    w_up,
    w_down,
    out_grad,
):
    n_tok, width = tokens.shape
    col_width = out_grad.shape[1]
    n_tensor = width // col_width
    n_expert = router_logits.shape[1]
    depth = n_expert // PLANE
    my_row = n_tok // n_tensor
    t_at = lax.axis_index("tensor")
    e_at = lax.axis_index("expert")

    def hop(x, step):
        pairs = [(i, (i + step) % n_tensor) for i in range(n_tensor)]
        return jax.tree.map(lambda a: lax.ppermute(a, "tensor", pairs), x)

    def plane(x, mask):
        pairs = [(i, i ^ mask) for i in range(n_expert)]
        return jax.tree.map(lambda a: lax.ppermute(a, "expert", pairs), x)

    def ring(x, step=1):
        pairs = [(i, (i + step * PLANE) % n_expert) for i in range(n_expert)]
        return jax.tree.map(lambda a: lax.ppermute(a, "expert", pairs), x)

    def peer(step):
        return lax.rem(t_at + step + n_tensor, n_tensor)

    def rows_of(x, who):
        return lax.dynamic_slice_in_dim(x, who * my_row, my_row, 0)

    def cols_of(x, who):
        return lax.dynamic_slice_in_dim(x, who * col_width, col_width, x.ndim - 1)

    def to_rows(x):
        out = jnp.zeros((my_row, width), x.dtype)
        out = lax.dynamic_update_slice(out, rows_of(x, t_at), (0, t_at * col_width))
        for s in range(1, n_tensor):
            got = hop(rows_of(x, peer(s)), s)
            out = lax.dynamic_update_slice(out, got, (0, peer(-s) * col_width))
        return out

    def to_cols(x):
        out = jnp.zeros((n_tok, col_width), x.dtype)
        out = lax.dynamic_update_slice(out, cols_of(x, t_at), (t_at * my_row, 0))
        for s in range(1, n_tensor):
            got = hop(cols_of(x, peer(s)), s)
            out = lax.dynamic_update_slice(out, got, (peer(-s) * my_row, 0))
        return out

    def gather_rows(x):
        out = jnp.zeros((n_tok,) + x.shape[1:], x.dtype)
        rest = (0,) * (x.ndim - 1)
        out = lax.dynamic_update_slice(out, x, (t_at * my_row,) + rest)
        for s in range(1, n_tensor):
            out = lax.dynamic_update_slice(out, hop(x, s), (peer(-s) * my_row,) + rest)
        return out

    slots = []
    held = (w_gate[0], w_up[0], w_down[0])
    for k in range(depth):
        if k:
            held = ring(held)
        slots.append([held] + [hop(held, s) for s in range(1, n_tensor)])

    ids_rows = rows_of(expert_ids, t_at)
    logit_rows = rows_of(router_logits, t_at)
    expert_range = jnp.arange(n_expert, dtype=jnp.int32)
    used = jnp.any(ids_rows[:, :, None] == expert_range[None, None, :], axis=1)
    masked = jnp.where(used, logit_rows, NEG)
    weights = jnp.where(used, jnp.exp(masked - jnp.max(masked, axis=1, keepdims=True)), 0.0)
    gates = weights / jnp.sum(weights, axis=1, keepdims=True)
    grad_rows = to_rows(out_grad.astype(BF16))
    masks = range(1, PLANE)
    gates_all = jnp.concatenate([gates] + [plane(gates, m) for m in masks], axis=0)
    grads_all = jnp.concatenate([grad_rows] + [plane(grad_rows, m) for m in masks], axis=0)
    out_pieces = [w_out] + [hop(w_out, s) for s in range(1, n_tensor)]

    start = jnp.sum((segment_ids[:, None] < segment_ids[None, :]).astype(jnp.int32), axis=0)
    places = jnp.arange(n_tok, dtype=jnp.int32) - start
    half = HEAD_SIZE // 2
    freq = jnp.power(THETA, -2.0 * jnp.arange(half, dtype=F32) / HEAD_SIZE)
    angles = freq[:, None] * places.astype(F32)[None, :]
    cos_t, sin_t = jnp.cos(angles), jnp.sin(angles)
    start = start[None, :]
    x_full = tokens.astype(F32)
    inv_one = lax.rsqrt(jnp.mean(x_full * x_full, axis=1, keepdims=True) + EPS)
    normed_one = x_full * inv_one
    attn_in = (normed_one * gain_attn).astype(BF16)

    def project(w):
        return jnp.einsum("td,dc->ct", attn_in, w, preferred_element_type=F32)

    q_t, k_t, o_t, lse = attn_forward(
        project(w_query), project(key_matrix), project(value_matrix).astype(BF16), cos_t, sin_t, start
    )
    v_t = project(value_matrix).astype(BF16)
    mixed = rows_of(tokens, t_at).astype(F32)
    for s in range(n_tensor):
        part = lax.dynamic_slice_in_dim(o_t, peer(s) * my_row, my_row, 1)
        if s:
            part = hop(part, s)
        mixed = mixed + jnp.einsum("ct,cd->td", part, out_pieces[s], preferred_element_type=F32)
    inv_two = lax.rsqrt(jnp.mean(mixed * mixed, axis=1, keepdims=True) + EPS)
    normed_two = mixed * inv_two
    mlp_in = (normed_two * gain_mlp).astype(BF16)
    mlp_all = jnp.concatenate([mlp_in] + [plane(mlp_in, m) for m in masks], axis=0)

    carry = None
    totals = []
    for k in range(depth):
        expert = lax.rem(e_at - k * PLANE + n_expert, n_expert).reshape(1)
        wg, wu, wd = zip(*slots[k])
        carry, grads = moe_slot(expert, mlp_all, grads_all, gates_all, wg, wu, wd, carry, my_row)
        total = [a.astype(F32) for a in grads[0]]
        for s in range(1, n_tensor):
            got = hop(grads[s], n_tensor - s)
            total = [a + b.astype(F32) for a, b in zip(total, got)]
        totals.append(total)
    moving = None
    for k in list(range(1, depth)) + [0]:
        total = totals[k]
        if moving is not None:
            total = [a + b.astype(F32) for a, b in zip(total, ring(moving))]
        moving = [a.astype(BF16) for a in total]
    grad_gate, grad_up, grad_down = (a[None] for a in total)

    out_all, dx_all, dgate_all = carry

    def home(x):
        total = x[:my_row].astype(F32)
        for m in masks:
            total = total + plane(x[m * my_row : (m + 1) * my_row], m).astype(F32)
        return total

    d_mlp_in = home(dx_all.astype(BF16))
    d_gates = home(dgate_all)
    block_out = to_cols((mixed + home(out_all.astype(BF16))).astype(BF16))
    grad_logits = gather_rows(gates * (d_gates - jnp.sum(gates * d_gates, axis=1, keepdims=True)))

    scaled_two = d_mlp_in * gain_mlp
    norm_dots = jnp.mean(scaled_two * normed_two, axis=1, keepdims=True)
    d_mixed = grad_rows.astype(F32) + inv_two * (scaled_two - normed_two * norm_dots)
    gain_two_all = jnp.sum(d_mlp_in * normed_two, axis=0)
    gain_two = cols_of(gain_two_all, t_at)
    for s in range(1, n_tensor):
        gain_two = gain_two + hop(cols_of(gain_two_all, peer(s)), s)
    dy_full = gather_rows(d_mixed.astype(BF16))

    out_grad_w = jnp.einsum("ct,td->cd", o_t, dy_full, preferred_element_type=F32)
    grad_out = lax.psum(out_grad_w.astype(BF16), "expert").astype(F32)
    do_t = jnp.einsum("td,cd->ct", dy_full, w_out, preferred_element_type=F32).astype(BF16)
    dq_t, dk_t, dv_t = attn_backward(q_t, k_t, v_t, do_t, lse, cos_t, sin_t, start)

    def weight_grad(d_t):
        return jnp.einsum("td,ct->dc", attn_in, d_t, preferred_element_type=F32).astype(BF16)

    def input_grad(d_t, w):
        return jnp.einsum("ct,dc->td", d_t, w, preferred_element_type=F32)

    grad_query, grad_key, grad_value = (
        a.astype(F32) for a in lax.psum((weight_grad(dq_t), weight_grad(dk_t), weight_grad(dv_t)), "expert")
    )
    in_terms = input_grad(dq_t, w_query) + input_grad(dk_t, key_matrix) + input_grad(dv_t, value_matrix)
    dots = jnp.sum(in_terms * gain_attn * normed_one, axis=1)
    d_attn_in = cols_of(in_terms, t_at)
    all_dots = dots
    for s in range(1, n_tensor):
        d_attn_in = d_attn_in + hop(cols_of(in_terms, peer(s)).astype(BF16), s).astype(F32)
        all_dots = all_dots + hop(dots, s)
    normed_cols = cols_of(normed_one, t_at)
    scaled_one = d_attn_in * cols_of(gain_attn, t_at)
    d_norm_one = inv_one * (scaled_one - normed_cols * (all_dots / width)[:, None])
    grad_tokens = cols_of(dy_full, t_at).astype(F32) + d_norm_one
    gain_one = jnp.sum(d_attn_in * normed_cols, axis=0)

    gains = jnp.stack([gain_one, gain_two])
    for m in (1, 2):
        gains = gains + plane(gains, m)
    gains = functools.reduce(jnp.add, [gains] + [ring(gains, s) for s in range(1, depth)])
    return (
        block_out,
        grad_tokens,
        grad_logits,
        gains[0],
        grad_query,
        grad_key,
        grad_value,
        grad_out,
        gains[1],
        grad_gate,
        grad_up,
        grad_down,
    )


def solution(mesh):
    return jax.shard_map(
        body,
        mesh=mesh,
        in_specs=(
            P("expert", None),
            P("expert"),
            P("expert", None),
            P("expert", None),
            P(),
            P(None, "tensor"),
            P(None, "tensor"),
            P(None, "tensor"),
            P("tensor", None),
            P(),
            P("expert", None, "tensor"),
            P("expert", None, "tensor"),
            P("expert", "tensor", None),
            P("expert", "tensor"),
        ),
        out_specs=(
            P("expert", "tensor"),
            P("expert", "tensor"),
            P("expert", None),
            P("tensor"),
            P(None, "tensor"),
            P(None, "tensor"),
            P(None, "tensor"),
            P("tensor", None),
            P("tensor"),
            P("expert", None, "tensor"),
            P("expert", None, "tensor"),
            P("expert", "tensor", None),
        ),
        check_vma=False,
    )
```

```python
import functools

import jax
import jax.numpy as jnp
from jax import lax
from jax.experimental import pallas as pl
from jax.experimental.pallas import tpu as pltpu
from jax.sharding import PartitionSpec as P

HEAD_SIZE = 64
EPS = 1e-06
THETA = 10000.0
NEG = -1e30
PLANE = 4
LANES = 128
F32 = jnp.float32
BF16 = jnp.bfloat16
NT = (((1,), (1,)), ((), ()))
TN = (((0,), (0,)), ((), ()))


def dot(a, b):
    return jnp.dot(a, b, preferred_element_type=F32)


def dot_nt(a, b):
    return lax.dot_general(a, b, NT, preferred_element_type=F32)


def dot_tn(a, b):
    return lax.dot_general(a, b, TN, preferred_element_type=F32)


def attn_mask(start, row_start, block, keys):
    first = start[:, row_start : row_start + block]
    first = jnp.concatenate([first, first], axis=1)
    key_at = lax.broadcasted_iota(jnp.int32, (keys, 2 * block), 0)
    lane = lax.broadcasted_iota(jnp.int32, (1, 2 * block), 1)
    row_at = row_start + jnp.where(lane >= block, lane - block, lane)
    return (key_at >= first) & (key_at <= row_at)


def rope(x, c, s):
    half = x.shape[0] // 2
    a, b = x[:half], x[half:]
    return jnp.concatenate([a * c - b * s, b * c + a * s], axis=0)


def attn_fwd_kernel(block, q_ref, k_ref, v_ref, cos_ref, sin_ref, start_ref, qo_ref, ko_ref, o_ref, lse_ref):
    hd = HEAD_SIZE
    n = k_ref.shape[1]
    c, s = cos_ref[...], sin_ref[...]
    k_rot = rope(k_ref[...], c, s)
    ko_ref[...] = k_rot.astype(BF16)
    keys = k_rot.T.astype(BF16)
    q0 = rope(q_ref[0:hd], c, s).astype(BF16)
    q1 = rope(q_ref[hd : 2 * hd], c, s).astype(BF16)
    qo_ref[0:hd] = q0
    qo_ref[hd : 2 * hd] = q1
    start = start_ref[...]
    for r0 in range(0, n, block):
        cn = r0 + block
        qb = jnp.concatenate([q0[:, r0:cn], q1[:, r0:cn]], axis=1) * jnp.asarray(hd**-0.5, BF16)
        scores = dot(keys[:cn], qb)
        scores = jnp.where(attn_mask(start, r0, block, cn), scores, NEG)
        peak = jnp.max(scores, axis=0, keepdims=True)
        p = jnp.exp(scores - peak)
        total = jnp.sum(p, axis=0, keepdims=True)
        o = dot(v_ref[:, :cn], p.astype(BF16)) / total
        o_ref[0:hd, r0:cn] = o[:, :block].astype(BF16)
        o_ref[hd : 2 * hd, r0:cn] = o[:, block:].astype(BF16)
        lse = peak + jnp.log(total)
        lse_ref[0, 0:1, r0:cn] = lse[:, :block]
        lse_ref[0, 1:2, r0:cn] = lse[:, block:]


def attn_bwd_kernel(
    block, q_ref, k_ref, v_ref, do_ref, lse_ref, cos_ref, sin_ref, start_ref, dq_ref, dk_ref, dv_ref, dk_acc, dv_acc
):
    hd = HEAD_SIZE
    n = k_ref.shape[1]
    c, s = cos_ref[...], sin_ref[...]
    keys = k_ref[...].astype(F32).T.astype(BF16)
    vals = v_ref[...].astype(F32).T.astype(BF16)
    start = start_ref[...]
    dk_acc[...] = jnp.zeros_like(dk_acc)
    dv_acc[...] = jnp.zeros_like(dv_acc)
    scale = hd**-0.5
    for r0 in range(0, n, block):
        cn = r0 + block
        qb = jnp.concatenate([q_ref[0:hd, r0:cn], q_ref[hd : 2 * hd, r0:cn]], axis=1)
        gb = jnp.concatenate([do_ref[0:hd, r0:cn], do_ref[hd : 2 * hd, r0:cn]], axis=1)
        lse = jnp.concatenate([lse_ref[0, 0:1, r0:cn], lse_ref[0, 1:2, r0:cn]], axis=1)
        scores = dot(keys[:cn], qb * jnp.asarray(scale, BF16))
        p = jnp.exp(jnp.where(attn_mask(start, r0, block, cn), scores, NEG) - lse)
        dv_acc[:, :cn] += dot_nt(gb, p.astype(BF16))
        dp = dot(vals[:cn], gb)
        delta = jnp.sum(p * dp, axis=0, keepdims=True)
        ds = (p * (dp - delta) * scale).astype(BF16)
        dq = dot(k_ref[:, :cn], ds)
        dk_acc[:, :cn] += dot_nt(qb, ds)
        cb, sb = c[:, r0:cn], -s[:, r0:cn]
        dq_ref[0:hd, r0:cn] = rope(dq[:, :block], cb, sb).astype(BF16)
        dq_ref[hd : 2 * hd, r0:cn] = rope(dq[:, block:], cb, sb).astype(BF16)
    dk_ref[...] = rope(dk_acc[...], c, -s).astype(BF16)
    dv_ref[...] = dv_acc[...].astype(BF16)


def attn_cost(heads, n, products):
    return pl.CostEstimate(
        flops=products * heads * n * n * HEAD_SIZE * 2, bytes_accessed=8 * heads * n * HEAD_SIZE, transcendentals=heads * n * n
    )


def attn_forward(q_t, k_t, v_t, cos_t, sin_t, start):
    n = q_t.shape[1]
    hd = HEAD_SIZE
    kv = k_t.shape[0] // hd
    block = min(256, n)
    pair = pl.BlockSpec((2 * hd, n), lambda h: (h, 0))
    one = pl.BlockSpec((hd, n), lambda h: (h, 0))
    table = pl.BlockSpec((hd // 2, n), lambda h: (0, 0))
    return pl.pallas_call(
        functools.partial(attn_fwd_kernel, block),
        grid=(kv,),
        in_specs=[pair, one, one, table, table, pl.BlockSpec((1, n), lambda h: (0, 0))],
        out_specs=[pair, one, pair, pl.BlockSpec((1, 2, n), lambda h: (h, 0, 0))],
        out_shape=[
            jax.ShapeDtypeStruct(q_t.shape, BF16),
            jax.ShapeDtypeStruct(k_t.shape, BF16),
            jax.ShapeDtypeStruct(q_t.shape, BF16),
            jax.ShapeDtypeStruct((kv, 2, n), F32),
        ],
        compiler_params=pltpu.CompilerParams(vmem_limit_bytes=48 * 2**20),
        cost_estimate=attn_cost(2 * kv, n, 4),
        name="attn_forward",
    )(q_t, k_t, v_t, cos_t, sin_t, start)


def attn_backward(q_t, k_t, v_t, do_t, lse, cos_t, sin_t, start):
    n = q_t.shape[1]
    hd = HEAD_SIZE
    kv = k_t.shape[0] // hd
    block = min(256, n)
    pair = pl.BlockSpec((2 * hd, n), lambda h: (h, 0))
    one = pl.BlockSpec((hd, n), lambda h: (h, 0))
    table = pl.BlockSpec((hd // 2, n), lambda h: (0, 0))
    return pl.pallas_call(
        functools.partial(attn_bwd_kernel, block),
        grid=(kv,),
        in_specs=[
            pair,
            one,
            one,
            pair,
            pl.BlockSpec((1, 2, n), lambda h: (h, 0, 0)),
            table,
            table,
            pl.BlockSpec((1, n), lambda h: (0, 0)),
        ],
        out_specs=[pair, one, one],
        out_shape=[
            jax.ShapeDtypeStruct(q_t.shape, BF16),
            jax.ShapeDtypeStruct(k_t.shape, BF16),
            jax.ShapeDtypeStruct(k_t.shape, BF16),
        ],
        scratch_shapes=[pltpu.VMEM((hd, n), F32), pltpu.VMEM((hd, n), F32)],
        compiler_params=pltpu.CompilerParams(vmem_limit_bytes=48 * 2**20),
        cost_estimate=attn_cost(2 * kv, n, 10),
        name="attn_backward",
    )(q_t, k_t, v_t, do_t, lse, cos_t, sin_t, start)


def data_kernel(first, last, blocks, slots, pieces, expert_ref, *refs):
    refs = list(refs)
    x, g_all = refs[0][...], refs[blocks][...]
    for i in range(1, blocks):
        here = pl.program_id(0) == i
        x = jnp.where(here, refs[i][...], x)
        g_all = jnp.where(here, refs[blocks + i][...], g_all)
    ws = refs[2 * blocks : 2 * blocks + slots * pieces]
    refs = refs[2 * blocks + slots * pieces :]
    if not first:
        out_in, dx_in, dgate_in = refs[:3]
        refs = refs[3:]
    if last:
        out_ref, dx_ref = refs[:2]
        refs = refs[2:]
    else:
        out_ref, dx_ref, dgate_ref = refs[:3]
        refs = refs[3:]
    hs, acts = refs[:slots], refs[slots : 2 * slots]
    acc_o, acc_x = refs[2 * slots :]
    width = x.shape[1]
    g = g_all[:, :width]
    gates = g_all[:, width:].astype(F32)
    lane = lax.broadcasted_iota(jnp.int32, gates.shape, 1)
    dgate = None if first else dgate_in[...]
    for j in range(slots):
        here = lane == expert_ref[j]
        both = here | (lane == expert_ref[j] + LANES // 2)
        gate = jnp.sum(jnp.where(both, gates, 0.0), axis=1, keepdims=True)
        row_sum = None
        for i in range(pieces):
            w = ws[j * pieces + i]
            hid = w.shape[2]
            gate_pre = dot(x, w[0])
            up_pre = dot(x, w[1])
            d_hidden = dot(g, w[2])
            sig = jax.nn.sigmoid(gate_pre)
            silu = gate_pre * sig
            act = silu * up_pre
            part = jnp.sum(act * d_hidden, axis=1, keepdims=True)
            row_sum = part if row_sum is None else row_sum + part
            act_w = (act * gate).astype(BF16)
            d_hidden = d_hidden * gate
            d_up = (d_hidden * silu).astype(BF16)
            d_gate = (d_hidden * up_pre * (sig + silu * (1.0 - sig))).astype(BF16)
            hs[j][:, 2 * i * hid : (2 * i + 1) * hid] = d_gate
            hs[j][:, (2 * i + 1) * hid : (2 * i + 2) * hid] = d_up
            acts[j][:, i * hid : (i + 1) * hid] = act_w
            out_term = dot_nt(act_w, w[2])
            dx_term = dot_nt(d_gate, w[0]) + dot_nt(d_up, w[1])
            if i == 0 and j == 0 and first:
                acc_o[...] = out_term
                acc_x[...] = dx_term
            elif i == 0 and j == 0:
                acc_o[...] = out_in[...] + out_term
                acc_x[...] = dx_in[...] + dx_term
            else:
                acc_o[...] += out_term
                acc_x[...] += dx_term
        term = jnp.where(here, row_sum, 0.0)
        dgate = term if dgate is None else dgate + term
    out_ref[...] = acc_o[...].astype(out_ref.dtype)
    if last:
        dx_ref[:, :width] = acc_x[...].astype(BF16)
        high = dgate.astype(BF16).astype(F32)
        low = pltpu.roll(dgate - high, LANES // 2, 1)
        dx_ref[:, width:] = jnp.where(lane < LANES // 2, high, low).astype(BF16)
    else:
        dx_ref[...] = acc_x[...]
        dgate_ref[...] = dgate


def expert_data(experts, xs, gs, ws, carry, last):
    blocks = len(xs)
    rows, width = xs[0].shape
    tile = min(256, rows)
    tiles = rows // tile
    full = gs[0].shape[1]
    slots = experts.shape[0]
    pieces = len(ws) // slots
    hidden = ws[0].shape[2]
    first = carry is None
    total = blocks * rows

    def out_spec(columns):
        return pl.BlockSpec((tile, columns), lambda b, i: (b * tiles + i, 0))

    def in_spec(columns):
        return pl.BlockSpec((tile, columns), lambda b, i: (i, 0))

    weight = pl.BlockSpec((3, width, hidden), lambda b, i: (0, 0, 0), pipeline_mode=pl.Buffered(1))
    ins = [experts, *xs, *gs, *ws]
    specs = [pl.BlockSpec(memory_space=pltpu.SMEM)] + [in_spec(width)] * blocks + [in_spec(full)] * blocks + [weight] * len(ws)
    if not first:
        ins += list(carry)
        specs += [out_spec(width), out_spec(width), out_spec(LANES)]
    if last:
        out_columns, out_types = [width, full], [BF16, BF16]
    else:
        out_columns, out_types = [width, width, LANES], [F32] * 3
    n = len(out_columns)
    out_columns += [2 * pieces * hidden] * slots + [pieces * hidden] * slots
    out_types += [BF16] * (2 * slots)
    single = pieces * hidden
    outs = pl.pallas_call(
        functools.partial(data_kernel, first, last, blocks, slots, pieces),
        grid=(blocks, tiles),
        in_specs=specs,
        out_specs=[out_spec(c) for c in out_columns],
        out_shape=[jax.ShapeDtypeStruct((total, c), t) for c, t in zip(out_columns, out_types)],
        scratch_shapes=[pltpu.VMEM((tile, width), F32), pltpu.VMEM((tile, width), F32)],
        compiler_params=pltpu.CompilerParams(vmem_limit_bytes=60 * 2**20),
        cost_estimate=pl.CostEstimate(
            flops=3 * slots * total * width * single,
            bytes_accessed=total * width * 12 + slots * pieces * width * hidden * 6,
            transcendentals=slots * total * single,
        ),
        name="expert_data",
    )(*ins)
    return outs[:n], outs[n : n + slots], outs[n + slots :]


def weight_kernel(shape, pieces, *refs):
    xt = gt = None
    refs = list(refs)
    for blocks in shape:
        xs, gs, h, a = refs[:blocks], refs[blocks : 2 * blocks], refs[2 * blocks], refs[2 * blocks + 1]
        refs = refs[2 * blocks + 2 :]
        rows = xs[0].shape[0]
        for i in range(blocks):
            span = slice(i * rows, (i + 1) * rows)
            xp, gp = dot_tn(xs[i][...], h[span]), dot_tn(gs[i][...], a[span])
            xt, gt = (xp, gp) if xt is None else (xt + xp, gt + gp)
    outs = refs
    hid = outs[0].shape[2]
    for i in range(pieces):
        outs[i][0] = xt[:, 2 * i * hid : (2 * i + 1) * hid].astype(BF16)
        outs[i][1] = xt[:, (2 * i + 1) * hid : (2 * i + 2) * hid].astype(BF16)
        outs[i][2] = gt[:, i * hid : (i + 1) * hid].astype(BF16)


def expert_weight(parts, pieces, width):
    hidden = parts[0][3].shape[1] // pieces
    block = 256
    ins, specs, shape, total = [], [], [], 0
    for xs, gs, h, a in parts:
        rows = xs[0].shape[0]
        col = pl.BlockSpec((rows, block), lambda i: (0, i))
        ins += [*xs, *gs, h, a]
        specs += [col] * (2 * len(xs))
        for v in (h, a):
            specs.append(pl.BlockSpec(v.shape, lambda i: (0, 0), pipeline_mode=pl.Buffered(1)))
        shape.append(len(xs))
        total += h.shape[0]
    return pl.pallas_call(
        functools.partial(weight_kernel, tuple(shape), pieces),
        grid=(width // block,),
        in_specs=specs,
        out_specs=[pl.BlockSpec((3, block, hidden), lambda i: (0, i, 0))] * pieces,
        out_shape=[jax.ShapeDtypeStruct((3, width, hidden), BF16)] * pieces,
        compiler_params=pltpu.CompilerParams(vmem_limit_bytes=60 * 2**20),
        cost_estimate=pl.CostEstimate(
            flops=total * width * hidden * pieces,
            bytes_accessed=total * (width * 4 + hidden * pieces * 6) + width * hidden * pieces * 6,
            transcendentals=0,
        ),
        name="expert_weight",
    )(*ins)


def lay_out_kernel(quarters, cuts, at_ref, *refs):
    pieces, outs = refs[:PLANE], refs[PLANE:]
    first, second = quarters
    for m in range(PLANE):
        who = at_ref[0] ^ m
        left = 0
        rows = pl.ds(pl.multiple_of(who * first, first), first)
        for out, cut in zip(outs, cuts):
            out[rows, :] = pieces[m][:first, left : left + cut].astype(F32)
            left += cut
        rows = pl.ds(pl.multiple_of(who * second, second), second)
        outs[-1][rows, :] = pieces[m][first : first + second].astype(F32)


def lay_out(at, pieces, quarters, cuts):
    first, second = (PLANE * q for q in quarters)
    whole = pl.BlockSpec(memory_space=pltpu.VMEM)
    return pl.pallas_call(
        functools.partial(lay_out_kernel, quarters, cuts),
        in_specs=[pl.BlockSpec(memory_space=pltpu.SMEM)] + [whole] * PLANE,
        out_specs=[whole] * (len(cuts) + 1),
        out_shape=[jax.ShapeDtypeStruct((first, c), F32) for c in cuts]
        + [jax.ShapeDtypeStruct((second, pieces[0].shape[1]), F32)],
        compiler_params=pltpu.CompilerParams(vmem_limit_bytes=48 * 2**20),
        cost_estimate=pl.CostEstimate(flops=0, bytes_accessed=6 * first * sum(cuts), transcendentals=0),
        name="lay_out",
    )(at, *pieces)


def after(x, *others):
    leaves, tree = jax.tree.flatten(x)
    extra = jax.tree.leaves(others)
    held = lax.optimization_barrier(tuple(leaves) + tuple(extra))
    return jax.tree.unflatten(tree, held[: len(leaves)])


def body(
    tokens,
    segment_ids,
    router_logits,
    expert_ids,
    gain_attn,
    w_query,
    key_matrix,
    value_matrix,
    w_out,
    gain_mlp,
    w_gate,
    w_up,
    w_down,
    out_grad,
):
    n_tok, width = tokens.shape
    col_width = out_grad.shape[1]
    n_tensor = width // col_width
    n_expert = router_logits.shape[1]
    depth = n_expert // PLANE
    my_row = n_tok // n_tensor
    t_at = lax.axis_index("tensor")
    e_at = lax.axis_index("expert")

    def hop(x, step):
        pairs = [(i, (i + step) % n_tensor) for i in range(n_tensor)]
        return jax.tree.map(lambda a: lax.ppermute(a, "tensor", pairs), x)

    def plane(x, mask):
        pairs = [(i, i ^ mask) for i in range(n_expert)]
        return jax.tree.map(lambda a: lax.ppermute(a, "expert", pairs), x)

    def ring(x, step=1):
        pairs = [(i, (i + step * PLANE) % n_expert) for i in range(n_expert)]
        return jax.tree.map(lambda a: lax.ppermute(a, "expert", pairs), x)

    def peer(step):
        return lax.rem(t_at + step + n_tensor, n_tensor)

    def rows_of(x, who):
        return lax.dynamic_slice_in_dim(x, who * my_row, my_row, 0)

    def cols_of(x, who):
        return lax.dynamic_slice_in_dim(x, who * col_width, col_width, x.ndim - 1)

    def place(parts, axis):
        if n_tensor == 2:
            return jnp.where(t_at == 0, jnp.concatenate(parts, axis), jnp.concatenate(parts[::-1], axis))
        size = parts[0].shape[axis]
        shape = list(parts[0].shape)
        shape[axis] *= n_tensor
        out = jnp.zeros(shape, parts[0].dtype)
        for s, v in enumerate(parts):
            out = lax.dynamic_update_slice_in_dim(out, v, peer(-s) * size, axis)
        return out

    def to_rows(x):
        return place([rows_of(x, t_at)] + [hop(rows_of(x, peer(s)), s) for s in range(1, n_tensor)], 1)

    def to_cols(x):
        return place([cols_of(x, t_at)] + [hop(cols_of(x, peer(s)), s) for s in range(1, n_tensor)], 0)

    def gather_rows(x):
        return place([x] + [hop(x, s) for s in range(1, n_tensor)], 0)

    ids_rows = rows_of(expert_ids, t_at)
    logit_rows = rows_of(router_logits, t_at)
    expert_range = jnp.arange(n_expert, dtype=jnp.int32)
    used = jnp.any(ids_rows[:, :, None] == expert_range[None, None, :], axis=1)
    masked = jnp.where(used, logit_rows, NEG)
    weights = jnp.where(used, jnp.exp(masked - jnp.max(masked, axis=1, keepdims=True)), 0.0)
    gates = weights / jnp.sum(weights, axis=1, keepdims=True)
    pad = ((0, 0), (0, LANES // 2 - n_expert))
    high = lax.optimization_barrier(gates.astype(BF16))
    low = (gates - high.astype(F32)).astype(BF16)
    grad_rows = to_rows(out_grad.astype(BF16))
    grad_wide = jnp.concatenate([grad_rows, jnp.pad(high, pad), jnp.pad(low, pad)], axis=1)
    held = [jnp.stack([w_gate[0], w_up[0], w_down[0].T])]
    half_row = my_row // 2

    start = jnp.sum((segment_ids[:, None] < segment_ids[None, :]).astype(jnp.int32), axis=0)
    places = jnp.arange(n_tok, dtype=jnp.int32) - start
    half = HEAD_SIZE // 2
    freq = jnp.power(THETA, -2.0 * jnp.arange(half, dtype=F32) / HEAD_SIZE)
    angles = freq[:, None] * places.astype(F32)[None, :]
    cos_t, sin_t = jnp.cos(angles), jnp.sin(angles)
    start = start[None, :]
    held.append(ring(held[0]))
    tokens, grad_wide = after((tokens, grad_wide))
    grad_x, grad_y = plane(grad_wide, 1), plane(grad_wide, 2)
    out_pieces = [w_out] + [hop(w_out, s) for s in range(1, n_tensor)]
    slots = [[held[0]] + [hop(held[0], s) for s in range(1, n_tensor)]]
    x_full = tokens.astype(F32)
    inv_one = lax.rsqrt(jnp.mean(x_full * x_full, axis=1, keepdims=True) + EPS)
    normed_one = x_full * inv_one
    attn_in = (normed_one * gain_attn).astype(BF16)

    def project(w):
        return jnp.einsum("td,dc->ct", attn_in, w, preferred_element_type=F32)

    v_t = project(value_matrix).astype(BF16)
    q_t, k_t, o_t, lse = attn_forward(project(w_query), project(key_matrix), v_t, cos_t, sin_t, start)
    o_t, grad_x, grad_y, slots[0], out_pieces, held[1] = after((o_t, grad_x, grad_y, slots[0], out_pieces, held[1]))
    held.append(ring(held[1]))
    grad_diag = [plane(grad_x[:half_row], 2), plane(grad_y[half_row:], 1)]
    mixed = rows_of(tokens, t_at).astype(F32)
    for s in range(n_tensor):
        part = lax.dynamic_slice_in_dim(o_t, peer(s) * my_row, my_row, 1)
        if s:
            part = hop(part, s)
        mixed = mixed + jnp.einsum("ct,cd->td", part, out_pieces[s], preferred_element_type=F32)
    inv_two = lax.rsqrt(jnp.mean(mixed * mixed, axis=1, keepdims=True) + EPS)
    normed_two = mixed * inv_two
    mlp_in = (normed_two * gain_mlp).astype(BF16)
    mlp_in, grad_diag = after((mlp_in, grad_diag))

    near = ([mlp_in], [grad_wide])
    sides, diag = None, None
    group = 2 if depth % 2 == 0 else 1
    carry = {"near": None, "sides": None, "diag": None}
    saved = [{} for _ in range(depth)]

    def run(name, blocks, k, ws):
        ks = range(k, k + group)
        experts = jnp.stack([lax.rem(e_at - i * PLANE + n_expert, n_expert) for i in ks])
        flat = [w for i in ks for w in ws[i]]
        carry[name], hs, acts = expert_data(experts, *blocks, flat, carry[name], k + group == depth)
        for i, h, a in zip(ks, hs, acts):
            saved[i][name] = (*blocks, h, a)

    def add_slot():
        k = len(slots)
        slots.append([held[k]] + [hop(held[k], s) for s in range(1, n_tensor)])

    mlp_x, mlp_y = plane(mlp_in, 1), plane(mlp_in, 2)
    for _ in range(1, group):
        add_slot()
    run("near", near, 0, slots)
    mlp_x, mlp_y, carry["near"], held[2] = after((mlp_x, mlp_y, carry["near"], held[2]))
    for _ in range(3, depth):
        held.append(ring(held[-1]))
    mlp_diag = [plane(mlp_x[:half_row], 2), plane(mlp_y[half_row:], 1)]
    sides = ([mlp_x, mlp_y], [grad_x, grad_y])
    run("sides", sides, 0, slots)
    carry["sides"], mlp_diag = after((carry["sides"], mlp_diag))
    diag = (mlp_diag, grad_diag)
    add_slot()
    run("diag", diag, 0, slots)

    def weight_total(k):
        grads = expert_weight(list(saved[k].values()), n_tensor, width)
        total = grads[0].astype(F32)
        for s in range(1, n_tensor):
            total = total + hop(grads[s], n_tensor - s).astype(F32)
        return total

    for k in range(group, depth - group, group):
        while len(slots) < k + group:
            add_slot()
        for name, blocks in (("near", near), ("sides", sides), ("diag", diag)):
            run(name, blocks, k, slots)
    carry["diag"] = after(carry["diag"], slots[-1])
    totals = {}
    order = list(range(1, depth)) + [0]
    early = order[: depth - group - 1]
    for k in early:
        totals[k] = weight_total(k)
    while len(slots) < depth:
        add_slot()
    slots[-1], totals = after((slots[-1], totals))
    moving = None

    def send_on(k, moving):
        total = totals[k]
        if moving is not None:
            total = total + moving.astype(F32)
        return ring(total.astype(BF16)) if k else total

    for k in early:
        moving = send_on(k, moving)
    rest = order[len(early) :]
    last = depth - group
    run("diag", diag, last, slots)
    top, low = slice(0, half_row), slice(half_row, my_row)

    def first_half(rows):
        return plane(rows[top], 1), plane(rows[low], 2)

    def second_half(rows):
        return plane(rows[:my_row][top], 1), plane(rows[my_row:][low], 2)

    def third_half(rows, part_y, part_x):
        low_x = rows[:my_row][low].astype(F32) + part_x.astype(F32)
        top_y = rows[my_row:][top].astype(F32) + part_y.astype(F32)
        return plane(low_x.astype(BF16), 1), plane(top_y.astype(BF16), 2)

    def home(own, top_x, low_y, low_x, top_y):
        first = own[top].astype(F32) + top_x.astype(F32) + top_y.astype(F32)
        return jnp.concatenate([first, own[low].astype(F32) + low_x.astype(F32) + low_y.astype(F32)], axis=0)

    parts = first_half(carry["diag"][1])
    run("sides", sides, last, slots)
    carry["sides"], near[0][0] = after((carry["sides"], near[0][0]))
    halves = second_half(carry["sides"][1])
    run("near", near, last, slots)
    parts, halves, carry["near"] = after((parts, halves, carry["near"]))
    others = third_half(carry["sides"][1], *parts)
    totals[rest[0]] = weight_total(rest[0])
    others, totals, moving = after((others, totals, moving))

    moving = send_on(rest[0], moving)
    out_parts = first_half(carry["diag"][0])
    back = home(carry["near"][1], *halves, *others)
    d_mlp_in = back[:, :width]
    d_gates = back[:, width : width + n_expert] + back[:, width + LANES // 2 : width + LANES // 2 + n_expert]
    scaled_two = d_mlp_in * gain_mlp
    norm_dots = jnp.mean(scaled_two * normed_two, axis=1, keepdims=True)
    d_mixed = grad_rows.astype(F32) + inv_two * (scaled_two - normed_two * norm_dots)
    dy_full = gather_rows(d_mixed.astype(BF16))
    for k in rest[1:]:
        if k:
            totals[k] = weight_total(k)
    dy_full, totals, out_parts = after((dy_full, totals, out_parts))
    halves = second_half(carry["sides"][0])
    others = third_half(carry["sides"][0], *out_parts)

    do_t = jnp.einsum("td,cd->ct", dy_full, w_out, preferred_element_type=F32).astype(BF16)
    out_grad_w = jnp.einsum("ct,td->cd", o_t, dy_full, preferred_element_type=F32)
    out_grad_w = out_grad_w.astype(BF16)
    dq_t, dk_t, dv_t = attn_backward(q_t, k_t, v_t, do_t, lse, cos_t, sin_t, start)
    gain_two_all = jnp.sum(d_mlp_in * normed_two, axis=0)
    gain_two = cols_of(gain_two_all, t_at)
    for s in range(1, n_tensor):
        gain_two = gain_two + hop(cols_of(gain_two_all, peer(s)), s)
    grad_logits = gather_rows(gates * (d_gates - jnp.sum(gates * d_gates, axis=1, keepdims=True)))
    dq_t, halves, others, moving, gain_two = after((dq_t, halves, others, moving, gain_two))
    for k in rest[1:-1]:
        moving = send_on(k, moving)
    saved[0], dq_t = after((saved[0], dq_t))
    totals[0] = weight_total(0)
    block_out = to_cols((mixed + home(carry["near"][0], *halves, *others)).astype(BF16))

    def weight_grad(d_t):
        return jnp.einsum("td,ct->dc", attn_in, d_t, preferred_element_type=F32).astype(BF16)

    def input_grad(d_t, w):
        return jnp.einsum("ct,dc->td", d_t, w, preferred_element_type=F32)

    def part(a, who, rows):
        return lax.dynamic_slice_in_dim(a, who * rows, rows, 0)

    local = jnp.concatenate([weight_grad(dq_t), weight_grad(dk_t), weight_grad(dv_t)], axis=1)
    quarters = (local.shape[0] // PLANE, out_grad_w.shape[0] // PLANE)
    wide = local.shape[1]
    out_rows = out_grad_w.shape[0] * width // wide
    out_grad_w = out_grad_w.reshape(out_rows, wide)
    quarters = (local.shape[0] // PLANE, out_rows // PLANE)
    p_at, z_at = lax.rem(e_at, PLANE), e_at // PLANE

    def quarter_of(who):
        return jnp.concatenate([part(v, who, q) for v, q in zip((local, out_grad_w), quarters)], axis=0)

    sent = [plane(quarter_of(p_at ^ m), m) for m in range(1, PLANE)]
    quarter = sum(quarters)
    small = quarter // depth

    in_terms = input_grad(dq_t, w_query) + input_grad(dk_t, key_matrix) + input_grad(dv_t, value_matrix)
    dots = jnp.sum(in_terms * gain_attn * normed_one, axis=1)
    d_attn_in = cols_of(in_terms, t_at)
    all_dots = dots
    for s in range(1, n_tensor):
        d_attn_in = d_attn_in + hop(cols_of(in_terms, peer(s)).astype(BF16), s).astype(F32)
        all_dots = all_dots + hop(dots, s)
    normed_cols = cols_of(normed_one, t_at)
    scaled_one = d_attn_in * cols_of(gain_attn, t_at)
    d_norm_one = inv_one * (scaled_one - normed_cols * (all_dots / width)[:, None])
    grad_tokens = cols_of(dy_full, t_at).astype(F32) + d_norm_one
    gain_one = jnp.sum(d_attn_in * normed_cols, axis=0)

    gains = jnp.concatenate([gain_one, gain_two]).astype(BF16)
    gains = jnp.broadcast_to(gains[None, :], (16, gains.shape[0]))
    mine = quarter_of(p_at).astype(F32)
    for v in sent:
        mine = mine + v.astype(F32)
    mine, gains = after((mine.astype(BF16), gains))
    rows = [jnp.concatenate([part(mine, lax.rem(z_at + s, depth), small), gains], axis=0) for s in range(depth)]
    total = rows[0].astype(F32)
    for v in [ring(rows[s], s) for s in range(1, depth)]:
        total = total + v.astype(F32)
    total = total.astype(BF16)
    gains, total = total[small:], total[:small]
    got = [ring(total, s) for s in range(1, depth)]
    out = jnp.zeros((quarter, total.shape[1]), BF16)
    out = lax.dynamic_update_slice(out, total, (z_at * small, 0))
    for s in range(1, depth):
        out = lax.dynamic_update_slice(out, got[s - 1], (lax.rem(z_at - s + depth, depth) * small, 0))
    out = jnp.concatenate([out, gains], axis=0)
    got = [out] + [plane(out, m) for m in range(1, PLANE)]
    gains = functools.reduce(jnp.add, [v[quarter].astype(F32) for v in got])
    cuts = [w_query.shape[1], key_matrix.shape[1], value_matrix.shape[1]]
    grad_query, grad_key, grad_value, grad_out = lay_out(p_at.reshape(1), got, quarters, cuts)
    moving = send_on(rest[-1], moving)
    return (
        block_out,
        grad_tokens,
        grad_logits,
        gains[:col_width],
        grad_query,
        grad_key,
        grad_value,
        grad_out.reshape(w_out.shape),
        gains[col_width:],
        moving[0][None],
        moving[1][None],
        moving[2].T[None],
    )


def solution(mesh):
    return jax.shard_map(
        body,
        mesh=mesh,
        in_specs=(
            P("expert", None),
            P("expert"),
            P("expert", None),
            P("expert", None),
            P(),
            P(None, "tensor"),
            P(None, "tensor"),
            P(None, "tensor"),
            P("tensor", None),
            P(),
            P("expert", None, "tensor"),
            P("expert", None, "tensor"),
            P("expert", "tensor", None),
            P("expert", "tensor"),
        ),
        out_specs=(
            P("expert", "tensor"),
            P("expert", "tensor"),
            P("expert", None),
            P("tensor"),
            P(None, "tensor"),
            P(None, "tensor"),
            P(None, "tensor"),
            P("tensor", None),
            P("tensor"),
            P("expert", None, "tensor"),
            P("expert", None, "tensor"),
            P("expert", "tensor", None),
        ),
        check_vma=False,
    )
```

```python
import functools

import jax
import jax.numpy as jnp
from jax import lax
from jax.experimental import pallas as pl
from jax.experimental.pallas import tpu as pltpu
from jax.sharding import PartitionSpec as P

HEAD_SIZE = 64
EPS = 1e-06
THETA = 10000.0
NEG = -1e30
PLANE = 4
LANES = 128
F32 = jnp.float32
BF16 = jnp.bfloat16
NT = (((1,), (1,)), ((), ()))
TN = (((0,), (0,)), ((), ()))


def dot(a, b):
    return jnp.dot(a, b, preferred_element_type=F32)


def dot_nt(a, b):
    return lax.dot_general(a, b, NT, preferred_element_type=F32)


def dot_tn(a, b):
    return lax.dot_general(a, b, TN, preferred_element_type=F32)


def attn_mask(start, row_start, block, keys):
    first = start[:, row_start : row_start + block]
    first = jnp.concatenate([first, first], axis=1)
    key_at = lax.broadcasted_iota(jnp.int32, (keys, 2 * block), 0)
    lane = lax.broadcasted_iota(jnp.int32, (1, 2 * block), 1)
    row_at = row_start + jnp.where(lane >= block, lane - block, lane)
    return (key_at >= first) & (key_at <= row_at)


def rope(x, c, s):
    half = x.shape[0] // 2
    a, b = x[:half], x[half:]
    return jnp.concatenate([a * c - b * s, b * c + a * s], axis=0)


def attn_fwd_kernel(block, q_ref, k_ref, v_ref, cos_ref, sin_ref, start_ref, qo_ref, ko_ref, o_ref, lse_ref):
    hd = HEAD_SIZE
    n = k_ref.shape[1]
    c, s = cos_ref[...], sin_ref[...]
    k_rot = rope(k_ref[...], c, s)
    ko_ref[...] = k_rot.astype(BF16)
    keys = k_rot.T.astype(BF16)
    q0 = rope(q_ref[0:hd], c, s).astype(BF16)
    q1 = rope(q_ref[hd : 2 * hd], c, s).astype(BF16)
    qo_ref[0:hd] = q0
    qo_ref[hd : 2 * hd] = q1
    start = start_ref[...]
    for r0 in range(0, n, block):
        cn = r0 + block
        qb = jnp.concatenate([q0[:, r0:cn], q1[:, r0:cn]], axis=1) * jnp.asarray(hd**-0.5, BF16)
        scores = dot(keys[:cn], qb)
        scores = jnp.where(attn_mask(start, r0, block, cn), scores, NEG)
        peak = jnp.max(scores, axis=0, keepdims=True)
        p = jnp.exp(scores - peak)
        total = jnp.sum(p, axis=0, keepdims=True)
        o = dot(v_ref[:, :cn], p.astype(BF16)) / total
        o_ref[0:hd, r0:cn] = o[:, :block].astype(BF16)
        o_ref[hd : 2 * hd, r0:cn] = o[:, block:].astype(BF16)
        lse = peak + jnp.log(total)
        lse_ref[0, 0:1, r0:cn] = lse[:, :block]
        lse_ref[0, 1:2, r0:cn] = lse[:, block:]


def attn_bwd_kernel(
    block, q_ref, k_ref, v_ref, do_ref, lse_ref, cos_ref, sin_ref, start_ref, dq_ref, dk_ref, dv_ref, dk_acc, dv_acc
):
    hd = HEAD_SIZE
    n = k_ref.shape[1]
    c, s = cos_ref[...], sin_ref[...]
    keys = k_ref[...].astype(F32).T.astype(BF16)
    vals = v_ref[...].astype(F32).T.astype(BF16)
    start = start_ref[...]
    dk_acc[...] = jnp.zeros_like(dk_acc)
    dv_acc[...] = jnp.zeros_like(dv_acc)
    scale = hd**-0.5
    for r0 in range(0, n, block):
        cn = r0 + block
        qb = jnp.concatenate([q_ref[0:hd, r0:cn], q_ref[hd : 2 * hd, r0:cn]], axis=1)
        gb = jnp.concatenate([do_ref[0:hd, r0:cn], do_ref[hd : 2 * hd, r0:cn]], axis=1)
        lse = jnp.concatenate([lse_ref[0, 0:1, r0:cn], lse_ref[0, 1:2, r0:cn]], axis=1)
        scores = dot(keys[:cn], qb * jnp.asarray(scale, BF16))
        p = jnp.exp(jnp.where(attn_mask(start, r0, block, cn), scores, NEG) - lse)
        dv_acc[:, :cn] += dot_nt(gb, p.astype(BF16))
        dp = dot(vals[:cn], gb)
        delta = jnp.sum(p * dp, axis=0, keepdims=True)
        ds = (p * (dp - delta) * scale).astype(BF16)
        dq = dot(k_ref[:, :cn], ds)
        dk_acc[:, :cn] += dot_nt(qb, ds)
        cb, sb = c[:, r0:cn], -s[:, r0:cn]
        dq_ref[0:hd, r0:cn] = rope(dq[:, :block], cb, sb).astype(BF16)
        dq_ref[hd : 2 * hd, r0:cn] = rope(dq[:, block:], cb, sb).astype(BF16)
    dk_ref[...] = rope(dk_acc[...], c, -s).astype(BF16)
    dv_ref[...] = dv_acc[...].astype(BF16)


def attn_cost(heads, n, products):
    return pl.CostEstimate(
        flops=products * heads * n * n * HEAD_SIZE * 2, bytes_accessed=8 * heads * n * HEAD_SIZE, transcendentals=heads * n * n
    )


def attn_forward(q_t, k_t, v_t, cos_t, sin_t, start):
    n = q_t.shape[1]
    hd = HEAD_SIZE
    kv = k_t.shape[0] // hd
    block = min(256, n)
    pair = pl.BlockSpec((2 * hd, n), lambda h: (h, 0))
    one = pl.BlockSpec((hd, n), lambda h: (h, 0))
    table = pl.BlockSpec((hd // 2, n), lambda h: (0, 0))
    return pl.pallas_call(
        functools.partial(attn_fwd_kernel, block),
        grid=(kv,),
        in_specs=[pair, one, one, table, table, pl.BlockSpec((1, n), lambda h: (0, 0))],
        out_specs=[pair, one, pair, pl.BlockSpec((1, 2, n), lambda h: (h, 0, 0))],
        out_shape=[
            jax.ShapeDtypeStruct(q_t.shape, BF16),
            jax.ShapeDtypeStruct(k_t.shape, BF16),
            jax.ShapeDtypeStruct(q_t.shape, BF16),
            jax.ShapeDtypeStruct((kv, 2, n), F32),
        ],
        compiler_params=pltpu.CompilerParams(vmem_limit_bytes=48 * 2**20),
        cost_estimate=attn_cost(2 * kv, n, 4),
        name="attn_forward",
    )(q_t, k_t, v_t, cos_t, sin_t, start)


def attn_backward(q_t, k_t, v_t, do_t, lse, cos_t, sin_t, start, first, count):
    n = q_t.shape[1]
    hd = HEAD_SIZE
    block = min(256, n)
    pair = pl.BlockSpec((2 * hd, n), lambda h: (h + first, 0))
    one = pl.BlockSpec((hd, n), lambda h: (h + first, 0))
    table = pl.BlockSpec((hd // 2, n), lambda h: (0, 0))
    return pl.pallas_call(
        functools.partial(attn_bwd_kernel, block),
        grid=(count,),
        in_specs=[
            pair,
            one,
            one,
            pair,
            pl.BlockSpec((1, 2, n), lambda h: (h + first, 0, 0)),
            table,
            table,
            pl.BlockSpec((1, n), lambda h: (0, 0)),
        ],
        out_specs=[pl.BlockSpec((r * hd, n), lambda h: (h, 0)) for r in (2, 1, 1)],
        out_shape=[jax.ShapeDtypeStruct((r * count * hd, n), BF16) for r in (2, 1, 1)],
        scratch_shapes=[pltpu.VMEM((hd, n), F32), pltpu.VMEM((hd, n), F32)],
        compiler_params=pltpu.CompilerParams(vmem_limit_bytes=48 * 2**20),
        cost_estimate=attn_cost(2 * count, n, 4),
        name="attn_backward",
    )(q_t, k_t, v_t, do_t, lse, cos_t, sin_t, start)


def data_kernel(first, last, blocks, tiles, slots, pieces, expert_ref, *refs):
    refs = list(refs)
    at, tile_at = pl.program_id(0), pl.program_id(1)
    x, g_all = refs[0][...], refs[blocks][...]
    for i in range(1, blocks):
        x = jnp.where(at == i, refs[i][...], x)
        g_all = jnp.where(at == i, refs[blocks + i][...], g_all)
    weights = refs[2 * blocks : 2 * blocks + slots * pieces]
    refs = refs[2 * blocks + slots * pieces :]
    if not first:
        out_in, dx_in, dgate_in = refs[:3]
        refs = refs[3:]
    if last:
        out_refs, dx_refs = refs[:blocks], refs[blocks : 2 * blocks]
        refs = refs[2 * blocks :]
    else:
        out_ref, dx_ref, dgate_ref = refs[:3]
        refs = refs[3:]
    hs, acts = refs[:slots], refs[slots : 2 * slots]
    acc_o, acc_x, held, sems = refs[2 * slots :]
    opening = (at == 0) & (tile_at == 0)

    def copies(n):
        return [pltpu.make_async_copy(weights[n].at[c], held.at[n, c], sems.at[n, c]) for c in range(3)]

    @pl.when(opening)
    def _():
        for n in range(slots * pieces):
            for copy in copies(n):
                copy.start()

    width = x.shape[1]
    g = g_all[:, :width]
    gates = g_all[:, width:].astype(F32)
    lane = lax.broadcasted_iota(jnp.int32, gates.shape, 1)
    dgate = None if first else dgate_in[...]
    for j in range(slots):
        here = lane == expert_ref[j]
        both = here | (lane == expert_ref[j] + LANES // 2)
        gate = jnp.sum(jnp.where(both, gates, 0.0), axis=1, keepdims=True)
        row_sum = None
        for i in range(pieces):
            n = j * pieces + i

            @pl.when(opening)
            def _():
                for copy in copies(n):
                    copy.wait()

            hid = held.shape[3]
            gate_pre = dot(x, held[n, 0])
            up_pre = dot(x, held[n, 1])
            d_hidden = dot(g, held[n, 2])
            sig = jax.nn.sigmoid(gate_pre)
            silu = gate_pre * sig
            act = silu * up_pre
            part = jnp.sum(act * d_hidden, axis=1, keepdims=True)
            row_sum = part if row_sum is None else row_sum + part
            act_w = (act * gate).astype(BF16)
            d_hidden = d_hidden * gate
            d_up = (d_hidden * silu).astype(BF16)
            d_gate = (d_hidden * up_pre * (sig + silu * (1.0 - sig))).astype(BF16)
            hs[j][:, 2 * i * hid : (2 * i + 1) * hid] = d_gate
            hs[j][:, (2 * i + 1) * hid : (2 * i + 2) * hid] = d_up
            acts[j][:, i * hid : (i + 1) * hid] = act_w
            out_term = dot_nt(act_w, held[n, 2])
            dx_term = dot_nt(d_gate, held[n, 0]) + dot_nt(d_up, held[n, 1])
            if n == 0 and first:
                acc_o[...] = out_term
                acc_x[...] = dx_term
            elif n == 0:
                acc_o[...] = out_in[...].astype(F32) + out_term
                acc_x[...] = dx_in[...].astype(F32) + dx_term
            else:
                acc_o[...] += out_term
                acc_x[...] += dx_term
        term = jnp.where(here, row_sum, 0.0)
        dgate = term if dgate is None else dgate + term
    if last:
        high = dgate.astype(BF16).astype(F32)
        low = pltpu.roll(dgate - high, LANES // 2, 1)
        tail = jnp.where(lane < LANES // 2, high, low).astype(BF16)
        for i in range(blocks):

            @pl.when(at == i)
            def _():
                out_refs[i][...] = acc_o[...].astype(BF16)
                dx_refs[i][:, :width] = acc_x[...].astype(BF16)
                dx_refs[i][:, width:] = tail
    else:
        out_ref[...] = acc_o[...].astype(BF16)
        dx_ref[...] = acc_x[...].astype(BF16)
        dgate_ref[...] = dgate


def expert_data(experts, xs, gs, rows, ws, carry, last):
    blocks = len(xs)
    width = xs[0][0].shape[1]
    tile = min(256, rows)
    tiles = rows // tile
    full = gs[0][0].shape[1]
    slots = experts.shape[0]
    pieces = len(ws) // slots
    hidden = ws[0].shape[2]
    first = carry is None
    total = blocks * rows

    def out_spec(columns):
        return pl.BlockSpec((tile, columns), lambda b, i: (b * tiles + i, 0))

    def in_spec(columns, offset):
        return pl.BlockSpec((tile, columns), lambda b, i: (offset * tiles + i, 0))

    def own_spec(columns, j):
        return pl.BlockSpec((tile, columns), lambda b, i: (jnp.clip((b - j) * tiles + i, 0, tiles - 1), 0))

    ins = [experts, *[x for x, _ in xs], *[g for g, _ in gs], *ws]
    specs = [pl.BlockSpec(memory_space=pltpu.SMEM)]
    specs += [in_spec(width, o) for _, o in xs] + [in_spec(full, o) for _, o in gs]
    specs += [pl.BlockSpec(memory_space=pl.ANY)] * len(ws)
    if not first:
        ins += list(carry)
        specs += [out_spec(width), out_spec(width), out_spec(LANES)]
    if last:
        out_specs = [own_spec(c, j) for c in (width, full) for j in range(blocks)]
        out_shape = [jax.ShapeDtypeStruct((rows, c), BF16) for c in (width, full) for _ in range(blocks)]
    else:
        out_specs = [out_spec(c) for c in (width, width, LANES)]
        out_shape = [jax.ShapeDtypeStruct((total, c), t) for c, t in ((width, BF16), (width, BF16), (LANES, F32))]
    n = len(out_specs)
    kept = [2 * pieces * hidden] * slots + [pieces * hidden] * slots
    single = pieces * hidden
    outs = pl.pallas_call(
        functools.partial(data_kernel, first, last, blocks, tiles, slots, pieces),
        grid=(blocks, tiles),
        in_specs=specs,
        out_specs=out_specs + [out_spec(c) for c in kept],
        out_shape=out_shape + [jax.ShapeDtypeStruct((total, c), BF16) for c in kept],
        scratch_shapes=[
            pltpu.VMEM((tile, width), F32),
            pltpu.VMEM((tile, width), F32),
            pltpu.VMEM((len(ws), 3, width, hidden), BF16),
            pltpu.SemaphoreType.DMA((len(ws), 3)),
        ],
        compiler_params=pltpu.CompilerParams(vmem_limit_bytes=60 * 2**20),
        cost_estimate=pl.CostEstimate(
            flops=3 * slots * total * width * single,
            bytes_accessed=total * width * 12 + slots * pieces * width * hidden * 6,
            transcendentals=slots * total * single,
        ),
        name="expert_data",
    )(*ins)
    result = (outs[:blocks], outs[blocks:n]) if last else outs[:n]
    return result, outs[n : n + slots], outs[n + slots :]


def weight_kernel(shape, pieces, *refs):
    xt = gt = None
    refs = list(refs)
    for blocks in shape:
        xs, gs, h, a = refs[:blocks], refs[blocks : 2 * blocks], refs[2 * blocks], refs[2 * blocks + 1]
        refs = refs[2 * blocks + 2 :]
        rows = xs[0].shape[0]
        for i in range(blocks):
            span = slice(i * rows, (i + 1) * rows)
            xp, gp = dot_tn(xs[i][...], h[span]), dot_tn(gs[i][...], a[span])
            xt, gt = (xp, gp) if xt is None else (xt + xp, gt + gp)
    outs = refs
    hid = outs[0].shape[2]
    for i in range(pieces):
        outs[i][0] = xt[:, 2 * i * hid : (2 * i + 1) * hid].astype(BF16)
        outs[i][1] = xt[:, (2 * i + 1) * hid : (2 * i + 2) * hid].astype(BF16)
        outs[i][2] = gt[:, i * hid : (i + 1) * hid].astype(BF16)


def expert_weight(parts, pieces, width):
    hidden = parts[0][4].shape[1] // pieces
    block = 256
    ins, specs, shape, total = [], [], [], 0
    for xs, gs, rows, h, a in parts:
        for v, o in [*xs, *gs]:
            ins.append(v)
            specs.append(pl.BlockSpec((rows, block), lambda i, o=o: (o, i)))
        for v in (h, a):
            ins.append(v)
            specs.append(pl.BlockSpec(v.shape, lambda i: (0, 0), pipeline_mode=pl.Buffered(1)))
        shape.append(len(xs))
        total += h.shape[0]
    return pl.pallas_call(
        functools.partial(weight_kernel, tuple(shape), pieces),
        grid=(width // block,),
        in_specs=specs,
        out_specs=[pl.BlockSpec((3, block, hidden), lambda i: (0, i, 0))] * pieces,
        out_shape=[jax.ShapeDtypeStruct((3, width, hidden), BF16)] * pieces,
        compiler_params=pltpu.CompilerParams(vmem_limit_bytes=60 * 2**20),
        cost_estimate=pl.CostEstimate(
            flops=total * width * hidden * pieces,
            bytes_accessed=total * (width * 4 + hidden * pieces * 6) + width * hidden * pieces * 6,
            transcendentals=0,
        ),
        name="expert_weight",
    )(*ins)


def rms_parts(v):
    inv = lax.rsqrt(jnp.mean(v * v, axis=1, keepdims=True) + EPS)
    return inv, v * inv


def join_kernel(pieces, at_ref, x_ref, gain_ref, *refs):
    os, ws = refs[:pieces], refs[pieces : 2 * pieces]
    mixed_ref, top_ref, low_ref = refs[2 * pieces :]
    mixed = x_ref[...].astype(F32)
    for o, w in zip(os, ws):
        mixed = mixed + dot_tn(o[...], w[...])
    mixed_ref[...] = mixed
    rows = (rms_parts(mixed)[1] * gain_ref[...]).astype(BF16)
    for i, ref in enumerate((top_ref, low_ref)):

        @pl.when(pl.program_id(0) == i)
        def _():
            ref[...] = rows


def join_heads(at, tokens, gain, os, ws, rows):
    width = tokens.shape[1]
    half = rows // 2
    heads = os[0].shape[0]
    own = pl.BlockSpec((heads, half), lambda i, at: (0, at[0] * 2 + i))
    o_specs = [own] + [pl.BlockSpec((heads, half), lambda i, at: (0, i))] * (len(os) - 1)
    if half % LANES:
        os = [lax.dynamic_slice_in_dim(os[0], at[0] * rows, rows, 1)] + os[1:]
        os = [jnp.stack([o[:, :half], o[:, half:]]) for o in os]
        o_specs = [pl.BlockSpec((None, heads, half), lambda i, at: (i, 0, 0))] * len(os)
    once = pl.BlockSpec((half, width), lambda i, at: (0, 0))
    return pl.pallas_call(
        functools.partial(join_kernel, len(os)),
        grid_spec=pltpu.PrefetchScalarGridSpec(
            num_scalar_prefetch=1,
            grid=(2,),
            in_specs=[
                pl.BlockSpec((half, width), lambda i, at: (at[0] * 2 + i, 0)),
                pl.BlockSpec((1, width), lambda i, at: (0, 0)),
            ]
            + o_specs
            + [pl.BlockSpec((heads, width), lambda i, at: (0, 0))] * len(ws),
            out_specs=[pl.BlockSpec((half, width), lambda i, at: (i, 0)), once, once],
        ),
        out_shape=[
            jax.ShapeDtypeStruct((rows, width), F32),
            jax.ShapeDtypeStruct((half, width), BF16),
            jax.ShapeDtypeStruct((half, width), BF16),
        ],
        compiler_params=pltpu.CompilerParams(vmem_limit_bytes=48 * 2**20),
        cost_estimate=pl.CostEstimate(
            flops=2 * rows * heads * len(os) * width, bytes_accessed=rows * width * 8, transcendentals=0
        ),
        name="join_heads",
    )(at, tokens, gain[None, :], *os, *ws)


def turn_kernel(near_ref, xt_ref, yl_ref, xl_ref, yt_ref, mixed_ref, grad_ref, gain_ref, dy_ref, gates_ref, sum_ref):
    step = pl.program_id(0)
    width = mixed_ref.shape[1]
    upper = step == 0
    back = near_ref[...].astype(F32)
    back = back + jnp.where(upper, xt_ref[...], xl_ref[...]).astype(F32)
    back = back + jnp.where(upper, yt_ref[...], yl_ref[...]).astype(F32)
    gates_ref[...] = back[:, width:]
    d_in = back[:, :width]
    inv, normed = rms_parts(mixed_ref[...])
    scaled = d_in * gain_ref[...]
    dots = jnp.mean(scaled * normed, axis=1, keepdims=True)
    dy_ref[...] = (grad_ref[...].astype(F32) + inv * (scaled - normed * dots)).astype(BF16)
    part = jnp.sum(d_in * normed, axis=0, keepdims=True)

    @pl.when(upper)
    def _():
        sum_ref[...] = part

    @pl.when(jnp.logical_not(upper))
    def _():
        sum_ref[...] += part


def turn_back(near, halves, others, mixed, grad_wide, gain):
    rows, width = mixed.shape
    half, full = rows // 2, near.shape[1]

    def spec(c):
        return pl.BlockSpec((half, c), lambda i: (i, 0))

    const = pl.BlockSpec((half, full), lambda i: (0, 0))
    line = pl.BlockSpec((1, width), lambda i: (0, 0))
    return pl.pallas_call(
        turn_kernel,
        grid=(2,),
        in_specs=[spec(full)] + [const] * 4 + [spec(width), spec(width), line],
        out_specs=[spec(width), spec(LANES), line],
        out_shape=[
            jax.ShapeDtypeStruct((rows, width), BF16),
            jax.ShapeDtypeStruct((rows, LANES), F32),
            jax.ShapeDtypeStruct((1, width), F32),
        ],
        compiler_params=pltpu.CompilerParams(vmem_limit_bytes=48 * 2**20),
        cost_estimate=pl.CostEstimate(flops=0, bytes_accessed=rows * width * 16, transcendentals=0),
        name="turn_back",
    )(near, *halves, *others, mixed, grad_wide, gain[None, :])


def lay_out_kernel(halves, cuts, at_ref, *refs):
    q_out, k_out, v_out, o_out = refs[2 * PLANE :]
    rows = q_out.shape[0]
    for m in range(PLANE):

        @pl.when(pl.program_id(0) == m)
        def _():
            first, second = refs[m], refs[PLANE + m]
            parts = [second] if halves == 1 else [first, second]
            for out, cut, left in zip((q_out, k_out, v_out), cuts, (0, cuts[0], cuts[0] + cuts[1])):
                for i, part in enumerate(parts):
                    out[:, i * cut : (i + 1) * cut] = part[:rows, left : left + cut].astype(F32)
            wide = 0 if halves == 1 else sum(cuts)
            o_out[...] = first[:, wide:].astype(F32).T


def lay_out(at, first, second, halves, cuts):
    rows = first[0].shape[0]
    out_width = first[0].shape[1] - (0 if halves == 1 else sum(cuts))
    shapes = [(PLANE * rows, halves * c) for c in cuts] + [(out_width, PLANE * rows)]
    specs = [pl.BlockSpec((rows, halves * c), lambda m, at: (at[0] ^ m, 0)) for c in cuts]
    return pl.pallas_call(
        functools.partial(lay_out_kernel, halves, cuts),
        grid_spec=pltpu.PrefetchScalarGridSpec(
            num_scalar_prefetch=1,
            grid=(PLANE,),
            in_specs=[pl.BlockSpec(v.shape, lambda m, at: (0, 0)) for v in [*first, *second]],
            out_specs=specs + [pl.BlockSpec((out_width, rows), lambda m, at: (0, at[0] ^ m))],
        ),
        out_shape=[jax.ShapeDtypeStruct(v, F32) for v in shapes],
        compiler_params=pltpu.CompilerParams(vmem_limit_bytes=48 * 2**20),
        cost_estimate=pl.CostEstimate(flops=0, bytes_accessed=24 * rows * out_width, transcendentals=0),
        name="lay_out",
    )(at, *first, *second)


def after(x, *others):
    leaves, tree = jax.tree.flatten(x)
    extra = jax.tree.leaves(others)
    held = lax.optimization_barrier(tuple(leaves) + tuple(extra))
    return jax.tree.unflatten(tree, held[: len(leaves)])


def body(
    tokens,
    segment_ids,
    router_logits,
    expert_ids,
    gain_attn,
    w_query,
    key_matrix,
    value_matrix,
    w_out,
    gain_mlp,
    w_gate,
    w_up,
    w_down,
    out_grad,
):
    n_tok, width = tokens.shape
    col_width = out_grad.shape[1]
    n_tensor = width // col_width
    n_expert = router_logits.shape[1]
    depth = n_expert // PLANE
    my_row = n_tok // n_tensor
    t_at = lax.axis_index("tensor")
    e_at = lax.axis_index("expert")

    def hop(x, step):
        pairs = [(i, (i + step) % n_tensor) for i in range(n_tensor)]
        return jax.tree.map(lambda a: lax.ppermute(a, "tensor", pairs), x)

    def plane(x, mask):
        pairs = [(i, i ^ mask) for i in range(n_expert)]
        return jax.tree.map(lambda a: lax.ppermute(a, "expert", pairs), x)

    def ring(x, step=1):
        pairs = [(i, (i + step * PLANE) % n_expert) for i in range(n_expert)]
        return jax.tree.map(lambda a: lax.ppermute(a, "expert", pairs), x)

    def peer(step):
        return lax.rem(t_at + step + n_tensor, n_tensor)

    def rows_of(x, who):
        return lax.dynamic_slice_in_dim(x, who * my_row, my_row, 0)

    def cols_of(x, who):
        return lax.dynamic_slice_in_dim(x, who * col_width, col_width, x.ndim - 1)

    def place(parts, axis):
        if n_tensor == 2:
            return jnp.where(t_at == 0, jnp.concatenate(parts, axis), jnp.concatenate(parts[::-1], axis))
        size = parts[0].shape[axis]
        shape = list(parts[0].shape)
        shape[axis] *= n_tensor
        out = jnp.zeros(shape, parts[0].dtype)
        for s, v in enumerate(parts):
            out = lax.dynamic_update_slice_in_dim(out, v, peer(-s) * size, axis)
        return out

    def to_rows(x):
        return place([rows_of(x, t_at)] + [hop(rows_of(x, peer(s)), s) for s in range(1, n_tensor)], 1)

    def to_cols(x):
        return place([cols_of(x, t_at)] + [hop(cols_of(x, peer(s)), s) for s in range(1, n_tensor)], 0)

    def gather_rows(x):
        return place([x] + [hop(x, s) for s in range(1, n_tensor)], 0)

    ids_rows = rows_of(expert_ids, t_at)
    logit_rows = rows_of(router_logits, t_at)
    expert_range = jnp.arange(n_expert, dtype=jnp.int32)
    used = jnp.any(ids_rows[:, :, None] == expert_range[None, None, :], axis=1)
    masked = jnp.where(used, logit_rows, NEG)
    weights = jnp.where(used, jnp.exp(masked - jnp.max(masked, axis=1, keepdims=True)), 0.0)
    gates = weights / jnp.sum(weights, axis=1, keepdims=True)
    pad = ((0, 0), (0, LANES // 2 - n_expert))
    high = lax.optimization_barrier(gates.astype(BF16))
    low = (gates - high.astype(F32)).astype(BF16)
    grad_rows = to_rows(out_grad.astype(BF16))
    grad_wide = jnp.concatenate([grad_rows, jnp.pad(high, pad), jnp.pad(low, pad)], axis=1)
    held = [jnp.stack([w_gate[0], w_up[0], w_down[0].T])]
    half_row = my_row // 2

    start = jnp.sum((segment_ids[:, None] < segment_ids[None, :]).astype(jnp.int32), axis=0)
    places = jnp.arange(n_tok, dtype=jnp.int32) - start
    half = HEAD_SIZE // 2
    freq = jnp.power(THETA, -2.0 * jnp.arange(half, dtype=F32) / HEAD_SIZE)
    angles = freq[:, None] * places.astype(F32)[None, :]
    cos_t, sin_t = jnp.cos(angles), jnp.sin(angles)
    start = start[None, :]
    held.append(ring(held[0]))
    tokens, grad_wide = after((tokens, grad_wide))
    grad_x, grad_y = plane(grad_wide, 1), plane(grad_wide, 2)
    out_pieces = [w_out] + [hop(w_out, s) for s in range(1, n_tensor)]
    slots = [[held[0]] + [hop(held[0], s) for s in range(1, n_tensor)]]
    x_full = tokens.astype(F32)
    inv_one = lax.rsqrt(jnp.mean(x_full * x_full, axis=1, keepdims=True) + EPS)
    normed_one = x_full * inv_one
    attn_in = (normed_one * gain_attn).astype(BF16)

    def project(w):
        return jnp.einsum("td,dc->ct", attn_in, w, preferred_element_type=F32)

    v_t = project(value_matrix).astype(BF16)
    q_t, k_t, o_t, lse = attn_forward(project(w_query), project(key_matrix), v_t, cos_t, sin_t, start)
    o_t, grad_x, grad_y, slots[0], out_pieces, held[1] = after((o_t, grad_x, grad_y, slots[0], out_pieces, held[1]))
    held.append(ring(held[1]))
    grad_diag = [plane(grad_x[:half_row], 2), plane(grad_y[half_row:], 1)]
    sent = [lax.dynamic_slice_in_dim(o_t, peer(s) * my_row, my_row, 1) for s in range(1, n_tensor)]
    os = [o_t] + [hop(v, s) for s, v in enumerate(sent, 1)]
    mixed, mlp_top, mlp_low = join_heads(t_at.reshape(1), tokens, gain_mlp, os, out_pieces, my_row)
    mlp_top, mlp_low, grad_diag = after((mlp_top, mlp_low, grad_diag))

    group = 2 if depth % 2 == 0 else 1
    last = depth - group
    carry = dict.fromkeys(("near", "one", "two", "diag"))
    saved = [{} for _ in range(depth)]
    where = {
        "near": ([(mlp_top, 0), (mlp_low, 0)], [(grad_wide, 0), (grad_wide, 1)]),
    }

    def run(name, k, fence=()):
        ks = range(k, k + group)
        experts = jnp.stack([lax.rem(e_at - i * PLANE + n_expert, n_expert) for i in ks])
        experts = after(experts, *fence) if fence else experts
        flat = [w for i in ks for w in slots[i]]
        xs, gs = where[name]
        carry[name], hs, acts = expert_data(experts, xs, gs, half_row, flat, carry[name], k == last)
        for i, h, a in zip(ks, hs, acts):
            saved[i][name] = (xs, gs, half_row, h, a)

    def add_slot():
        k = len(slots)
        slots.append([held[k]] + [hop(held[k], s) for s in range(1, n_tensor)])

    def weight_pieces(k, fence=()):
        parts = list(saved[k].values())
        if fence:
            xs, gs, rows, h, a = parts[0]
            parts[0] = (xs, gs, rows, after(h, *fence), a)
        return expert_weight(parts, n_tensor, width)

    def hop_back(grads):
        return [hop(grads[s], n_tensor - s) for s in range(1, n_tensor)]

    def total_of(grads, got):
        return functools.reduce(jnp.add, [v.astype(F32) for v in [grads[0], *got]])

    def weight_total(k):
        grads = weight_pieces(k)
        return total_of(grads, hop_back(grads))

    def send_on(k, moving):
        total = totals[k]
        if moving is not None:
            total = total + moving.astype(F32)
        return ring(total.astype(BF16)) if k else total

    for _ in range(1, group):
        add_slot()
    slots, mlp_top, mlp_low = after((slots, mlp_top, mlp_low))
    x_top, y_low = plane(mlp_top, 1), plane(mlp_low, 2)
    run("near", 0)
    x_top, y_low, carry["near"], held[2] = after((x_top, y_low, carry["near"], held[2]))
    for _ in range(3, depth):
        held.append(ring(held[-1]))
    x_low, y_top = plane(mlp_low, 1), plane(mlp_top, 2)
    where["one"] = ([(x_top, 0), (y_low, 0)], [(grad_x, 0), (grad_y, 1)])
    run("one", 0)
    x_low, y_top, carry["one"] = after((x_low, y_top, carry["one"]))
    mlp_diag = [plane(x_top, 2), plane(y_low, 1)]
    where["two"] = ([(x_low, 0), (y_top, 0)], [(grad_x, 1), (grad_y, 0)])
    run("two", 0)
    mlp_diag, carry["two"] = after((mlp_diag, carry["two"]))
    add_slot()
    where["diag"] = ([(v, 0) for v in mlp_diag], [(v, 0) for v in grad_diag])
    run("diag", 0)
    slots, carry["diag"] = after((slots, carry["diag"]))
    for k in range(group, last, group):
        while len(slots) < k + group:
            add_slot()
        for name in ("near", "one", "two", "diag"):
            run(name, k)
    totals = {}
    order = list(range(1, depth)) + [0]
    early = order[: depth - group - 1]
    for k in early:
        totals[k] = weight_total(k)
    while len(slots) < depth:
        add_slot()
    slots[-1], totals = after((slots[-1], totals))
    moving = None
    for k in early:
        moving = send_on(k, moving)
    rest = order[len(early) :]

    run("diag", last)
    parts = [plane(v, m) for v, m in zip(carry["diag"][1], (1, 2))]
    run("one", last, [carry["diag"]])
    parts, carry["one"] = after((parts, carry["one"]))
    halves = [plane(v, m) for v, m in zip(carry["one"][1], (1, 2))]
    run("two", last, [carry["one"]])
    low_x, top_y = ((v.astype(F32) + p.astype(F32)).astype(BF16) for v, p in zip(carry["two"][1], parts[::-1]))
    halves, low_x, top_y = after((halves, low_x, top_y))
    others = [plane(low_x, 1), plane(top_y, 2)]
    run("near", last, [low_x, top_y])
    others, carry["near"], moving = after((others, carry["near"], moving))

    near_dx = jnp.concatenate(carry["near"][1], axis=0)
    dy, d_gates, gain_two_all = turn_back(near_dx, halves, others, mixed, grad_wide, gain_mlp)
    out_diag, dy = after((carry["diag"][0], dy))
    out_parts = [plane(v, m) for v, m in zip(out_diag, (1, 2))]
    dy_full = gather_rows(dy)
    late = {rest[0]: weight_pieces(rest[0], [dy])}
    dy_full, late, out_parts = after((dy_full, late, out_parts))
    d_gates = d_gates[:, :n_expert] + d_gates[:, LANES // 2 : LANES // 2 + n_expert]

    arrived = moving
    late_got = hop_back(late[rest[0]])
    out_halves = [plane(v, m) for v, m in zip(carry["one"][0], (1, 2))]
    do_t = jnp.einsum("td,cd->ct", dy_full, w_out, preferred_element_type=F32).astype(BF16)
    out_w_grad = jnp.einsum("td,ct->dc", dy_full, o_t, preferred_element_type=F32).astype(BF16)
    kv = k_t.shape[0] // HEAD_SIZE
    parts = 2 if kv % 2 == 0 else 1
    count = kv // parts

    def backward(i, do_t):
        return attn_backward(q_t, k_t, v_t, do_t, lse, cos_t, sin_t, start, i * count, count)

    def columns(w, i):
        size = w.shape[1] // parts
        return w[:, i * size : (i + 1) * size]

    def weight_grads(ds):
        return [jnp.einsum("td,ct->dc", attn_in, d, preferred_element_type=F32).astype(BF16) for d in ds]

    def input_grads(ds, i):
        ws = (w_query, key_matrix, value_matrix)
        terms = [jnp.einsum("ct,dc->td", d, columns(w, i), preferred_element_type=F32) for d, w in zip(ds, ws)]
        return functools.reduce(jnp.add, terms)

    def part(a, who, rows):
        return lax.dynamic_slice_in_dim(a, who * rows, rows, 0)

    p_at, z_at = lax.rem(e_at, PLANE), e_at // PLANE

    def plane_shares(a):
        quarter = a.shape[0] // PLANE
        return [plane(part(a, p_at ^ m, quarter), m) for m in range(1, PLANE)]

    def plane_sum(a, shares):
        total = part(a, p_at, a.shape[0] // PLANE).astype(F32)
        for v in shares:
            total = total + v.astype(F32)
        return total.astype(BF16)

    def swap(a, bit):
        pairs = [(i, i ^ (bit * PLANE)) for i in range(n_expert)]
        return lax.ppermute(a, "expert", pairs)

    bits = [1 << i for i in range(depth.bit_length() - 1)]

    def upper(bit):
        return (z_at // bit) % 2

    def z_cut(a, bit, tail=None):
        rows = a.shape[0] // 2
        stay, go = part(a, upper(bit), rows), part(a, 1 - upper(bit), rows)
        return stay, go if tail is None else jnp.concatenate([go, tail], axis=0)

    def add(a, b):
        return (a.astype(F32) + b.astype(F32)).astype(BF16)

    def z_join(a, got, bit):
        return jnp.where(upper(bit) == 0, jnp.concatenate([a, got], 0), jnp.concatenate([got, a], 0))

    first = out_w_grad
    ds = []
    do_t, out_w_grad = after((do_t, out_w_grad))
    if parts == 2:
        ds.append(backward(0, do_t))
        ds[0], out_halves, do_t, late_got = after((ds[0], out_halves, do_t, late_got))
        first = jnp.concatenate(weight_grads(ds[0]) + [out_w_grad], axis=1)

    def next_moving(k, got, arrived):
        total = total_of(late[k], got)
        if arrived is not None:
            total = total + arrived.astype(F32)
        return total.astype(BF16)

    moving = next_moving(rest[0], late_got, arrived)
    first, out_halves, moving, do_t = after((first, out_halves, moving, do_t))
    ring_on = [ring(moving[c]) for c in range(2)]
    first_sent = plane_shares(first)
    ds.append(backward(parts - 1, do_t))
    first_sent, ring_on, ds = after((first_sent, ring_on, ds))

    second = jnp.concatenate(weight_grads(ds[-1]), axis=1)
    first = plane_sum(first, first_sent)
    stay, go = z_cut(first, bits[0])
    second, stay, go, ds = after((second, stay, go, ds))
    second_sent = plane_shares(second)
    got = swap(go, bits[0])
    ring_on.append(ring(moving[2]))
    in_terms = functools.reduce(jnp.add, [input_grads(d, i) for i, d in enumerate(ds)])
    dots = jnp.sum(in_terms * gain_attn * normed_one, axis=1)
    own_terms = cols_of(in_terms, t_at)
    far_terms = [cols_of(in_terms, peer(s)).astype(BF16) for s in range(1, n_tensor)]
    second_sent, got, ring_on, far_terms, dots = after((second_sent, got, ring_on, far_terms, dots))

    first = add(stay, got)
    out_two = [add(v, p) for v, p in zip(carry["two"][0], out_parts[::-1])]
    gain_two = cols_of(gain_two_all[0], t_at)
    far_gains = [cols_of(gain_two_all[0], peer(s)) for s in range(1, n_tensor)]
    cuts = [z_cut(first, bits[1])] if len(bits) > 1 else []
    cuts, out_two, far_terms, dots = after((cuts, out_two, far_terms, dots))
    out_others = [plane(v, m) for v, m in zip(out_two, (1, 2))]
    far_terms = [hop(v, s) for s, v in enumerate(far_terms, 1)]
    far_dots = [hop(jnp.concatenate([dots, v]), s) for s, v in enumerate(far_gains, 1)]
    gots = [swap(go, bits[1]) for _, go in cuts]
    for k in rest[1:-1]:
        late[k] = weight_pieces(k, [dots])
    gots, out_others, far_terms, far_dots, late = after((gots, out_others, far_terms, far_dots, late))
    second = plane_sum(second, second_sent)
    for (stay, _), got in zip(cuts, gots):
        first = add(stay, got)
    for bit in bits[2:]:
        stay, go = z_cut(first, bit)
        first = add(stay, swap(go, bit))
    gain_two = functools.reduce(jnp.add, [gain_two] + [v[n_tok:] for v in far_dots])
    far_dots = [v[:n_tok] for v in far_dots]

    d_attn_in = functools.reduce(jnp.add, [own_terms] + [v.astype(F32) for v in far_terms])
    all_dots = functools.reduce(jnp.add, [dots] + far_dots)
    normed_cols = cols_of(normed_one, t_at)
    scaled_one = d_attn_in * cols_of(gain_attn, t_at)
    d_norm_one = inv_one * (scaled_one - normed_cols * (all_dots / width)[:, None])
    grad_tokens = cols_of(dy_full, t_at).astype(F32) + d_norm_one
    gain_one = jnp.sum(d_attn_in * normed_cols, axis=0)
    wide = second.shape[1]
    gains = jnp.concatenate([gain_one, gain_two]).astype(BF16).reshape(-1, wide)
    gain_rows = gains.shape[0]
    gains = jnp.pad(gains, ((0, 16 - gain_rows), (0, 0)))
    grad_logits = gather_rows(gates * (d_gates - jnp.sum(gates * d_gates, axis=1, keepdims=True)))
    late_got = {k: hop_back(late[k]) for k in rest[1:-1]}
    for i, bit in enumerate(bits):
        rows = second.shape[0] // 2
        stay, go = z_cut(second, bit, gains)
        back = bits[-1 - i]
        first, go, late_got = after((first, go, late_got))
        got, first_got = swap(go, bit), swap(first, back)
        got, first_got = after((got, first_got))
        second, gains = add(stay, got[:rows]), add(gains, got[rows:])
        first = z_join(first, first_got, back)
    moving = jnp.stack(ring_on)
    for k in rest[1:-1]:
        moving = next_moving(k, late_got[k], moving)
        first, second, moving = after((first, second, moving))
        ring_on = [ring(moving[c]) for c in range(3)]
        moving = jnp.stack(ring_on[:2] + [ring_on[2]])
    first_all = [first] + [plane(first, m) for m in range(1, PLANE)]
    late[0] = weight_pieces(0, [first])
    for bit in bits[::-1]:
        second = z_join(second, swap(second, bit), bit)
    rows = second.shape[0]
    second = jnp.concatenate([second, gains], axis=0)
    out_top, out_low = carry["near"][0]
    top_rows = out_top.astype(F32) + out_halves[0].astype(F32) + out_others[1].astype(F32)
    low_rows = out_low.astype(F32) + out_others[0].astype(F32) + out_halves[1].astype(F32)
    block_out = to_cols((mixed + jnp.concatenate([top_rows, low_rows], axis=0)).astype(BF16))
    second, block_out, first_all, ring_on[:2], late[0] = after((second, block_out, first_all, ring_on[:2], late[0]))
    late_got[0] = hop_back(late[0])
    second_all = [second] + [plane(second, m) for m in range(1, PLANE)]
    gains = functools.reduce(jnp.add, [v[rows : rows + gain_rows].astype(F32) for v in second_all]).reshape(-1)
    final = [a + b.astype(F32) for a, b in zip(total_of(late[0], late_got[0]), ring_on)]
    cuts = [w.shape[1] // parts for w in (w_query, key_matrix, value_matrix)]
    grad_query, grad_key, grad_value, grad_out = lay_out(p_at.reshape(1), first_all, second_all, parts, cuts)
    return (
        block_out,
        grad_tokens,
        grad_logits,
        gains[:col_width],
        grad_query,
        grad_key,
        grad_value,
        grad_out,
        gains[col_width:],
        final[0][None],
        final[1][None],
        final[2].T[None],
    )


def solution(mesh):
    return jax.shard_map(
        body,
        mesh=mesh,
        in_specs=(
            P("expert", None),
            P("expert"),
            P("expert", None),
            P("expert", None),
            P(),
            P(None, "tensor"),
            P(None, "tensor"),
            P(None, "tensor"),
            P("tensor", None),
            P(),
            P("expert", None, "tensor"),
            P("expert", None, "tensor"),
            P("expert", "tensor", None),
            P("expert", "tensor"),
        ),
        out_specs=(
            P("expert", "tensor"),
            P("expert", "tensor"),
            P("expert", None),
            P("tensor"),
            P(None, "tensor"),
            P(None, "tensor"),
            P(None, "tensor"),
            P("tensor", None),
            P("tensor"),
            P("expert", None, "tensor"),
            P("expert", None, "tensor"),
            P("expert", "tensor", None),
        ),
        check_vma=False,
    )
```

```python
import functools

import jax
import jax.numpy as jnp
from jax import lax
from jax.experimental import pallas as pl
from jax.experimental.pallas import tpu as pltpu
from jax.sharding import PartitionSpec as P

HEAD_SIZE = 64
EPS = 1e-06
THETA = 10000.0
NEG = -1e30
PLANE = 4
LANES = 128
F32 = jnp.float32
BF16 = jnp.bfloat16
NT = (((1,), (1,)), ((), ()))
TN = (((0,), (0,)), ((), ()))


def dot(a, b):
    return jnp.dot(a, b, preferred_element_type=F32)


def dot_nt(a, b):
    return lax.dot_general(a, b, NT, preferred_element_type=F32)


def dot_tn(a, b):
    return lax.dot_general(a, b, TN, preferred_element_type=F32)


def attn_mask(start, row_start, block, keys):
    first = start[:, row_start : row_start + block]
    first = jnp.concatenate([first, first], axis=1)
    key_at = lax.broadcasted_iota(jnp.int32, (keys, 2 * block), 0)
    lane = lax.broadcasted_iota(jnp.int32, (1, 2 * block), 1)
    row_at = row_start + jnp.where(lane >= block, lane - block, lane)
    return (key_at >= first) & (key_at <= row_at)


def rope(x, c, s):
    half = x.shape[0] // 2
    a, b = x[:half], x[half:]
    return jnp.concatenate([a * c - b * s, b * c + a * s], axis=0)


def attn_fwd_kernel(block, q_ref, k_ref, v_ref, cos_ref, sin_ref, start_ref, qo_ref, ko_ref, o_ref, lse_ref):
    hd = HEAD_SIZE
    n = k_ref.shape[1]
    c, s = cos_ref[...], sin_ref[...]
    k_rot = rope(k_ref[...], c, s)
    ko_ref[...] = k_rot.astype(BF16)
    keys = k_rot.T.astype(BF16)
    q0 = rope(q_ref[0:hd], c, s).astype(BF16)
    q1 = rope(q_ref[hd : 2 * hd], c, s).astype(BF16)
    qo_ref[0:hd] = q0
    qo_ref[hd : 2 * hd] = q1
    start = start_ref[...]
    for r0 in range(0, n, block):
        cn = r0 + block
        qb = jnp.concatenate([q0[:, r0:cn], q1[:, r0:cn]], axis=1) * jnp.asarray(hd**-0.5, BF16)
        scores = dot(keys[:cn], qb)
        scores = jnp.where(attn_mask(start, r0, block, cn), scores, NEG)
        peak = jnp.max(scores, axis=0, keepdims=True)
        p = jnp.exp(scores - peak)
        total = jnp.sum(p, axis=0, keepdims=True)
        o = dot(v_ref[:, :cn], p.astype(BF16)) / total
        o_ref[0:hd, r0:cn] = o[:, :block].astype(BF16)
        o_ref[hd : 2 * hd, r0:cn] = o[:, block:].astype(BF16)
        lse = peak + jnp.log(total)
        lse_ref[0, 0:1, r0:cn] = lse[:, :block]
        lse_ref[0, 1:2, r0:cn] = lse[:, block:]


def attn_bwd_kernel(
    block, q_ref, k_ref, v_ref, do_ref, lse_ref, cos_ref, sin_ref, start_ref, dq_ref, dk_ref, dv_ref, dk_acc, dv_acc
):
    hd = HEAD_SIZE
    n = k_ref.shape[1]
    c, s = cos_ref[...], sin_ref[...]
    keys = k_ref[...].astype(F32).T.astype(BF16)
    vals = v_ref[...].astype(F32).T.astype(BF16)
    start = start_ref[...]
    dk_acc[...] = jnp.zeros_like(dk_acc)
    dv_acc[...] = jnp.zeros_like(dv_acc)
    scale = hd**-0.5
    for r0 in range(0, n, block):
        cn = r0 + block
        qb = jnp.concatenate([q_ref[0:hd, r0:cn], q_ref[hd : 2 * hd, r0:cn]], axis=1)
        gb = jnp.concatenate([do_ref[0:hd, r0:cn], do_ref[hd : 2 * hd, r0:cn]], axis=1)
        lse = jnp.concatenate([lse_ref[0, 0:1, r0:cn], lse_ref[0, 1:2, r0:cn]], axis=1)
        scores = dot(keys[:cn], qb * jnp.asarray(scale, BF16))
        p = jnp.exp(jnp.where(attn_mask(start, r0, block, cn), scores, NEG) - lse)
        dv_acc[:, :cn] += dot_nt(gb, p.astype(BF16))
        dp = dot(vals[:cn], gb)
        delta = jnp.sum(p * dp, axis=0, keepdims=True)
        ds = (p * (dp - delta) * scale).astype(BF16)
        dq = dot(k_ref[:, :cn], ds)
        dk_acc[:, :cn] += dot_nt(qb, ds)
        cb, sb = c[:, r0:cn], -s[:, r0:cn]
        dq_ref[0:hd, r0:cn] = rope(dq[:, :block], cb, sb).astype(BF16)
        dq_ref[hd : 2 * hd, r0:cn] = rope(dq[:, block:], cb, sb).astype(BF16)
    dk_ref[...] = rope(dk_acc[...], c, -s).astype(BF16)
    dv_ref[...] = dv_acc[...].astype(BF16)


def attn_cost(heads, n, products):
    return pl.CostEstimate(
        flops=products * heads * n * n * HEAD_SIZE * 2, bytes_accessed=8 * heads * n * HEAD_SIZE, transcendentals=heads * n * n
    )


def attn_forward(q_t, k_t, v_t, cos_t, sin_t, start, first, count):
    n = q_t.shape[1]
    hd = HEAD_SIZE
    block = min(256, n)
    pair = pl.BlockSpec((2 * hd, n), lambda h: (h + first, 0))
    one = pl.BlockSpec((hd, n), lambda h: (h + first, 0))
    table = pl.BlockSpec((hd // 2, n), lambda h: (0, 0))
    return pl.pallas_call(
        functools.partial(attn_fwd_kernel, block),
        grid=(count,),
        in_specs=[pair, one, one, table, table, pl.BlockSpec((1, n), lambda h: (0, 0))],
        out_specs=[pl.BlockSpec((r * hd, n), lambda h: (h, 0)) for r in (2, 1, 2)]
        + [pl.BlockSpec((1, 2, n), lambda h: (h, 0, 0))],
        out_shape=[jax.ShapeDtypeStruct((r * count * hd, n), BF16) for r in (2, 1, 2)]
        + [jax.ShapeDtypeStruct((count, 2, n), F32)],
        compiler_params=pltpu.CompilerParams(vmem_limit_bytes=48 * 2**20),
        cost_estimate=attn_cost(2 * count, n, 4),
        name="attn_forward",
    )(q_t, k_t, v_t, cos_t, sin_t, start)


def attn_backward(q_t, k_t, v_t, do_t, lse, cos_t, sin_t, start, first, count):
    n = q_t.shape[1]
    hd = HEAD_SIZE
    block = min(256, n)
    table = pl.BlockSpec((hd // 2, n), lambda h: (0, 0))
    return pl.pallas_call(
        functools.partial(attn_bwd_kernel, block),
        grid=(count,),
        in_specs=[
            pl.BlockSpec((2 * hd, n), lambda h: (h, 0)),
            pl.BlockSpec((hd, n), lambda h: (h, 0)),
            pl.BlockSpec((hd, n), lambda h: (h + first, 0)),
            pl.BlockSpec((2 * hd, n), lambda h: (h + first, 0)),
            pl.BlockSpec((1, 2, n), lambda h: (h, 0, 0)),
            table,
            table,
            pl.BlockSpec((1, n), lambda h: (0, 0)),
        ],
        out_specs=[pl.BlockSpec((r * hd, n), lambda h: (h, 0)) for r in (2, 1, 1)],
        out_shape=[jax.ShapeDtypeStruct((r * count * hd, n), BF16) for r in (2, 1, 1)],
        scratch_shapes=[pltpu.VMEM((hd, n), F32), pltpu.VMEM((hd, n), F32)],
        compiler_params=pltpu.CompilerParams(vmem_limit_bytes=48 * 2**20),
        cost_estimate=attn_cost(2 * count, n, 4),
        name="attn_backward",
    )(q_t, k_t, v_t, do_t, lse, cos_t, sin_t, start)


def data_kernel(first, last, blocks, tiles, slots, pieces, expert_ref, *refs):
    refs = list(refs)
    at, tile_at = pl.program_id(0), pl.program_id(1)
    x, g_all = refs[0][...], refs[blocks][...]
    for i in range(1, blocks):
        x = jnp.where(at == i, refs[i][...], x)
        g_all = jnp.where(at == i, refs[blocks + i][...], g_all)
    weights = refs[2 * blocks : 2 * blocks + slots * pieces]
    refs = refs[2 * blocks + slots * pieces :]
    if not first:
        out_in, dx_in, dgate_in = refs[:3]
        refs = refs[3:]
    if last:
        out_refs, dx_refs = refs[:blocks], refs[blocks : 2 * blocks]
        refs = refs[2 * blocks :]
    else:
        out_ref, dx_ref, dgate_ref = refs[:3]
        refs = refs[3:]
    hs, acts = refs[:slots], refs[slots : 2 * slots]
    acc_o, acc_x, held, sems = refs[2 * slots :]
    opening = (at == 0) & (tile_at == 0)

    def copies(n):
        return [pltpu.make_async_copy(weights[n].at[c], held.at[n, c], sems.at[n, c]) for c in range(3)]

    @pl.when(opening)
    def _():
        for n in range(slots * pieces):
            for copy in copies(n):
                copy.start()

    width = x.shape[1]
    g = g_all[:, :width]
    gates = g_all[:, width:].astype(F32)
    lane = lax.broadcasted_iota(jnp.int32, gates.shape, 1)
    dgate = None if first else dgate_in[...]
    for j in range(slots):
        here = lane == expert_ref[j]
        both = here | (lane == expert_ref[j] + LANES // 2)
        gate = jnp.sum(jnp.where(both, gates, 0.0), axis=1, keepdims=True)
        row_sum = None
        for i in range(pieces):
            n = j * pieces + i

            @pl.when(opening)
            def _():
                for copy in copies(n):
                    copy.wait()

            hid = held.shape[3]
            gate_pre = dot(x, held[n, 0])
            up_pre = dot(x, held[n, 1])
            d_hidden = dot(g, held[n, 2])
            sig = jax.nn.sigmoid(gate_pre)
            silu = gate_pre * sig
            act = silu * up_pre
            part = jnp.sum(act * d_hidden, axis=1, keepdims=True)
            row_sum = part if row_sum is None else row_sum + part
            act_w = (act * gate).astype(BF16)
            d_hidden = d_hidden * gate
            d_up = (d_hidden * silu).astype(BF16)
            d_gate = (d_hidden * up_pre * (sig + silu * (1.0 - sig))).astype(BF16)
            hs[j][:, 2 * i * hid : (2 * i + 1) * hid] = d_gate
            hs[j][:, (2 * i + 1) * hid : (2 * i + 2) * hid] = d_up
            acts[j][:, i * hid : (i + 1) * hid] = act_w
            out_term = dot_nt(act_w, held[n, 2])
            dx_term = dot_nt(d_gate, held[n, 0]) + dot_nt(d_up, held[n, 1])
            if n == 0 and first:
                acc_o[...] = out_term
                acc_x[...] = dx_term
            elif n == 0:
                acc_o[...] = out_in[...].astype(F32) + out_term
                acc_x[...] = dx_in[...].astype(F32) + dx_term
            else:
                acc_o[...] += out_term
                acc_x[...] += dx_term
        term = jnp.where(here, row_sum, 0.0)
        dgate = term if dgate is None else dgate + term
    if last:
        high = dgate.astype(BF16).astype(F32)
        low = pltpu.roll(dgate - high, LANES // 2, 1)
        tail = jnp.where(lane < LANES // 2, high, low).astype(BF16)
        for i in range(blocks):

            @pl.when(at == i)
            def _():
                out_refs[i][...] = acc_o[...].astype(BF16)
                dx_refs[i][:, :width] = acc_x[...].astype(BF16)
                dx_refs[i][:, width:] = tail
    else:
        out_ref[...] = acc_o[...].astype(BF16)
        dx_ref[...] = acc_x[...].astype(BF16)
        dgate_ref[...] = dgate


def expert_data(experts, xs, gs, rows, ws, carry, last):
    blocks = len(xs)
    width = xs[0][0].shape[1]
    tile = min(256, rows)
    tiles = rows // tile
    full = gs[0][0].shape[1]
    slots = experts.shape[0]
    pieces = len(ws) // slots
    hidden = ws[0].shape[2]
    first = carry is None
    total = blocks * rows

    def out_spec(columns):
        return pl.BlockSpec((tile, columns), lambda b, i: (b * tiles + i, 0))

    def in_spec(columns, offset):
        return pl.BlockSpec((tile, columns), lambda b, i: (offset * tiles + i, 0))

    def own_spec(columns, j):
        return pl.BlockSpec((tile, columns), lambda b, i: (jnp.clip((b - j) * tiles + i, 0, tiles - 1), 0))

    ins = [experts, *[x for x, _ in xs], *[g for g, _ in gs], *ws]
    specs = [pl.BlockSpec(memory_space=pltpu.SMEM)]
    specs += [in_spec(width, o) for _, o in xs] + [in_spec(full, o) for _, o in gs]
    specs += [pl.BlockSpec(memory_space=pl.ANY)] * len(ws)
    if not first:
        ins += list(carry)
        specs += [out_spec(width), out_spec(width), out_spec(LANES)]
    if last:
        out_specs = [own_spec(c, j) for c in (width, full) for j in range(blocks)]
        out_shape = [jax.ShapeDtypeStruct((rows, c), BF16) for c in (width, full) for _ in range(blocks)]
    else:
        out_specs = [out_spec(c) for c in (width, width, LANES)]
        out_shape = [jax.ShapeDtypeStruct((total, c), t) for c, t in ((width, BF16), (width, BF16), (LANES, F32))]
    n = len(out_specs)
    kept = [2 * pieces * hidden] * slots + [pieces * hidden] * slots
    single = pieces * hidden
    outs = pl.pallas_call(
        functools.partial(data_kernel, first, last, blocks, tiles, slots, pieces),
        grid=(blocks, tiles),
        in_specs=specs,
        out_specs=out_specs + [out_spec(c) for c in kept],
        out_shape=out_shape + [jax.ShapeDtypeStruct((total, c), BF16) for c in kept],
        scratch_shapes=[
            pltpu.VMEM((tile, width), F32),
            pltpu.VMEM((tile, width), F32),
            pltpu.VMEM((len(ws), 3, width, hidden), BF16),
            pltpu.SemaphoreType.DMA((len(ws), 3)),
        ],
        compiler_params=pltpu.CompilerParams(vmem_limit_bytes=60 * 2**20),
        cost_estimate=pl.CostEstimate(
            flops=3 * slots * total * width * single,
            bytes_accessed=total * width * 12 + slots * pieces * width * hidden * 6,
            transcendentals=slots * total * single,
        ),
        name="expert_data",
    )(*ins)
    result = (outs[:blocks], outs[blocks:n]) if last else outs[:n]
    return result, outs[n : n + slots], outs[n + slots :]


def weight_kernel(shape, pieces, *refs):
    xt = gt = None
    refs = list(refs)
    for blocks in shape:
        xs, gs, h, a = refs[:blocks], refs[blocks : 2 * blocks], refs[2 * blocks], refs[2 * blocks + 1]
        refs = refs[2 * blocks + 2 :]
        rows = xs[0].shape[0]
        for i in range(blocks):
            span = slice(i * rows, (i + 1) * rows)
            xp, gp = dot_tn(xs[i][...], h[span]), dot_tn(gs[i][...], a[span])
            xt, gt = (xp, gp) if xt is None else (xt + xp, gt + gp)
    outs = refs
    hid = outs[0].shape[2]
    for i in range(pieces):
        outs[i][0] = xt[:, 2 * i * hid : (2 * i + 1) * hid].astype(BF16)
        outs[i][1] = xt[:, (2 * i + 1) * hid : (2 * i + 2) * hid].astype(BF16)
        outs[i][2] = gt[:, i * hid : (i + 1) * hid].astype(BF16)


def expert_weight(parts, pieces, width):
    hidden = parts[0][4].shape[1] // pieces
    block = 256
    ins, specs, shape, total = [], [], [], 0
    for xs, gs, rows, h, a in parts:
        for v, o in [*xs, *gs]:
            ins.append(v)
            specs.append(pl.BlockSpec((rows, block), lambda i, o=o: (o, i)))
        for v in (h, a):
            ins.append(v)
            specs.append(pl.BlockSpec(v.shape, lambda i: (0, 0), pipeline_mode=pl.Buffered(1)))
        shape.append(len(xs))
        total += h.shape[0]
    return pl.pallas_call(
        functools.partial(weight_kernel, tuple(shape), pieces),
        grid=(width // block,),
        in_specs=specs,
        out_specs=[pl.BlockSpec((3, block, hidden), lambda i: (0, i, 0))] * pieces,
        out_shape=[jax.ShapeDtypeStruct((3, width, hidden), BF16)] * pieces,
        compiler_params=pltpu.CompilerParams(vmem_limit_bytes=60 * 2**20),
        cost_estimate=pl.CostEstimate(
            flops=total * width * hidden * pieces,
            bytes_accessed=total * (width * 4 + hidden * pieces * 6) + width * hidden * pieces * 6,
            transcendentals=0,
        ),
        name="expert_weight",
    )(*ins)


def rms_parts(v):
    inv = lax.rsqrt(jnp.mean(v * v, axis=1, keepdims=True) + EPS)
    return inv, v * inv


def join_kernel(pieces, at_ref, x_ref, gain_ref, *refs):
    os, ws = refs[:pieces], refs[pieces : 2 * pieces]
    mixed_ref, top_ref, low_ref = refs[2 * pieces :]
    mixed = x_ref[...].astype(F32)
    for o, w in zip(os, ws):
        mixed = mixed + dot_tn(o[...], w[...])
    mixed_ref[...] = mixed
    rows = (rms_parts(mixed)[1] * gain_ref[...]).astype(BF16)
    for i, ref in enumerate((top_ref, low_ref)):

        @pl.when(pl.program_id(0) == i)
        def _():
            ref[...] = rows


def join_heads(at, tokens, gain, own, far, ws, rows):
    width = tokens.shape[1]
    half = rows // 2
    heads = own[0].shape[0]
    n = len(ws)
    o_specs = [pl.BlockSpec((heads, half), lambda i, at: (0, at[0] * 2 + i))] * len(own)
    o_specs += [pl.BlockSpec((heads, half), lambda i, at: (0, i))] * len(far)
    os = [*own, *far]
    if half % LANES:
        os = [lax.dynamic_slice_in_dim(o, at[0] * rows, rows, 1) for o in own] + far
        os = [jnp.stack([o[:, :half], o[:, half:]]) for o in os]
        o_specs = [pl.BlockSpec((None, heads, half), lambda i, at: (i, 0, 0))] * n
    once = pl.BlockSpec((half, width), lambda i, at: (0, 0))
    return pl.pallas_call(
        functools.partial(join_kernel, n),
        grid_spec=pltpu.PrefetchScalarGridSpec(
            num_scalar_prefetch=1,
            grid=(2,),
            in_specs=[
                pl.BlockSpec((half, width), lambda i, at: (at[0] * 2 + i, 0)),
                pl.BlockSpec((1, width), lambda i, at: (0, 0)),
            ]
            + o_specs
            + [pl.BlockSpec((heads, width), lambda i, at, b=b: (b, 0)) for _, b in ws],
            out_specs=[pl.BlockSpec((half, width), lambda i, at: (i, 0)), once, once],
        ),
        out_shape=[
            jax.ShapeDtypeStruct((rows, width), F32),
            jax.ShapeDtypeStruct((half, width), BF16),
            jax.ShapeDtypeStruct((half, width), BF16),
        ],
        compiler_params=pltpu.CompilerParams(vmem_limit_bytes=48 * 2**20),
        cost_estimate=pl.CostEstimate(
            flops=2 * rows * heads * n * width, bytes_accessed=rows * width * 8, transcendentals=0
        ),
        name="join_heads",
    )(at, tokens, gain[None, :], *os, *[w for w, _ in ws])


def input_kernel(groups, n_tensor, at_ref, x_ref, gain_ref, *refs):
    ds, ws = refs[: 3 * groups], refs[3 * groups : 3 * groups + 3]
    own_ref, *fars, dots_ref, acc = refs[3 * groups + 3 :]
    total = None
    for j in range(3):
        d = jnp.concatenate([ds[3 * i + j][...] for i in range(groups)], axis=0)
        term = lax.dot_general(d, ws[j][...], (((0,), (1,)), ((), ())), preferred_element_type=F32)
        total = term if total is None else total + term
    acc[...] = total
    normed = rms_parts(x_ref[...].astype(F32))[1]
    dots_ref[...] = jnp.sum(total * gain_ref[...] * normed, axis=1, keepdims=True)
    cols = own_ref.shape[1]
    for s, ref in enumerate([own_ref, *fars]):
        who = lax.rem(at_ref[0] + s, n_tensor)
        ref[...] = acc[:, pl.ds(pl.multiple_of(who * cols, cols), cols)].astype(ref.dtype)


def input_terms(at, tokens, gain, ds, ws, n_tensor):
    n, width = tokens.shape
    cols = width // n_tensor
    tile = min(256, n)
    flat = [d for group in ds for d in group]
    return pl.pallas_call(
        functools.partial(input_kernel, len(ds), n_tensor),
        grid_spec=pltpu.PrefetchScalarGridSpec(
            num_scalar_prefetch=1,
            grid=(n // tile,),
            in_specs=[pl.BlockSpec((tile, width), lambda i, at: (i, 0)), pl.BlockSpec((1, width), lambda i, at: (0, 0))]
            + [pl.BlockSpec((d.shape[0], tile), lambda i, at: (0, i)) for d in flat]
            + [pl.BlockSpec(w.shape, lambda i, at: (0, 0)) for w in ws],
            out_specs=[pl.BlockSpec((tile, cols), lambda i, at: (i, 0))] * n_tensor
            + [pl.BlockSpec((tile, 1), lambda i, at: (i, 0))],
            scratch_shapes=[pltpu.VMEM((tile, width), F32)],
        ),
        out_shape=[jax.ShapeDtypeStruct((n, cols), F32)]
        + [jax.ShapeDtypeStruct((n, cols), BF16)] * (n_tensor - 1)
        + [jax.ShapeDtypeStruct((n, 1), F32)],
        compiler_params=pltpu.CompilerParams(vmem_limit_bytes=48 * 2**20),
        cost_estimate=pl.CostEstimate(
            flops=2 * n * width * sum(w.shape[1] for w in ws), bytes_accessed=n * width * 8, transcendentals=0
        ),
        name="input_terms",
    )(at, tokens, gain[None, :], *flat, *ws)


def turn_kernel(top_ref, low_ref, xt_ref, yl_ref, xl_ref, yt_ref, mixed_ref, grad_ref, gain_ref, dy_ref, gates_ref, sum_ref):
    step = pl.program_id(0)
    width = mixed_ref.shape[1]
    upper = step == 0
    back = jnp.where(upper, top_ref[...], low_ref[...]).astype(F32)
    back = back + jnp.where(upper, xt_ref[...], xl_ref[...]).astype(F32)
    back = back + jnp.where(upper, yt_ref[...], yl_ref[...]).astype(F32)
    gates_ref[...] = back[:, width:]
    d_in = back[:, :width]
    inv, normed = rms_parts(mixed_ref[...])
    scaled = d_in * gain_ref[...]
    dots = jnp.mean(scaled * normed, axis=1, keepdims=True)
    dy_ref[...] = (grad_ref[...].astype(F32) + inv * (scaled - normed * dots)).astype(BF16)
    part = jnp.sum(d_in * normed, axis=0, keepdims=True)

    @pl.when(upper)
    def _():
        sum_ref[...] = part

    @pl.when(jnp.logical_not(upper))
    def _():
        sum_ref[...] += part


def turn_back(near, halves, others, mixed, grad_wide, gain):
    rows, width = mixed.shape
    half, full = rows // 2, near[0].shape[1]

    def spec(c):
        return pl.BlockSpec((half, c), lambda i: (i, 0))

    const = pl.BlockSpec((half, full), lambda i: (0, 0))
    line = pl.BlockSpec((1, width), lambda i: (0, 0))
    return pl.pallas_call(
        turn_kernel,
        grid=(2,),
        in_specs=[const] * 6 + [spec(width), spec(width), line],
        out_specs=[spec(width), spec(LANES), line],
        out_shape=[
            jax.ShapeDtypeStruct((rows, width), BF16),
            jax.ShapeDtypeStruct((rows, LANES), F32),
            jax.ShapeDtypeStruct((1, width), F32),
        ],
        compiler_params=pltpu.CompilerParams(vmem_limit_bytes=48 * 2**20),
        cost_estimate=pl.CostEstimate(flops=0, bytes_accessed=rows * width * 16, transcendentals=0),
        name="turn_back",
    )(*near, *halves, *others, mixed, grad_wide, gain[None, :])


def lay_out_kernel(halves, cuts, at_ref, *refs):
    q_out, k_out, v_out, o_out = refs[2 * PLANE :]
    rows = q_out.shape[0]
    for m in range(PLANE):

        @pl.when(pl.program_id(0) == m)
        def _():
            first, second = refs[m], refs[PLANE + m]
            parts = [second] if halves == 1 else [first, second]
            for out, cut, left in zip((q_out, k_out, v_out), cuts, (0, cuts[0], cuts[0] + cuts[1])):
                for i, part in enumerate(parts):
                    out[:, i * cut : (i + 1) * cut] = part[:rows, left : left + cut].astype(F32)
            wide = 0 if halves == 1 else sum(cuts)
            o_out[...] = first[:, wide:].astype(F32).T


def lay_out(at, first, second, halves, cuts):
    rows = first[0].shape[0]
    out_width = first[0].shape[1] - (0 if halves == 1 else sum(cuts))
    shapes = [(PLANE * rows, halves * c) for c in cuts] + [(out_width, PLANE * rows)]
    specs = [pl.BlockSpec((rows, halves * c), lambda m, at: (at[0] ^ m, 0)) for c in cuts]
    return pl.pallas_call(
        functools.partial(lay_out_kernel, halves, cuts),
        grid_spec=pltpu.PrefetchScalarGridSpec(
            num_scalar_prefetch=1,
            grid=(PLANE,),
            in_specs=[pl.BlockSpec(v.shape, lambda m, at: (0, 0)) for v in [*first, *second]],
            out_specs=specs + [pl.BlockSpec((out_width, rows), lambda m, at: (0, at[0] ^ m))],
        ),
        out_shape=[jax.ShapeDtypeStruct(v, F32) for v in shapes],
        compiler_params=pltpu.CompilerParams(vmem_limit_bytes=48 * 2**20),
        cost_estimate=pl.CostEstimate(flops=0, bytes_accessed=24 * rows * out_width, transcendentals=0),
        name="lay_out",
    )(at, *first, *second)


def after(x, *others):
    leaves, tree = jax.tree.flatten(x)
    extra = jax.tree.leaves(others)
    held = lax.optimization_barrier(tuple(leaves) + tuple(extra))
    return jax.tree.unflatten(tree, held[: len(leaves)])


def body(
    tokens,
    segment_ids,
    router_logits,
    expert_ids,
    gain_attn,
    w_query,
    key_matrix,
    value_matrix,
    w_out,
    gain_mlp,
    w_gate,
    w_up,
    w_down,
    out_grad,
):
    n_tok, width = tokens.shape
    col_width = out_grad.shape[1]
    n_tensor = width // col_width
    n_expert = router_logits.shape[1]
    depth = n_expert // PLANE
    my_row = n_tok // n_tensor
    t_at = lax.axis_index("tensor")
    e_at = lax.axis_index("expert")

    def hop(x, step):
        pairs = [(i, (i + step) % n_tensor) for i in range(n_tensor)]
        return jax.tree.map(lambda a: lax.ppermute(a, "tensor", pairs), x)

    def plane(x, mask):
        pairs = [(i, i ^ mask) for i in range(n_expert)]
        return jax.tree.map(lambda a: lax.ppermute(a, "expert", pairs), x)

    def ring(x, step=1):
        pairs = [(i, (i + step * PLANE) % n_expert) for i in range(n_expert)]
        return jax.tree.map(lambda a: lax.ppermute(a, "expert", pairs), x)

    def peer(step):
        return lax.rem(t_at + step + n_tensor, n_tensor)

    def rows_of(x, who):
        return lax.dynamic_slice_in_dim(x, who * my_row, my_row, 0)

    def cols_of(x, who):
        return lax.dynamic_slice_in_dim(x, who * col_width, col_width, x.ndim - 1)

    def place(parts, axis):
        if n_tensor == 2:
            return jnp.where(t_at == 0, jnp.concatenate(parts, axis), jnp.concatenate(parts[::-1], axis))
        size = parts[0].shape[axis]
        shape = list(parts[0].shape)
        shape[axis] *= n_tensor
        out = jnp.zeros(shape, parts[0].dtype)
        for s, v in enumerate(parts):
            out = lax.dynamic_update_slice_in_dim(out, v, peer(-s) * size, axis)
        return out

    def to_rows(x):
        return place([rows_of(x, t_at)] + [hop(rows_of(x, peer(s)), s) for s in range(1, n_tensor)], 1)

    def to_cols(x):
        return place([cols_of(x, t_at)] + [hop(cols_of(x, peer(s)), s) for s in range(1, n_tensor)], 0)

    def gather_rows(x):
        return place([x] + [hop(x, s) for s in range(1, n_tensor)], 0)

    ids_rows = rows_of(expert_ids, t_at)
    logit_rows = rows_of(router_logits, t_at)
    expert_range = jnp.arange(n_expert, dtype=jnp.int32)
    used = jnp.any(ids_rows[:, :, None] == expert_range[None, None, :], axis=1)
    masked = jnp.where(used, logit_rows, NEG)
    weights = jnp.where(used, jnp.exp(masked - jnp.max(masked, axis=1, keepdims=True)), 0.0)
    gates = weights / jnp.sum(weights, axis=1, keepdims=True)
    pad = ((0, 0), (0, LANES // 2 - n_expert))
    high = lax.optimization_barrier(gates.astype(BF16))
    low = (gates - high.astype(F32)).astype(BF16)
    gate_pair = jnp.concatenate([jnp.pad(high, pad), jnp.pad(low, pad)], axis=1)
    grad_low = out_grad.astype(BF16)
    grad_cols = [rows_of(grad_low, peer(s)) for s in range(n_tensor)]
    grad_cols, w_up, gate_pair = after((grad_cols, w_up, gate_pair))
    grad_cols = [grad_cols[0]] + [hop(grad_cols[s], s) for s in range(1, n_tensor)]
    held = [jnp.stack([w_gate[0], w_up[0], w_down[0].T])]
    grad_cols, held[0] = after((grad_cols, held[0]))
    grad_wide = jnp.concatenate([place(grad_cols, 1), gate_pair], axis=1)
    half_row = my_row // 2

    start = jnp.sum((segment_ids[:, None] < segment_ids[None, :]).astype(jnp.int32), axis=0)
    places = jnp.arange(n_tok, dtype=jnp.int32) - start
    half = HEAD_SIZE // 2
    freq = jnp.power(THETA, -2.0 * jnp.arange(half, dtype=F32) / HEAD_SIZE)
    angles = freq[:, None] * places.astype(F32)[None, :]
    cos_t, sin_t = jnp.cos(angles), jnp.sin(angles)
    start = start[None, :]
    held.append(ring(held[0]))
    tokens, grad_wide = after((tokens, grad_wide))
    grad_x, grad_y = plane(grad_wide, 1), plane(grad_wide, 2)
    out_pieces = [w_out] + [hop(w_out, s) for s in range(1, n_tensor)]
    slots = [[held[0]] + [hop(held[0], s) for s in range(1, n_tensor)]]
    x_full = tokens.astype(F32)
    inv_one = lax.rsqrt(jnp.mean(x_full * x_full, axis=1, keepdims=True) + EPS)
    normed_one = x_full * inv_one
    attn_in = (normed_one * gain_attn).astype(BF16)

    def project(w):
        return jnp.einsum("td,dc->ct", attn_in, w, preferred_element_type=F32)

    v_t = project(value_matrix).astype(BF16)
    q_pre, k_pre = project(w_query), project(key_matrix)
    kv = k_pre.shape[0] // HEAD_SIZE
    parts = 2 if kv % 2 == 0 else 1
    count = kv // parts
    q_t, k_t, o_t, lse = ([None] * parts for _ in range(4))
    far_os = []

    def head_group(i):
        q_t[i], k_t[i], o_t[i], lse[i] = attn_forward(q_pre, k_pre, v_t, cos_t, sin_t, start, i * count, count)

    def far_heads(i):
        sent = [lax.dynamic_slice_in_dim(o_t[i], peer(s) * my_row, my_row, 1) for s in range(1, n_tensor)]
        return [hop(v, s) for s, v in enumerate(sent, 1)]

    for i in range(parts):
        head_group(i)
    o_t, grad_x, grad_y = after((o_t, grad_x, grad_y))
    grad_diag = [plane(grad_x[:half_row], 2), plane(grad_y[half_row:], 1)]
    far_os = [far_heads(i) for i in range(parts)]
    far = [far_os[i][s] for s in range(n_tensor - 1) for i in range(parts)]
    out_ws = [(w, i) for w in out_pieces for i in range(parts)]
    mixed, mlp_top, mlp_low = join_heads(t_at.reshape(1), tokens, gain_mlp, o_t, far, out_ws, my_row)
    mlp_top, mlp_low, grad_diag, held[1] = after((mlp_top, mlp_low, grad_diag, held[1]))
    held.append(ring(held[1]))

    group = 2 if depth % 2 == 0 else 1
    last = depth - group
    carry = dict.fromkeys(("near", "one", "two", "diag"))
    saved = [{} for _ in range(depth)]
    where = {
        "near": ([(mlp_top, 0), (mlp_low, 0)], [(grad_wide, 0), (grad_wide, 1)]),
    }

    def run(name, k, fence=()):
        ks = range(k, k + group)
        experts = jnp.stack([lax.rem(e_at - i * PLANE + n_expert, n_expert) for i in ks])
        experts = after(experts, *fence) if fence else experts
        flat = [w for i in ks for w in slots[i]]
        xs, gs = where[name]
        carry[name], hs, acts = expert_data(experts, xs, gs, half_row, flat, carry[name], k == last)
        for i, h, a in zip(ks, hs, acts):
            saved[i][name] = (xs, gs, half_row, h, a)

    def add_slot():
        k = len(slots)
        slots.append([held[k]] + [hop(held[k], s) for s in range(1, n_tensor)])

    def weight_pieces(k, fence=()):
        parts = list(saved[k].values())
        if fence:
            xs, gs, rows, h, a = parts[0]
            parts[0] = (xs, gs, rows, after(h, *fence), a)
        return expert_weight(parts, n_tensor, width)

    def hop_back(grads):
        return [hop(grads[s], n_tensor - s) for s in range(1, n_tensor)]

    def total_of(grads, got):
        return functools.reduce(jnp.add, [v.astype(F32) for v in [grads[0], *got]])

    def weight_total(k):
        grads = weight_pieces(k)
        return total_of(grads, hop_back(grads))

    def send_on(k, moving):
        total = totals[k]
        if moving is not None:
            total = total + moving.astype(F32)
        return ring(total.astype(BF16)) if k else total

    for _ in range(1, group):
        add_slot()
    slots, mlp_top, mlp_low = after((slots, mlp_top, mlp_low))
    x_top, y_low = plane(mlp_top, 1), plane(mlp_low, 2)
    run("near", 0)
    x_top, y_low, carry["near"] = after((x_top, y_low, carry["near"]))
    x_low, y_top = plane(mlp_low, 1), plane(mlp_top, 2)
    where["one"] = ([(x_top, 0), (y_low, 0)], [(grad_x, 0), (grad_y, 1)])
    run("one", 0)
    x_low, y_top, carry["one"], held[2] = after((x_low, y_top, carry["one"], held[2]))
    for _ in range(3, depth):
        held.append(ring(held[-1]))
    mlp_diag = [plane(x_top, 2), plane(y_low, 1)]
    where["two"] = ([(x_low, 0), (y_top, 0)], [(grad_x, 1), (grad_y, 0)])
    run("two", 0)
    mlp_diag, carry["two"] = after((mlp_diag, carry["two"]))
    add_slot()
    where["diag"] = ([(v, 0) for v in mlp_diag], [(v, 0) for v in grad_diag])
    run("diag", 0)
    slots, carry["diag"] = after((slots, carry["diag"]))
    for k in range(group, last, group):
        while len(slots) < k + group:
            add_slot()
        for name in ("near", "one", "two", "diag"):
            run(name, k)
    totals = {}
    order = list(range(1, depth)) + [0]
    early = order[: depth - group - 1]
    for k in early:
        totals[k] = weight_total(k)
    while len(slots) < depth:
        add_slot()
    slots[-1], totals = after((slots[-1], totals))
    moving = None
    for k in early:
        moving = send_on(k, moving)
    rest = order[len(early) :]

    run("diag", last)
    back_parts = [plane(v, m) for v, m in zip(carry["diag"][1], (1, 2))]
    run("one", last, [carry["diag"]])
    back_parts, carry["one"] = after((back_parts, carry["one"]))
    halves = [plane(v, m) for v, m in zip(carry["one"][1], (1, 2))]
    run("two", last, [carry["one"]])
    low_x, top_y = ((v.astype(F32) + p.astype(F32)).astype(BF16) for v, p in zip(carry["two"][1], back_parts[::-1]))
    halves, low_x, top_y = after((halves, low_x, top_y))
    others = [plane(low_x, 1), plane(top_y, 2)]
    run("near", last, [low_x, top_y])
    others, carry["near"], moving = after((others, carry["near"], moving))

    dy, d_gates, gain_two_all = turn_back(carry["near"][1], halves, others, mixed, grad_wide, gain_mlp)
    out_diag, dy = after((carry["diag"][0], dy))
    out_parts = [plane(v, m) for v, m in zip(out_diag, (1, 2))]
    dy_full = gather_rows(dy)
    late = {rest[0]: weight_pieces(rest[0], [dy])}
    dy_full, late, out_parts = after((dy_full, late, out_parts))
    d_gates = d_gates[:, :n_expert] + d_gates[:, LANES // 2 : LANES // 2 + n_expert]

    arrived = moving
    late_got = hop_back(late[rest[0]])
    out_halves = [plane(v, m) for v, m in zip(carry["one"][0], (1, 2))]
    do_t = jnp.einsum("td,cd->ct", dy_full, w_out, preferred_element_type=F32).astype(BF16)
    out_w_grad = [jnp.einsum("td,ct->dc", dy_full, o, preferred_element_type=F32).astype(BF16) for o in o_t]

    def backward(i, do_t):
        return attn_backward(q_t[i], k_t[i], v_t, do_t, lse[i], cos_t, sin_t, start, i * count, count)

    def weight_grads(ds):
        return [jnp.einsum("td,ct->dc", attn_in, d, preferred_element_type=F32).astype(BF16) for d in ds]

    def part(a, who, rows):
        return lax.dynamic_slice_in_dim(a, who * rows, rows, 0)

    p_at, z_at = lax.rem(e_at, PLANE), e_at // PLANE

    def plane_shares(a):
        quarter = a.shape[0] // PLANE
        return [plane(part(a, p_at ^ m, quarter), m) for m in range(1, PLANE)]

    def plane_sum(a, shares):
        total = part(a, p_at, a.shape[0] // PLANE).astype(F32)
        for v in shares:
            total = total + v.astype(F32)
        return total.astype(BF16)

    def swap(a, bit):
        pairs = [(i, i ^ (bit * PLANE)) for i in range(n_expert)]
        return lax.ppermute(a, "expert", pairs)

    bits = [1 << i for i in range(depth.bit_length() - 1)]

    def upper(bit):
        return (z_at // bit) % 2

    def z_cut(a, bit, tail=None):
        rows = a.shape[0] // 2
        stay, go = part(a, upper(bit), rows), part(a, 1 - upper(bit), rows)
        return stay, go if tail is None else jnp.concatenate([go, tail], axis=0)

    def add(a, b):
        return (a.astype(F32) + b.astype(F32)).astype(BF16)

    def z_join(a, got, bit):
        return jnp.where(upper(bit) == 0, jnp.concatenate([a, got], 0), jnp.concatenate([got, a], 0))

    first = jnp.concatenate(out_w_grad, axis=1)
    ds = []
    do_t, out_w_grad = after((do_t, out_w_grad))
    if parts == 2:
        ds.append(backward(0, do_t))
        ds[0], out_halves, do_t, late_got = after((ds[0], out_halves, do_t, late_got))
        first = jnp.concatenate(weight_grads(ds[0]) + out_w_grad, axis=1)

    def next_moving(k, got, arrived):
        total = total_of(late[k], got)
        if arrived is not None:
            total = total + arrived.astype(F32)
        return total.astype(BF16)

    moving = next_moving(rest[0], late_got, arrived)
    first, out_halves, moving, do_t = after((first, out_halves, moving, do_t))
    ring_on = [ring(moving[c]) for c in range(2)]
    first_sent = plane_shares(first)
    ds.append(backward(parts - 1, do_t))
    third = rest[1]
    late[third] = weight_pieces(third, [ds[-1]])
    first_sent, ring_on, ds, late = after((first_sent, ring_on, ds, late))

    second = jnp.concatenate(weight_grads(ds[-1]), axis=1)
    first = plane_sum(first, first_sent)
    stay, go = z_cut(first, bits[0])
    second, stay, go, ds = after((second, stay, go, ds))
    second_sent = plane_shares(second)
    got = swap(go, bits[0])
    ring_on.append(ring(moving[2]))
    late_got = hop_back(late[third])
    own_terms, *far_terms, dots = input_terms(
        t_at.reshape(1), tokens, gain_attn, ds, (w_query, key_matrix, value_matrix), n_tensor
    )
    dots = dots[:, 0]
    second_sent, got, ring_on, far_terms, dots, late_got = after((second_sent, got, ring_on, far_terms, dots, late_got))
    moving = next_moving(third, late_got, jnp.stack(ring_on))

    first = add(stay, got)
    out_two = [add(v, p) for v, p in zip(carry["two"][0], out_parts[::-1])]
    gain_two = cols_of(gain_two_all[0], t_at)
    far_gains = [cols_of(gain_two_all[0], peer(s)) for s in range(1, n_tensor)]
    cuts = [z_cut(first, bits[1])] if len(bits) > 1 else []
    cuts, far_terms, dots = after((cuts, far_terms, dots))
    far_terms = [hop(v, s) for s, v in enumerate(far_terms, 1)]
    far_dots = [hop(jnp.concatenate([dots, v]), s) for s, v in enumerate(far_gains, 1)]
    gots = [swap(go, bits[1]) for _, go in cuts]
    gots, far_terms, far_dots, out_two = after((gots, far_terms, far_dots, out_two))
    out_others = [plane(v, m) for v, m in zip(out_two, (1, 2))]
    second = plane_sum(second, second_sent)
    for (stay, _), got in zip(cuts, gots):
        first = add(stay, got)
    for bit in bits[2:]:
        stay, go = z_cut(first, bit)
        first = add(stay, swap(go, bit))
    gain_two = functools.reduce(jnp.add, [gain_two] + [v[n_tok:] for v in far_dots])
    far_dots = [v[:n_tok] for v in far_dots]

    d_attn_in = functools.reduce(jnp.add, [own_terms] + [v.astype(F32) for v in far_terms])
    all_dots = functools.reduce(jnp.add, [dots] + far_dots)
    normed_cols = cols_of(tokens, t_at).astype(F32) * inv_one
    scaled_one = d_attn_in * cols_of(gain_attn, t_at)
    d_norm_one = inv_one * (scaled_one - normed_cols * (all_dots / width)[:, None])
    grad_tokens = cols_of(dy_full, t_at).astype(F32) + d_norm_one
    gain_one = jnp.sum(d_attn_in * normed_cols, axis=0)
    wide = second.shape[1]
    gains = jnp.concatenate([gain_one, gain_two]).astype(BF16).reshape(-1, wide)
    gain_rows = gains.shape[0]
    gains = jnp.pad(gains, ((0, 16 - gain_rows), (0, 0)))
    grad_logits = gather_rows(gates * (d_gates - jnp.sum(gates * d_gates, axis=1, keepdims=True)))
    for i, bit in enumerate(bits):
        rows = second.shape[0] // 2
        stay, go = z_cut(second, bit, gains)
        back = bits[-1 - i]
        first, go = after((first, go))
        got, first_got = swap(go, bit), swap(first, back)
        got, first_got, out_others = after((got, first_got, out_others))
        second, gains = add(stay, got[:rows]), add(gains, got[rows:])
        first = z_join(first, first_got, back)
    first, second, moving = after((first, second, moving))
    first_all = [first] + [plane(first, m) for m in range(1, PLANE)]
    late[0] = weight_pieces(0, [first])
    for bit in bits[::-1]:
        second = z_join(second, swap(second, bit), bit)
    moving, second = after((moving, second))
    ring_on = [ring(moving[c]) for c in range(3)]
    rows = second.shape[0]
    second = jnp.concatenate([second, gains], axis=0)
    out_top, out_low = carry["near"][0]
    top_rows = out_top.astype(F32) + out_halves[0].astype(F32) + out_others[1].astype(F32)
    low_rows = out_low.astype(F32) + out_others[0].astype(F32) + out_halves[1].astype(F32)
    block_out = to_cols((mixed + jnp.concatenate([top_rows, low_rows], axis=0)).astype(BF16))
    second, block_out, first_all, ring_on[0], late[0] = after((second, block_out, first_all, ring_on[0], late[0]))
    late_got = hop_back(late[0])
    second_all = [second] + [plane(second, m) for m in range(1, PLANE)]
    final = [a + b.astype(F32) for a, b in zip(total_of(late[0], late_got), ring_on)]
    final[2] = final[2].T
    second_all, final = after((second_all, final))
    gains = functools.reduce(jnp.add, [v[rows : rows + gain_rows].astype(F32) for v in second_all]).reshape(-1)
    cuts = [w.shape[1] // parts for w in (w_query, key_matrix, value_matrix)]
    grad_query, grad_key, grad_value, grad_out = lay_out(p_at.reshape(1), first_all, second_all, parts, cuts)
    return (
        block_out,
        grad_tokens,
        grad_logits,
        gains[:col_width],
        grad_query,
        grad_key,
        grad_value,
        grad_out,
        gains[col_width:],
        final[0][None],
        final[1][None],
        final[2][None],
    )


def solution(mesh):
    return jax.shard_map(
        body,
        mesh=mesh,
        in_specs=(
            P("expert", None),
            P("expert"),
            P("expert", None),
            P("expert", None),
            P(),
            P(None, "tensor"),
            P(None, "tensor"),
            P(None, "tensor"),
            P("tensor", None),
            P(),
            P("expert", None, "tensor"),
            P("expert", None, "tensor"),
            P("expert", "tensor", None),
            P("expert", "tensor"),
        ),
        out_specs=(
            P("expert", "tensor"),
            P("expert", "tensor"),
            P("expert", None),
            P("tensor"),
            P(None, "tensor"),
            P(None, "tensor"),
            P(None, "tensor"),
            P("tensor", None),
            P("tensor"),
            P("expert", None, "tensor"),
            P("expert", None, "tensor"),
            P("expert", "tensor", None),
        ),
        check_vma=False,
    )
```

```python
import functools

import jax
import jax.numpy as jnp
from jax import lax
from jax.experimental import pallas as pl
from jax.experimental.pallas import tpu as pltpu
from jax.sharding import PartitionSpec as P

HEAD_SIZE = 64
EPS = 1e-06
THETA = 10000.0
NEG = -1e30
PLANE = 4
LANES = 128
F32 = jnp.float32
BF16 = jnp.bfloat16
NT = (((1,), (1,)), ((), ()))
TN = (((0,), (0,)), ((), ()))


def dot(a, b):
    return jnp.dot(a, b, preferred_element_type=F32)


def dot_nt(a, b):
    return lax.dot_general(a, b, NT, preferred_element_type=F32)


def dot_tn(a, b):
    return lax.dot_general(a, b, TN, preferred_element_type=F32)


def attn_mask(start, row_start, block, keys):
    first = start[:, row_start : row_start + block]
    first = jnp.concatenate([first, first], axis=1)
    key_at = lax.broadcasted_iota(jnp.int32, (keys, 2 * block), 0)
    lane = lax.broadcasted_iota(jnp.int32, (1, 2 * block), 1)
    row_at = row_start + jnp.where(lane >= block, lane - block, lane)
    return (key_at >= first) & (key_at <= row_at)


def rope(x, c, s):
    half = x.shape[0] // 2
    a, b = x[:half], x[half:]
    return jnp.concatenate([a * c - b * s, b * c + a * s], axis=0)


def attn_fwd_kernel(block, q_ref, k_ref, v_ref, cos_ref, sin_ref, start_ref, qo_ref, ko_ref, o_ref, lse_ref):
    hd = HEAD_SIZE
    n = k_ref.shape[1]
    c, s = cos_ref[...], sin_ref[...]
    k_rot = rope(k_ref[...], c, s)
    ko_ref[...] = k_rot.astype(BF16)
    keys = k_rot.T.astype(BF16)
    q0 = rope(q_ref[0:hd], c, s).astype(BF16)
    q1 = rope(q_ref[hd : 2 * hd], c, s).astype(BF16)
    qo_ref[0:hd] = q0
    qo_ref[hd : 2 * hd] = q1
    start = start_ref[...]
    for r0 in range(0, n, block):
        cn = r0 + block
        qb = jnp.concatenate([q0[:, r0:cn], q1[:, r0:cn]], axis=1) * jnp.asarray(hd**-0.5, BF16)
        scores = dot(keys[:cn], qb)
        scores = jnp.where(attn_mask(start, r0, block, cn), scores, NEG)
        peak = jnp.max(scores, axis=0, keepdims=True)
        p = jnp.exp(scores - peak)
        total = jnp.sum(p, axis=0, keepdims=True)
        o = dot(v_ref[:, :cn], p.astype(BF16)) / total
        o_ref[0:hd, r0:cn] = o[:, :block].astype(BF16)
        o_ref[hd : 2 * hd, r0:cn] = o[:, block:].astype(BF16)
        lse = peak + jnp.log(total)
        lse_ref[0, 0:1, r0:cn] = lse[:, :block]
        lse_ref[0, 1:2, r0:cn] = lse[:, block:]


def attn_bwd_kernel(
    block, q_ref, k_ref, v_ref, do_ref, lse_ref, cos_ref, sin_ref, start_ref, dq_ref, dk_ref, dv_ref, dk_acc, dv_acc
):
    hd = HEAD_SIZE
    n = k_ref.shape[1]
    c, s = cos_ref[...], sin_ref[...]
    keys = k_ref[...].astype(F32).T.astype(BF16)
    vals = v_ref[...].astype(F32).T.astype(BF16)
    start = start_ref[...]
    dk_acc[...] = jnp.zeros_like(dk_acc)
    dv_acc[...] = jnp.zeros_like(dv_acc)
    scale = hd**-0.5
    for r0 in range(0, n, block):
        cn = r0 + block
        qb = jnp.concatenate([q_ref[0:hd, r0:cn], q_ref[hd : 2 * hd, r0:cn]], axis=1)
        gb = jnp.concatenate([do_ref[0:hd, r0:cn], do_ref[hd : 2 * hd, r0:cn]], axis=1)
        lse = jnp.concatenate([lse_ref[0, 0:1, r0:cn], lse_ref[0, 1:2, r0:cn]], axis=1)
        scores = dot(keys[:cn], qb * jnp.asarray(scale, BF16))
        p = jnp.exp(jnp.where(attn_mask(start, r0, block, cn), scores, NEG) - lse)
        dv_acc[:, :cn] += dot_nt(gb, p.astype(BF16))
        dp = dot(vals[:cn], gb)
        delta = jnp.sum(p * dp, axis=0, keepdims=True)
        ds = (p * (dp - delta) * scale).astype(BF16)
        dq = dot(k_ref[:, :cn], ds)
        dk_acc[:, :cn] += dot_nt(qb, ds)
        cb, sb = c[:, r0:cn], -s[:, r0:cn]
        dq_ref[0:hd, r0:cn] = rope(dq[:, :block], cb, sb).astype(BF16)
        dq_ref[hd : 2 * hd, r0:cn] = rope(dq[:, block:], cb, sb).astype(BF16)
    dk_ref[...] = rope(dk_acc[...], c, -s).astype(BF16)
    dv_ref[...] = dv_acc[...].astype(BF16)


def attn_cost(heads, n, products):
    return pl.CostEstimate(
        flops=products * heads * n * n * HEAD_SIZE * 2, bytes_accessed=8 * heads * n * HEAD_SIZE, transcendentals=heads * n * n
    )


def attn_forward(q_t, k_t, v_t, cos_t, sin_t, start, first, count):
    n = q_t.shape[1]
    hd = HEAD_SIZE
    block = min(256, n)
    pair = pl.BlockSpec((2 * hd, n), lambda h: (h + first, 0))
    one = pl.BlockSpec((hd, n), lambda h: (h + first, 0))
    table = pl.BlockSpec((hd // 2, n), lambda h: (0, 0))
    return pl.pallas_call(
        functools.partial(attn_fwd_kernel, block),
        grid=(count,),
        in_specs=[pair, one, one, table, table, pl.BlockSpec((1, n), lambda h: (0, 0))],
        out_specs=[pl.BlockSpec((r * hd, n), lambda h: (h, 0)) for r in (2, 1, 2)]
        + [pl.BlockSpec((1, 2, n), lambda h: (h, 0, 0))],
        out_shape=[jax.ShapeDtypeStruct((r * count * hd, n), BF16) for r in (2, 1, 2)]
        + [jax.ShapeDtypeStruct((count, 2, n), F32)],
        compiler_params=pltpu.CompilerParams(vmem_limit_bytes=48 * 2**20),
        cost_estimate=attn_cost(2 * count, n, 4),
        name="attn_forward",
    )(q_t, k_t, v_t, cos_t, sin_t, start)


def attn_backward(q_t, k_t, v_t, do_t, lse, cos_t, sin_t, start, first, count):
    n = q_t.shape[1]
    hd = HEAD_SIZE
    block = min(256, n)
    table = pl.BlockSpec((hd // 2, n), lambda h: (0, 0))
    return pl.pallas_call(
        functools.partial(attn_bwd_kernel, block),
        grid=(count,),
        in_specs=[
            pl.BlockSpec((2 * hd, n), lambda h: (h, 0)),
            pl.BlockSpec((hd, n), lambda h: (h, 0)),
            pl.BlockSpec((hd, n), lambda h: (h + first, 0)),
            pl.BlockSpec((2 * hd, n), lambda h: (h + first, 0)),
            pl.BlockSpec((1, 2, n), lambda h: (h, 0, 0)),
            table,
            table,
            pl.BlockSpec((1, n), lambda h: (0, 0)),
        ],
        out_specs=[pl.BlockSpec((r * hd, n), lambda h: (h, 0)) for r in (2, 1, 1)],
        out_shape=[jax.ShapeDtypeStruct((r * count * hd, n), BF16) for r in (2, 1, 1)],
        scratch_shapes=[pltpu.VMEM((hd, n), F32), pltpu.VMEM((hd, n), F32)],
        compiler_params=pltpu.CompilerParams(vmem_limit_bytes=48 * 2**20),
        cost_estimate=attn_cost(2 * count, n, 4),
        name="attn_backward",
    )(q_t, k_t, v_t, do_t, lse, cos_t, sin_t, start)


def data_kernel(first, last, blocks, tiles, slots, pieces, expert_ref, *refs):
    refs = list(refs)
    at, tile_at = pl.program_id(0), pl.program_id(1)
    x, g_all = refs[0][...], refs[blocks][...]
    for i in range(1, blocks):
        x = jnp.where(at == i, refs[i][...], x)
        g_all = jnp.where(at == i, refs[blocks + i][...], g_all)
    weights = refs[2 * blocks : 2 * blocks + slots * pieces]
    refs = refs[2 * blocks + slots * pieces :]
    if not first:
        out_in, dx_in, dgate_in = refs[:3]
        refs = refs[3:]
    if last:
        out_refs, dx_refs = refs[:blocks], refs[blocks : 2 * blocks]
        refs = refs[2 * blocks :]
    else:
        out_ref, dx_ref, dgate_ref = refs[:3]
        refs = refs[3:]
    hs, acts = refs[:slots], refs[slots : 2 * slots]
    acc_o, acc_x, held, sems = refs[2 * slots :]
    opening = (at == 0) & (tile_at == 0)

    def copies(n):
        return [pltpu.make_async_copy(weights[n].at[c], held.at[n, c], sems.at[n, c]) for c in range(3)]

    @pl.when(opening)
    def _():
        for n in range(slots * pieces):
            for copy in copies(n):
                copy.start()

    width = x.shape[1]
    g = g_all[:, :width]
    gates = g_all[:, width:].astype(F32)
    lane = lax.broadcasted_iota(jnp.int32, gates.shape, 1)
    dgate = None if first else dgate_in[...]
    for j in range(slots):
        here = lane == expert_ref[j]
        both = here | (lane == expert_ref[j] + LANES // 2)
        gate = jnp.sum(jnp.where(both, gates, 0.0), axis=1, keepdims=True)
        row_sum = None
        for i in range(pieces):
            n = j * pieces + i

            @pl.when(opening)
            def _():
                for copy in copies(n):
                    copy.wait()

            hid = held.shape[3]
            gate_pre = dot(x, held[n, 0])
            up_pre = dot(x, held[n, 1])
            d_hidden = dot(g, held[n, 2])
            sig = jax.nn.sigmoid(gate_pre)
            silu = gate_pre * sig
            act = silu * up_pre
            part = jnp.sum(act * d_hidden, axis=1, keepdims=True)
            row_sum = part if row_sum is None else row_sum + part
            act_w = (act * gate).astype(BF16)
            d_hidden = d_hidden * gate
            d_up = (d_hidden * silu).astype(BF16)
            d_gate = (d_hidden * up_pre * (sig + silu * (1.0 - sig))).astype(BF16)
            hs[j][:, 2 * i * hid : (2 * i + 1) * hid] = d_gate
            hs[j][:, (2 * i + 1) * hid : (2 * i + 2) * hid] = d_up
            acts[j][:, i * hid : (i + 1) * hid] = act_w
            out_term = dot_nt(act_w, held[n, 2])
            dx_term = dot_nt(d_gate, held[n, 0]) + dot_nt(d_up, held[n, 1])
            if n == 0 and first:
                acc_o[...] = out_term
                acc_x[...] = dx_term
            elif n == 0:
                acc_o[...] = out_in[...].astype(F32) + out_term
                acc_x[...] = dx_in[...].astype(F32) + dx_term
            else:
                acc_o[...] += out_term
                acc_x[...] += dx_term
        term = jnp.where(here, row_sum, 0.0)
        dgate = term if dgate is None else dgate + term
    if last:
        high = dgate.astype(BF16).astype(F32)
        low = pltpu.roll(dgate - high, LANES // 2, 1)
        tail = jnp.where(lane < LANES // 2, high, low).astype(BF16)
        for i in range(blocks):

            @pl.when(at == i)
            def _():
                out_refs[i][...] = acc_o[...].astype(BF16)
                dx_refs[i][:, :width] = acc_x[...].astype(BF16)
                dx_refs[i][:, width:] = tail
    else:
        out_ref[...] = acc_o[...].astype(BF16)
        dx_ref[...] = acc_x[...].astype(BF16)
        dgate_ref[...] = dgate


def expert_data(experts, xs, gs, rows, ws, carry, last):
    blocks = len(xs)
    width = xs[0][0].shape[1]
    tile = min(256, rows)
    tiles = rows // tile
    full = gs[0][0].shape[1]
    slots = experts.shape[0]
    pieces = len(ws) // slots
    hidden = ws[0].shape[2]
    first = carry is None
    total = blocks * rows

    def out_spec(columns):
        return pl.BlockSpec((tile, columns), lambda b, i: (b * tiles + i, 0))

    def in_spec(columns, offset):
        return pl.BlockSpec((tile, columns), lambda b, i: (offset * tiles + i, 0))

    def own_spec(columns, j):
        return pl.BlockSpec((tile, columns), lambda b, i: (jnp.clip((b - j) * tiles + i, 0, tiles - 1), 0))

    ins = [experts, *[x for x, _ in xs], *[g for g, _ in gs], *ws]
    specs = [pl.BlockSpec(memory_space=pltpu.SMEM)]
    specs += [in_spec(width, o) for _, o in xs] + [in_spec(full, o) for _, o in gs]
    specs += [pl.BlockSpec(memory_space=pl.ANY)] * len(ws)
    if not first:
        ins += list(carry)
        specs += [out_spec(width), out_spec(width), out_spec(LANES)]
    if last:
        out_specs = [own_spec(c, j) for c in (width, full) for j in range(blocks)]
        out_shape = [jax.ShapeDtypeStruct((rows, c), BF16) for c in (width, full) for _ in range(blocks)]
    else:
        out_specs = [out_spec(c) for c in (width, width, LANES)]
        out_shape = [jax.ShapeDtypeStruct((total, c), t) for c, t in ((width, BF16), (width, BF16), (LANES, F32))]
    n = len(out_specs)
    kept = [2 * pieces * hidden] * slots + [pieces * hidden] * slots
    single = pieces * hidden
    outs = pl.pallas_call(
        functools.partial(data_kernel, first, last, blocks, tiles, slots, pieces),
        grid=(blocks, tiles),
        in_specs=specs,
        out_specs=out_specs + [out_spec(c) for c in kept],
        out_shape=out_shape + [jax.ShapeDtypeStruct((total, c), BF16) for c in kept],
        scratch_shapes=[
            pltpu.VMEM((tile, width), F32),
            pltpu.VMEM((tile, width), F32),
            pltpu.VMEM((len(ws), 3, width, hidden), BF16),
            pltpu.SemaphoreType.DMA((len(ws), 3)),
        ],
        compiler_params=pltpu.CompilerParams(vmem_limit_bytes=60 * 2**20),
        cost_estimate=pl.CostEstimate(
            flops=3 * slots * total * width * single,
            bytes_accessed=total * width * 12 + slots * pieces * width * hidden * 6,
            transcendentals=slots * total * single,
        ),
        name="expert_data",
    )(*ins)
    result = (outs[:blocks], outs[blocks:n]) if last else outs[:n]
    return result, outs[n : n + slots], outs[n + slots :]


def weight_kernel(shape, pieces, *refs):
    xt = gt = None
    refs = list(refs)
    for blocks in shape:
        xs, gs, h, a = refs[:blocks], refs[blocks : 2 * blocks], refs[2 * blocks], refs[2 * blocks + 1]
        refs = refs[2 * blocks + 2 :]
        rows = xs[0].shape[0]
        for i in range(blocks):
            span = slice(i * rows, (i + 1) * rows)
            xp, gp = dot_tn(xs[i][...], h[span]), dot_tn(gs[i][...], a[span])
            xt, gt = (xp, gp) if xt is None else (xt + xp, gt + gp)
    outs = refs
    hid = outs[0].shape[2]
    for i in range(pieces):
        outs[i][0] = xt[:, 2 * i * hid : (2 * i + 1) * hid].astype(BF16)
        outs[i][1] = xt[:, (2 * i + 1) * hid : (2 * i + 2) * hid].astype(BF16)
        outs[i][2] = gt[:, i * hid : (i + 1) * hid].astype(BF16)


def expert_weight(parts, pieces, width):
    hidden = parts[0][4].shape[1] // pieces
    block = 256
    ins, specs, shape, total = [], [], [], 0
    for xs, gs, rows, h, a in parts:
        for v, o in [*xs, *gs]:
            ins.append(v)
            specs.append(pl.BlockSpec((rows, block), lambda i, o=o: (o, i)))
        for v in (h, a):
            ins.append(v)
            specs.append(pl.BlockSpec(v.shape, lambda i: (0, 0), pipeline_mode=pl.Buffered(1)))
        shape.append(len(xs))
        total += h.shape[0]
    return pl.pallas_call(
        functools.partial(weight_kernel, tuple(shape), pieces),
        grid=(width // block,),
        in_specs=specs,
        out_specs=[pl.BlockSpec((3, block, hidden), lambda i: (0, i, 0))] * pieces,
        out_shape=[jax.ShapeDtypeStruct((3, width, hidden), BF16)] * pieces,
        compiler_params=pltpu.CompilerParams(vmem_limit_bytes=60 * 2**20),
        cost_estimate=pl.CostEstimate(
            flops=total * width * hidden * pieces,
            bytes_accessed=total * (width * 4 + hidden * pieces * 6) + width * hidden * pieces * 6,
            transcendentals=0,
        ),
        name="expert_weight",
    )(*ins)


def rms_parts(v):
    inv = lax.rsqrt(jnp.mean(v * v, axis=1, keepdims=True) + EPS)
    return inv, v * inv


def join_kernel(pieces, at_ref, x_ref, gain_ref, *refs):
    os, ws = refs[:pieces], refs[pieces : 2 * pieces]
    mixed_ref, top_ref, low_ref = refs[2 * pieces :]
    mixed = x_ref[...].astype(F32)
    for o, w in zip(os, ws):
        mixed = mixed + dot_tn(o[...], w[...])
    mixed_ref[...] = mixed
    rows = (rms_parts(mixed)[1] * gain_ref[...]).astype(BF16)
    for i, ref in enumerate((top_ref, low_ref)):

        @pl.when(pl.program_id(0) == i)
        def _():
            ref[...] = rows


def join_heads(at, tokens, gain, own, far, ws, rows):
    width = tokens.shape[1]
    half = rows // 2
    heads = own[0].shape[0]
    n = len(ws)
    o_specs = [pl.BlockSpec((heads, half), lambda i, at: (0, at[0] * 2 + i))] * len(own)
    o_specs += [pl.BlockSpec((heads, half), lambda i, at: (0, i))] * len(far)
    os = [*own, *far]
    if half % LANES:
        os = [lax.dynamic_slice_in_dim(o, at[0] * rows, rows, 1) for o in own] + far
        os = [jnp.stack([o[:, :half], o[:, half:]]) for o in os]
        o_specs = [pl.BlockSpec((None, heads, half), lambda i, at: (i, 0, 0))] * n
    once = pl.BlockSpec((half, width), lambda i, at: (0, 0))
    return pl.pallas_call(
        functools.partial(join_kernel, n),
        grid_spec=pltpu.PrefetchScalarGridSpec(
            num_scalar_prefetch=1,
            grid=(2,),
            in_specs=[
                pl.BlockSpec((half, width), lambda i, at: (at[0] * 2 + i, 0)),
                pl.BlockSpec((1, width), lambda i, at: (0, 0)),
            ]
            + o_specs
            + [pl.BlockSpec((heads, width), lambda i, at, b=b: (b, 0)) for _, b in ws],
            out_specs=[pl.BlockSpec((half, width), lambda i, at: (i, 0)), once, once],
        ),
        out_shape=[
            jax.ShapeDtypeStruct((rows, width), F32),
            jax.ShapeDtypeStruct((half, width), BF16),
            jax.ShapeDtypeStruct((half, width), BF16),
        ],
        compiler_params=pltpu.CompilerParams(vmem_limit_bytes=48 * 2**20),
        cost_estimate=pl.CostEstimate(
            flops=2 * rows * heads * n * width, bytes_accessed=rows * width * 8, transcendentals=0
        ),
        name="join_heads",
    )(at, tokens, gain[None, :], *os, *[w for w, _ in ws])


def input_kernel(groups, n_tensor, at_ref, x_ref, gain_ref, *refs):
    ds, ws = refs[: 3 * groups], refs[3 * groups : 3 * groups + 3]
    own_ref, *fars, dots_ref, acc = refs[3 * groups + 3 :]
    total = None
    for j in range(3):
        d = jnp.concatenate([ds[3 * i + j][...] for i in range(groups)], axis=0)
        term = lax.dot_general(d, ws[j][...], (((0,), (1,)), ((), ())), preferred_element_type=F32)
        total = term if total is None else total + term
    acc[...] = total
    normed = rms_parts(x_ref[...].astype(F32))[1]
    dots_ref[...] = jnp.sum(total * gain_ref[...] * normed, axis=1, keepdims=True)
    cols = own_ref.shape[1]
    for s, ref in enumerate([own_ref, *fars]):
        who = lax.rem(at_ref[0] + s, n_tensor)
        ref[...] = acc[:, pl.ds(pl.multiple_of(who * cols, cols), cols)].astype(ref.dtype)


def input_terms(at, tokens, gain, ds, ws, n_tensor):
    n, width = tokens.shape
    cols = width // n_tensor
    tile = min(256, n)
    flat = [d for group in ds for d in group]
    return pl.pallas_call(
        functools.partial(input_kernel, len(ds), n_tensor),
        grid_spec=pltpu.PrefetchScalarGridSpec(
            num_scalar_prefetch=1,
            grid=(n // tile,),
            in_specs=[pl.BlockSpec((tile, width), lambda i, at: (i, 0)), pl.BlockSpec((1, width), lambda i, at: (0, 0))]
            + [pl.BlockSpec((d.shape[0], tile), lambda i, at: (0, i)) for d in flat]
            + [pl.BlockSpec(w.shape, lambda i, at: (0, 0)) for w in ws],
            out_specs=[pl.BlockSpec((tile, cols), lambda i, at: (i, 0))] * n_tensor
            + [pl.BlockSpec((tile, 1), lambda i, at: (i, 0))],
            scratch_shapes=[pltpu.VMEM((tile, width), F32)],
        ),
        out_shape=[jax.ShapeDtypeStruct((n, cols), F32)]
        + [jax.ShapeDtypeStruct((n, cols), BF16)] * (n_tensor - 1)
        + [jax.ShapeDtypeStruct((n, 1), F32)],
        compiler_params=pltpu.CompilerParams(vmem_limit_bytes=48 * 2**20),
        cost_estimate=pl.CostEstimate(
            flops=2 * n * width * sum(w.shape[1] for w in ws), bytes_accessed=n * width * 8, transcendentals=0
        ),
        name="input_terms",
    )(at, tokens, gain[None, :], *flat, *ws)


def turn_kernel(top_ref, low_ref, xt_ref, yl_ref, xl_ref, yt_ref, mixed_ref, grad_ref, gain_ref, dy_ref, gates_ref, sum_ref):
    step = pl.program_id(0)
    width = mixed_ref.shape[1]
    upper = step == 0
    back = jnp.where(upper, top_ref[...], low_ref[...]).astype(F32)
    back = back + jnp.where(upper, xt_ref[...], xl_ref[...]).astype(F32)
    back = back + jnp.where(upper, yt_ref[...], yl_ref[...]).astype(F32)
    gates_ref[...] = back[:, width:]
    d_in = back[:, :width]
    inv, normed = rms_parts(mixed_ref[...])
    scaled = d_in * gain_ref[...]
    dots = jnp.mean(scaled * normed, axis=1, keepdims=True)
    dy_ref[...] = (grad_ref[...].astype(F32) + inv * (scaled - normed * dots)).astype(BF16)
    part = jnp.sum(d_in * normed, axis=0, keepdims=True)

    @pl.when(upper)
    def _():
        sum_ref[...] = part

    @pl.when(jnp.logical_not(upper))
    def _():
        sum_ref[...] += part


def turn_back(near, halves, others, mixed, grad_wide, gain):
    rows, width = mixed.shape
    half, full = rows // 2, near[0].shape[1]

    def spec(c):
        return pl.BlockSpec((half, c), lambda i: (i, 0))

    const = pl.BlockSpec((half, full), lambda i: (0, 0))
    line = pl.BlockSpec((1, width), lambda i: (0, 0))
    return pl.pallas_call(
        turn_kernel,
        grid=(2,),
        in_specs=[const] * 6 + [spec(width), spec(width), line],
        out_specs=[spec(width), spec(LANES), line],
        out_shape=[
            jax.ShapeDtypeStruct((rows, width), BF16),
            jax.ShapeDtypeStruct((rows, LANES), F32),
            jax.ShapeDtypeStruct((1, width), F32),
        ],
        compiler_params=pltpu.CompilerParams(vmem_limit_bytes=48 * 2**20),
        cost_estimate=pl.CostEstimate(flops=0, bytes_accessed=rows * width * 16, transcendentals=0),
        name="turn_back",
    )(*near, *halves, *others, mixed, grad_wide, gain[None, :])


def lay_out_kernel(halves, cuts, at_ref, *refs):
    q_out, k_out, v_out, o_out = refs[2 * PLANE :]
    rows = q_out.shape[0]
    for m in range(PLANE):

        @pl.when(pl.program_id(0) == m)
        def _():
            first, second = refs[m], refs[PLANE + m]
            parts = [second] if halves == 1 else [first, second]
            for out, cut, left in zip((q_out, k_out, v_out), cuts, (0, cuts[0], cuts[0] + cuts[1])):
                for i, part in enumerate(parts):
                    out[:, i * cut : (i + 1) * cut] = part[:rows, left : left + cut].astype(F32)
            wide = 0 if halves == 1 else sum(cuts)
            o_out[...] = first[:, wide:].astype(F32).T


def lay_out(at, first, second, halves, cuts):
    rows = first[0].shape[0]
    out_width = first[0].shape[1] - (0 if halves == 1 else sum(cuts))
    shapes = [(PLANE * rows, halves * c) for c in cuts] + [(out_width, PLANE * rows)]
    specs = [pl.BlockSpec((rows, halves * c), lambda m, at: (at[0] ^ m, 0)) for c in cuts]
    return pl.pallas_call(
        functools.partial(lay_out_kernel, halves, cuts),
        grid_spec=pltpu.PrefetchScalarGridSpec(
            num_scalar_prefetch=1,
            grid=(PLANE,),
            in_specs=[pl.BlockSpec(v.shape, lambda m, at: (0, 0)) for v in [*first, *second]],
            out_specs=specs + [pl.BlockSpec((out_width, rows), lambda m, at: (0, at[0] ^ m))],
        ),
        out_shape=[jax.ShapeDtypeStruct(v, F32) for v in shapes],
        compiler_params=pltpu.CompilerParams(vmem_limit_bytes=48 * 2**20),
        cost_estimate=pl.CostEstimate(flops=0, bytes_accessed=24 * rows * out_width, transcendentals=0),
        name="lay_out",
    )(at, *first, *second)


def after(x, *others):
    leaves, tree = jax.tree.flatten(x)
    extra = jax.tree.leaves(others)
    held = lax.optimization_barrier(tuple(leaves) + tuple(extra))
    return jax.tree.unflatten(tree, held[: len(leaves)])


def body(
    tokens,
    segment_ids,
    router_logits,
    expert_ids,
    gain_attn,
    w_query,
    key_matrix,
    value_matrix,
    w_out,
    gain_mlp,
    w_gate,
    w_up,
    w_down,
    out_grad,
):
    n_tok, width = tokens.shape
    col_width = out_grad.shape[1]
    n_tensor = width // col_width
    n_expert = router_logits.shape[1]
    depth = n_expert // PLANE
    my_row = n_tok // n_tensor
    t_at = lax.axis_index("tensor")
    e_at = lax.axis_index("expert")

    def hop(x, step):
        pairs = [(i, (i + step) % n_tensor) for i in range(n_tensor)]
        return jax.tree.map(lambda a: lax.ppermute(a, "tensor", pairs), x)

    def plane(x, mask):
        pairs = [(i, i ^ mask) for i in range(n_expert)]
        return jax.tree.map(lambda a: lax.ppermute(a, "expert", pairs), x)

    def ring(x, step=1):
        pairs = [(i, (i + step * PLANE) % n_expert) for i in range(n_expert)]
        return jax.tree.map(lambda a: lax.ppermute(a, "expert", pairs), x)

    def peer(step):
        return lax.rem(t_at + step + n_tensor, n_tensor)

    def rows_of(x, who):
        return lax.dynamic_slice_in_dim(x, who * my_row, my_row, 0)

    def cols_of(x, who):
        return lax.dynamic_slice_in_dim(x, who * col_width, col_width, x.ndim - 1)

    def place(parts, axis):
        if n_tensor == 2:
            return jnp.where(t_at == 0, jnp.concatenate(parts, axis), jnp.concatenate(parts[::-1], axis))
        size = parts[0].shape[axis]
        shape = list(parts[0].shape)
        shape[axis] *= n_tensor
        out = jnp.zeros(shape, parts[0].dtype)
        for s, v in enumerate(parts):
            out = lax.dynamic_update_slice_in_dim(out, v, peer(-s) * size, axis)
        return out

    def to_rows(x):
        return place([rows_of(x, t_at)] + [hop(rows_of(x, peer(s)), s) for s in range(1, n_tensor)], 1)

    def to_cols(x):
        return place([cols_of(x, t_at)] + [hop(cols_of(x, peer(s)), s) for s in range(1, n_tensor)], 0)

    def gather_rows(x):
        return place([x] + [hop(x, s) for s in range(1, n_tensor)], 0)

    ids_rows = rows_of(expert_ids, t_at)
    logit_rows = rows_of(router_logits, t_at)
    expert_range = jnp.arange(n_expert, dtype=jnp.int32)
    used = jnp.any(ids_rows[:, :, None] == expert_range[None, None, :], axis=1)
    masked = jnp.where(used, logit_rows, NEG)
    weights = jnp.where(used, jnp.exp(masked - jnp.max(masked, axis=1, keepdims=True)), 0.0)
    gates = weights / jnp.sum(weights, axis=1, keepdims=True)
    pad = ((0, 0), (0, LANES // 2 - n_expert))
    high = lax.optimization_barrier(gates.astype(BF16))
    low = (gates - high.astype(F32)).astype(BF16)
    gate_pair = jnp.concatenate([jnp.pad(high, pad), jnp.pad(low, pad)], axis=1)
    grad_low = out_grad.astype(BF16)
    grad_cols = [rows_of(grad_low, peer(s)) for s in range(n_tensor)]
    grad_cols, w_up, gate_pair = after((grad_cols, w_up, gate_pair))
    grad_cols = [grad_cols[0]] + [hop(grad_cols[s], s) for s in range(1, n_tensor)]
    held = [jnp.stack([w_gate[0], w_up[0], w_down[0].T])]
    grad_cols, held[0] = after((grad_cols, held[0]))
    grad_wide = jnp.concatenate([place(grad_cols, 1), gate_pair], axis=1)
    half_row = my_row // 2

    start = jnp.sum((segment_ids[:, None] < segment_ids[None, :]).astype(jnp.int32), axis=0)
    places = jnp.arange(n_tok, dtype=jnp.int32) - start
    half = HEAD_SIZE // 2
    freq = jnp.power(THETA, -2.0 * jnp.arange(half, dtype=F32) / HEAD_SIZE)
    angles = freq[:, None] * places.astype(F32)[None, :]
    cos_t, sin_t = jnp.cos(angles), jnp.sin(angles)
    start = start[None, :]
    held.append(ring(held[0]))
    tokens, grad_wide = after((tokens, grad_wide))
    grad_x, grad_y = plane(grad_wide, 1), plane(grad_wide, 2)
    out_pieces = [w_out] + [hop(w_out, s) for s in range(1, n_tensor)]
    slots = [[held[0]] + [hop(held[0], s) for s in range(1, n_tensor)]]
    x_full = tokens.astype(F32)
    inv_one = lax.rsqrt(jnp.mean(x_full * x_full, axis=1, keepdims=True) + EPS)
    normed_one = x_full * inv_one
    attn_in = (normed_one * gain_attn).astype(BF16)

    def project(w):
        return jnp.einsum("td,dc->ct", attn_in, w, preferred_element_type=F32)

    v_t = project(value_matrix).astype(BF16)
    q_pre, k_pre = project(w_query), project(key_matrix)
    kv = k_pre.shape[0] // HEAD_SIZE
    parts = 2 if kv % 2 == 0 else 1
    count = kv // parts
    q_t, k_t, o_t, lse = ([None] * parts for _ in range(4))
    far_os = []

    def head_group(i):
        q_t[i], k_t[i], o_t[i], lse[i] = attn_forward(q_pre, k_pre, v_t, cos_t, sin_t, start, i * count, count)

    def far_heads(i):
        sent = [lax.dynamic_slice_in_dim(o_t[i], peer(s) * my_row, my_row, 1) for s in range(1, n_tensor)]
        return [hop(v, s) for s, v in enumerate(sent, 1)]

    for i in range(parts):
        head_group(i)
    o_t, grad_x, grad_y = after((o_t, grad_x, grad_y))
    grad_diag = [plane(grad_x[:half_row], 2), plane(grad_y[half_row:], 1)]
    far_os = [far_heads(i) for i in range(parts)]
    far = [far_os[i][s] for s in range(n_tensor - 1) for i in range(parts)]
    out_ws = [(w, i) for w in out_pieces for i in range(parts)]
    mixed, mlp_top, mlp_low = join_heads(t_at.reshape(1), tokens, gain_mlp, o_t, far, out_ws, my_row)
    mlp_top, mlp_low, grad_diag, held[1] = after((mlp_top, mlp_low, grad_diag, held[1]))
    held.append(ring(held[1]))

    group = 2 if depth % 2 == 0 else 1
    last = depth - group
    carry = dict.fromkeys(("near", "one", "two", "diag"))
    saved = [{} for _ in range(depth)]
    where = {
        "near": ([(mlp_top, 0), (mlp_low, 0)], [(grad_wide, 0), (grad_wide, 1)]),
    }

    def run(name, k, fence=()):
        ks = range(k, k + group)
        experts = jnp.stack([lax.rem(e_at - i * PLANE + n_expert, n_expert) for i in ks])
        experts = after(experts, *fence) if fence else experts
        flat = [w for i in ks for w in slots[i]]
        xs, gs = where[name]
        carry[name], hs, acts = expert_data(experts, xs, gs, half_row, flat, carry[name], k == last)
        for i, h, a in zip(ks, hs, acts):
            saved[i][name] = (xs, gs, half_row, h, a)

    def add_slot():
        k = len(slots)
        slots.append([held[k]] + [hop(held[k], s) for s in range(1, n_tensor)])

    def add(a, b):
        return (a.astype(F32) + b.astype(F32)).astype(BF16)

    def weight_pieces(k, fence=()):
        parts = list(saved[k].values())
        if fence:
            xs, gs, rows, h, a = parts[0]
            parts[0] = (xs, gs, rows, after(h, *fence), a)
        return expert_weight(parts, n_tensor, width)

    def hop_back(grads):
        return [hop(grads[s], n_tensor - s) for s in range(1, n_tensor)]

    def total_of(grads, got):
        return functools.reduce(jnp.add, [v.astype(F32) for v in [grads[0], *got]])

    def weight_total(k):
        grads = weight_pieces(k)
        return total_of(grads, hop_back(grads)).astype(BF16)

    def send_on(k, moving):
        total = totals[k]
        if moving is not None:
            total = add(total, moving)
        return ring(total)

    for _ in range(1, group):
        add_slot()
    slots, mlp_top, mlp_low = after((slots, mlp_top, mlp_low))
    x_top, y_low = plane(mlp_top, 1), plane(mlp_low, 2)
    run("near", 0)
    x_top, y_low, carry["near"] = after((x_top, y_low, carry["near"]))
    x_low, y_top = plane(mlp_low, 1), plane(mlp_top, 2)
    where["one"] = ([(x_top, 0), (y_low, 0)], [(grad_x, 0), (grad_y, 1)])
    run("one", 0)
    x_low, y_top, carry["one"], held[2] = after((x_low, y_top, carry["one"], held[2]))
    for _ in range(3, depth):
        held.append(ring(held[-1]))
    mlp_diag = [plane(x_top, 2), plane(y_low, 1)]
    where["two"] = ([(x_low, 0), (y_top, 0)], [(grad_x, 1), (grad_y, 0)])
    run("two", 0)
    mlp_diag, carry["two"] = after((mlp_diag, carry["two"]))
    add_slot()
    where["diag"] = ([(v, 0) for v in mlp_diag], [(v, 0) for v in grad_diag])
    run("diag", 0)
    slots, carry["diag"] = after((slots, carry["diag"]))
    for k in range(group, last, group):
        while len(slots) < k + group:
            add_slot()
        for name in ("near", "one", "two", "diag"):
            run(name, k)
    totals = {}
    order = list(range(1, depth)) + [0]
    early = order[: depth - group - 1]
    for k in early:
        totals[k] = weight_total(k)
    while len(slots) < depth:
        add_slot()
    slots[-1], totals = after((slots[-1], totals))
    moving = None
    for k in early:
        moving = send_on(k, moving)
    rest = order[len(early) :]

    run("diag", last)
    back_parts = [plane(v, m) for v, m in zip(carry["diag"][1], (1, 2))]
    run("one", last, [carry["diag"]])
    back_parts, carry["one"] = after((back_parts, carry["one"]))
    halves = [plane(v, m) for v, m in zip(carry["one"][1], (1, 2))]
    run("two", last, [carry["one"]])
    low_x, top_y = ((v.astype(F32) + p.astype(F32)).astype(BF16) for v, p in zip(carry["two"][1], back_parts[::-1]))
    halves, low_x, top_y = after((halves, low_x, top_y))
    others = [plane(low_x, 1), plane(top_y, 2)]
    run("near", last, [low_x, top_y])
    others, carry["near"], moving = after((others, carry["near"], moving))

    dy, d_gates, gain_two_all = turn_back(carry["near"][1], halves, others, mixed, grad_wide, gain_mlp)
    out_diag, dy = after((carry["diag"][0], dy))
    out_parts = [plane(v, m) for v, m in zip(out_diag, (1, 2))]
    dy_full = gather_rows(dy)
    late = {rest[0]: weight_pieces(rest[0], [dy])}
    dy_full, late, out_parts = after((dy_full, late, out_parts))
    d_gates = d_gates[:, :n_expert] + d_gates[:, LANES // 2 : LANES // 2 + n_expert]

    arrived = moving
    late_got = hop_back(late[rest[0]])
    out_halves = [plane(v, m) for v, m in zip(carry["one"][0], (1, 2))]
    do_t = jnp.einsum("td,cd->ct", dy_full, w_out, preferred_element_type=F32).astype(BF16)
    out_w_grad = [jnp.einsum("td,ct->dc", dy_full, o, preferred_element_type=F32).astype(BF16) for o in o_t]

    def backward(i, do_t):
        return attn_backward(q_t[i], k_t[i], v_t, do_t, lse[i], cos_t, sin_t, start, i * count, count)

    def weight_grads(ds):
        return [jnp.einsum("td,ct->dc", attn_in, d, preferred_element_type=F32).astype(BF16) for d in ds]

    def part(a, who, rows):
        return lax.dynamic_slice_in_dim(a, who * rows, rows, 0)

    p_at, z_at = lax.rem(e_at, PLANE), e_at // PLANE

    def plane_shares(a):
        quarter = a.shape[0] // PLANE
        return [plane(part(a, p_at ^ m, quarter), m) for m in range(1, PLANE)]

    def plane_sum(a, shares):
        total = part(a, p_at, a.shape[0] // PLANE).astype(F32)
        for v in shares:
            total = total + v.astype(F32)
        return total.astype(BF16)

    def swap(a, bit):
        pairs = [(i, i ^ (bit * PLANE)) for i in range(n_expert)]
        return lax.ppermute(a, "expert", pairs)

    bits = [1 << i for i in range(depth.bit_length() - 1)]

    def upper(bit):
        return (z_at // bit) % 2

    def z_cut(a, bit, tail=None):
        rows = a.shape[0] // 2
        stay, go = part(a, upper(bit), rows), part(a, 1 - upper(bit), rows)
        return stay, go if tail is None else jnp.concatenate([go, tail], axis=0)

    def z_join(a, got, bit):
        return jnp.where(upper(bit) == 0, jnp.concatenate([a, got], 0), jnp.concatenate([got, a], 0))

    first = jnp.concatenate(out_w_grad, axis=1)
    ds = []
    do_t, out_w_grad = after((do_t, out_w_grad))
    if parts == 2:
        ds.append(backward(0, do_t))
        ds[0], out_halves, do_t, late_got = after((ds[0], out_halves, do_t, late_got))
        first = jnp.concatenate(weight_grads(ds[0]) + out_w_grad, axis=1)

    def next_moving(k, got, arrived):
        total = total_of(late[k], got)
        if arrived is not None:
            total = total + arrived.astype(F32)
        return total.astype(BF16)

    moving = next_moving(rest[0], late_got, arrived)
    first, out_halves, moving, do_t = after((first, out_halves, moving, do_t))
    ring_on = [ring(moving[c]) for c in range(2)]
    first_sent = plane_shares(first)
    ds.append(backward(parts - 1, do_t))
    third = rest[1]
    late[third] = weight_pieces(third, [ds[-1]])
    first_sent, ring_on, ds, late = after((first_sent, ring_on, ds, late))

    second = jnp.concatenate(weight_grads(ds[-1]), axis=1)
    first = plane_sum(first, first_sent)
    stay, go = z_cut(first, bits[0])
    second, stay, go, ds = after((second, stay, go, ds))
    second_sent = plane_shares(second)
    got = swap(go, bits[0])
    ring_on.append(ring(moving[2]))
    late_got = hop_back(late[third])
    own_terms, *far_terms, dots = input_terms(
        t_at.reshape(1), tokens, gain_attn, ds, (w_query, key_matrix, value_matrix), n_tensor
    )
    dots = dots[:, 0]
    second_sent, got, ring_on, far_terms, dots, late_got = after((second_sent, got, ring_on, far_terms, dots, late_got))
    moving = next_moving(third, late_got, jnp.stack(ring_on))

    first = add(stay, got)
    out_two = [add(v, p) for v, p in zip(carry["two"][0], out_parts[::-1])]
    gain_two = cols_of(gain_two_all[0], t_at)
    far_gains = [cols_of(gain_two_all[0], peer(s)) for s in range(1, n_tensor)]
    cuts = [z_cut(first, bits[1])] if len(bits) > 1 else []
    cuts, far_terms, dots = after((cuts, far_terms, dots))
    far_terms = [hop(v, s) for s, v in enumerate(far_terms, 1)]
    far_dots = [hop(jnp.concatenate([dots, v]), s) for s, v in enumerate(far_gains, 1)]
    gots = [swap(go, bits[1]) for _, go in cuts]
    gots, far_terms, far_dots, out_two = after((gots, far_terms, far_dots, out_two))
    out_others = [plane(v, m) for v, m in zip(out_two, (1, 2))]
    second = plane_sum(second, second_sent)
    for (stay, _), got in zip(cuts, gots):
        first = add(stay, got)
    for bit in bits[2:]:
        stay, go = z_cut(first, bit)
        first = add(stay, swap(go, bit))
    gain_two = functools.reduce(jnp.add, [gain_two] + [v[n_tok:] for v in far_dots])
    far_dots = [v[:n_tok] for v in far_dots]

    d_attn_in = functools.reduce(jnp.add, [own_terms] + [v.astype(F32) for v in far_terms])
    all_dots = functools.reduce(jnp.add, [dots] + far_dots)
    normed_cols = cols_of(tokens, t_at).astype(F32) * inv_one
    scaled_one = d_attn_in * cols_of(gain_attn, t_at)
    d_norm_one = inv_one * (scaled_one - normed_cols * (all_dots / width)[:, None])
    grad_tokens = cols_of(dy_full, t_at).astype(F32) + d_norm_one
    gain_one = jnp.sum(d_attn_in * normed_cols, axis=0)
    wide = second.shape[1]
    gains = jnp.concatenate([gain_one, gain_two]).astype(BF16).reshape(-1, wide)
    gain_rows = gains.shape[0]
    gains = jnp.pad(gains, ((0, 16 - gain_rows), (0, 0)))
    grad_logits = gather_rows(gates * (d_gates - jnp.sum(gates * d_gates, axis=1, keepdims=True)))
    for i, bit in enumerate(bits):
        rows = second.shape[0] // 2
        stay, go = z_cut(second, bit, gains)
        back = bits[-1 - i]
        first, go = after((first, go))
        got, first_got = swap(go, bit), swap(first, back)
        got, first_got, out_others = after((got, first_got, out_others))
        second, gains = add(stay, got[:rows]), add(gains, got[rows:])
        first = z_join(first, first_got, back)
    first, second, moving = after((first, second, moving))
    first_all = [first] + [plane(first, m) for m in range(1, PLANE)]
    late[0] = weight_pieces(0, [first])
    for bit in bits[::-1]:
        second = z_join(second, swap(second, bit), bit)
    moving, second = after((moving, second))
    ring_on = [ring(moving[c]) for c in range(3)]
    rows = second.shape[0]
    second = jnp.concatenate([second, gains], axis=0)
    out_top, out_low = carry["near"][0]
    top_rows = out_top.astype(F32) + out_halves[0].astype(F32) + out_others[1].astype(F32)
    low_rows = out_low.astype(F32) + out_others[0].astype(F32) + out_halves[1].astype(F32)
    block_out = to_cols((mixed + jnp.concatenate([top_rows, low_rows], axis=0)).astype(BF16))
    second, block_out, first_all, ring_on[0], late[0] = after((second, block_out, first_all, ring_on[0], late[0]))
    late_got = hop_back(late[0])
    second_all = [second] + [plane(second, m) for m in range(1, PLANE)]
    own = total_of(late[0], late_got)
    final = [own[c] + ring_on[c].astype(F32) for c in range(2)]
    second_all, final = after((second_all, final))
    gains = functools.reduce(jnp.add, [v[rows : rows + gain_rows].astype(F32) for v in second_all]).reshape(-1)
    cuts = [w.shape[1] // parts for w in (w_query, key_matrix, value_matrix)]
    laid = lay_out(p_at.reshape(1), first_all, second_all, parts, cuts)
    grad_query, grad_key, grad_value, grad_out = laid
    grad_query, down_arrived = after((grad_query, ring_on[2]))
    final.append((own[2] + down_arrived.astype(F32)).T)
    return (
        block_out,
        grad_tokens,
        grad_logits,
        gains[:col_width],
        grad_query,
        grad_key,
        grad_value,
        grad_out,
        gains[col_width:],
        final[0][None],
        final[1][None],
        final[2][None],
    )


def solution(mesh):
    return jax.shard_map(
        body,
        mesh=mesh,
        in_specs=(
            P("expert", None),
            P("expert"),
            P("expert", None),
            P("expert", None),
            P(),
            P(None, "tensor"),
            P(None, "tensor"),
            P(None, "tensor"),
            P("tensor", None),
            P(),
            P("expert", None, "tensor"),
            P("expert", None, "tensor"),
            P("expert", "tensor", None),
            P("expert", "tensor"),
        ),
        out_specs=(
            P("expert", "tensor"),
            P("expert", "tensor"),
            P("expert", None),
            P("tensor"),
            P(None, "tensor"),
            P(None, "tensor"),
            P(None, "tensor"),
            P("tensor", None),
            P("tensor"),
            P("expert", None, "tensor"),
            P("expert", None, "tensor"),
            P("expert", "tensor", None),
        ),
        check_vma=False,
    )
```

```python
import functools

import jax
import jax.numpy as jnp
from jax import lax
from jax.experimental import pallas as pl
from jax.experimental.pallas import tpu as pltpu
from jax.sharding import PartitionSpec as P

HEAD_SIZE = 64
EPS = 1e-06
THETA = 10000.0
NEG = -1e30
PLANE = 4
LANES = 128
F32 = jnp.float32
BF16 = jnp.bfloat16
NT = (((1,), (1,)), ((), ()))
TN = (((0,), (0,)), ((), ()))


def dot(a, b):
    return jnp.dot(a, b, preferred_element_type=F32)


def dot_nt(a, b):
    return lax.dot_general(a, b, NT, preferred_element_type=F32)


def dot_tn(a, b):
    return lax.dot_general(a, b, TN, preferred_element_type=F32)


def attn_mask(start, row_start, block, keys):
    first = start[:, row_start : row_start + block]
    first = jnp.concatenate([first, first], axis=1)
    key_at = lax.broadcasted_iota(jnp.int32, (keys, 2 * block), 0)
    lane = lax.broadcasted_iota(jnp.int32, (1, 2 * block), 1)
    row_at = row_start + jnp.where(lane >= block, lane - block, lane)
    return (key_at >= first) & (key_at <= row_at)


def rope(x, c, s):
    half = x.shape[0] // 2
    a, b = x[:half], x[half:]
    return jnp.concatenate([a * c - b * s, b * c + a * s], axis=0)


def attn_fwd_kernel(block, q_ref, k_ref, v_ref, cos_ref, sin_ref, start_ref, qo_ref, ko_ref, o_ref, lse_ref):
    hd = HEAD_SIZE
    n = k_ref.shape[1]
    c, s = cos_ref[...], sin_ref[...]
    k_rot = rope(k_ref[...], c, s)
    ko_ref[...] = k_rot.astype(BF16)
    keys = k_rot.T.astype(BF16)
    q0 = rope(q_ref[0:hd], c, s).astype(BF16)
    q1 = rope(q_ref[hd : 2 * hd], c, s).astype(BF16)
    qo_ref[0:hd] = q0
    qo_ref[hd : 2 * hd] = q1
    start = start_ref[...]
    for r0 in range(0, n, block):
        cn = r0 + block
        qb = jnp.concatenate([q0[:, r0:cn], q1[:, r0:cn]], axis=1) * jnp.asarray(hd**-0.5, BF16)
        scores = dot(keys[:cn], qb)
        scores = jnp.where(attn_mask(start, r0, block, cn), scores, NEG)
        peak = jnp.max(scores, axis=0, keepdims=True)
        p = jnp.exp(scores - peak)
        total = jnp.sum(p, axis=0, keepdims=True)
        o = dot(v_ref[:, :cn], p.astype(BF16)) / total
        o_ref[0:hd, r0:cn] = o[:, :block].astype(BF16)
        o_ref[hd : 2 * hd, r0:cn] = o[:, block:].astype(BF16)
        lse = peak + jnp.log(total)
        lse_ref[0, 0:1, r0:cn] = lse[:, :block]
        lse_ref[0, 1:2, r0:cn] = lse[:, block:]


def attn_bwd_kernel(
    block, q_ref, k_ref, v_ref, do_ref, lse_ref, cos_ref, sin_ref, start_ref, dq_ref, dk_ref, dv_ref, dk_acc, dv_acc
):
    hd = HEAD_SIZE
    n = k_ref.shape[1]
    c, s = cos_ref[...], sin_ref[...]
    keys = k_ref[...].astype(F32).T.astype(BF16)
    vals = v_ref[...].astype(F32).T.astype(BF16)
    start = start_ref[...]
    dk_acc[...] = jnp.zeros_like(dk_acc)
    dv_acc[...] = jnp.zeros_like(dv_acc)
    scale = hd**-0.5
    for r0 in range(0, n, block):
        cn = r0 + block
        qb = jnp.concatenate([q_ref[0:hd, r0:cn], q_ref[hd : 2 * hd, r0:cn]], axis=1)
        gb = jnp.concatenate([do_ref[0:hd, r0:cn], do_ref[hd : 2 * hd, r0:cn]], axis=1)
        lse = jnp.concatenate([lse_ref[0, 0:1, r0:cn], lse_ref[0, 1:2, r0:cn]], axis=1)
        scores = dot(keys[:cn], qb * jnp.asarray(scale, BF16))
        p = jnp.exp(jnp.where(attn_mask(start, r0, block, cn), scores, NEG) - lse)
        dv_acc[:, :cn] += dot_nt(gb, p.astype(BF16))
        dp = dot(vals[:cn], gb)
        delta = jnp.sum(p * dp, axis=0, keepdims=True)
        ds = (p * (dp - delta) * scale).astype(BF16)
        dq = dot(k_ref[:, :cn], ds)
        dk_acc[:, :cn] += dot_nt(qb, ds)
        cb, sb = c[:, r0:cn], -s[:, r0:cn]
        dq_ref[0:hd, r0:cn] = rope(dq[:, :block], cb, sb).astype(BF16)
        dq_ref[hd : 2 * hd, r0:cn] = rope(dq[:, block:], cb, sb).astype(BF16)
    dk_ref[...] = rope(dk_acc[...], c, -s).astype(BF16)
    dv_ref[...] = dv_acc[...].astype(BF16)


def attn_cost(heads, n, products):
    return pl.CostEstimate(
        flops=products * heads * n * n * HEAD_SIZE * 2, bytes_accessed=8 * heads * n * HEAD_SIZE, transcendentals=heads * n * n
    )


def attn_forward(q_t, k_t, v_t, cos_t, sin_t, start, first, count):
    n = q_t.shape[1]
    hd = HEAD_SIZE
    block = min(256, n)
    pair = pl.BlockSpec((2 * hd, n), lambda h: (h + first, 0))
    one = pl.BlockSpec((hd, n), lambda h: (h + first, 0))
    table = pl.BlockSpec((hd // 2, n), lambda h: (0, 0))
    return pl.pallas_call(
        functools.partial(attn_fwd_kernel, block),
        grid=(count,),
        in_specs=[pair, one, one, table, table, pl.BlockSpec((1, n), lambda h: (0, 0))],
        out_specs=[pl.BlockSpec((r * hd, n), lambda h: (h, 0)) for r in (2, 1, 2)]
        + [pl.BlockSpec((1, 2, n), lambda h: (h, 0, 0))],
        out_shape=[jax.ShapeDtypeStruct((r * count * hd, n), BF16) for r in (2, 1, 2)]
        + [jax.ShapeDtypeStruct((count, 2, n), F32)],
        compiler_params=pltpu.CompilerParams(vmem_limit_bytes=48 * 2**20),
        cost_estimate=attn_cost(2 * count, n, 4),
        name="attn_forward",
    )(q_t, k_t, v_t, cos_t, sin_t, start)


def attn_backward(q_t, k_t, v_t, do_t, lse, cos_t, sin_t, start, first, count):
    n = q_t.shape[1]
    hd = HEAD_SIZE
    block = min(256, n)
    table = pl.BlockSpec((hd // 2, n), lambda h: (0, 0))
    return pl.pallas_call(
        functools.partial(attn_bwd_kernel, block),
        grid=(count,),
        in_specs=[
            pl.BlockSpec((2 * hd, n), lambda h: (h, 0)),
            pl.BlockSpec((hd, n), lambda h: (h, 0)),
            pl.BlockSpec((hd, n), lambda h: (h + first, 0)),
            pl.BlockSpec((2 * hd, n), lambda h: (h + first, 0)),
            pl.BlockSpec((1, 2, n), lambda h: (h, 0, 0)),
            table,
            table,
            pl.BlockSpec((1, n), lambda h: (0, 0)),
        ],
        out_specs=[pl.BlockSpec((r * hd, n), lambda h: (h, 0)) for r in (2, 1, 1)],
        out_shape=[jax.ShapeDtypeStruct((r * count * hd, n), BF16) for r in (2, 1, 1)],
        scratch_shapes=[pltpu.VMEM((hd, n), F32), pltpu.VMEM((hd, n), F32)],
        compiler_params=pltpu.CompilerParams(vmem_limit_bytes=48 * 2**20),
        cost_estimate=attn_cost(2 * count, n, 4),
        name="attn_backward",
    )(q_t, k_t, v_t, do_t, lse, cos_t, sin_t, start)


def data_kernel(first, last, blocks, tiles, slots, pieces, expert_ref, *refs):
    refs = list(refs)
    at, tile_at = pl.program_id(0), pl.program_id(1)
    x, g_all = refs[0][...], refs[blocks][...]
    for i in range(1, blocks):
        x = jnp.where(at == i, refs[i][...], x)
        g_all = jnp.where(at == i, refs[blocks + i][...], g_all)
    weights = refs[2 * blocks : 2 * blocks + slots * pieces]
    refs = refs[2 * blocks + slots * pieces :]
    if not first:
        out_in, dx_in, dgate_in = refs[:3]
        refs = refs[3:]
    if last:
        out_refs, dx_refs = refs[:blocks], refs[blocks : 2 * blocks]
        refs = refs[2 * blocks :]
    else:
        out_ref, dx_ref, dgate_ref = refs[:3]
        refs = refs[3:]
    hs, acts = refs[:slots], refs[slots : 2 * slots]
    acc_o, acc_x, held, sems = refs[2 * slots :]
    opening = (at == 0) & (tile_at == 0)

    def copies(n):
        return [pltpu.make_async_copy(weights[n].at[c], held.at[n, c], sems.at[n, c]) for c in range(3)]

    @pl.when(opening)
    def _():
        for n in range(slots * pieces):
            for copy in copies(n):
                copy.start()

    width = x.shape[1]
    g = g_all[:, :width]
    gates = g_all[:, width:].astype(F32)
    lane = lax.broadcasted_iota(jnp.int32, gates.shape, 1)
    dgate = None if first else dgate_in[...]
    for j in range(slots):
        here = lane == expert_ref[j]
        both = here | (lane == expert_ref[j] + LANES // 2)
        gate = jnp.sum(jnp.where(both, gates, 0.0), axis=1, keepdims=True)
        row_sum = None
        for i in range(pieces):
            n = j * pieces + i

            @pl.when(opening)
            def _():
                for copy in copies(n):
                    copy.wait()

            hid = held.shape[3]
            gate_pre = dot(x, held[n, 0])
            up_pre = dot(x, held[n, 1])
            d_hidden = dot(g, held[n, 2])
            sig = jax.nn.sigmoid(gate_pre)
            silu = gate_pre * sig
            act = silu * up_pre
            part = jnp.sum(act * d_hidden, axis=1, keepdims=True)
            row_sum = part if row_sum is None else row_sum + part
            act_w = (act * gate).astype(BF16)
            d_hidden = d_hidden * gate
            d_up = (d_hidden * silu).astype(BF16)
            d_gate = (d_hidden * up_pre * (sig + silu * (1.0 - sig))).astype(BF16)
            hs[j][:, 2 * i * hid : (2 * i + 1) * hid] = d_gate
            hs[j][:, (2 * i + 1) * hid : (2 * i + 2) * hid] = d_up
            acts[j][:, i * hid : (i + 1) * hid] = act_w
            out_term = dot_nt(act_w, held[n, 2])
            dx_term = dot_nt(d_gate, held[n, 0]) + dot_nt(d_up, held[n, 1])
            if n == 0 and first:
                acc_o[...] = out_term
                acc_x[...] = dx_term
            elif n == 0:
                acc_o[...] = out_in[...].astype(F32) + out_term
                acc_x[...] = dx_in[...].astype(F32) + dx_term
            else:
                acc_o[...] += out_term
                acc_x[...] += dx_term
        term = jnp.where(here, row_sum, 0.0)
        dgate = term if dgate is None else dgate + term
    if last:
        high = dgate.astype(BF16).astype(F32)
        low = pltpu.roll(dgate - high, LANES // 2, 1)
        tail = jnp.where(lane < LANES // 2, high, low).astype(BF16)
        for i in range(blocks):

            @pl.when(at == i)
            def _():
                out_refs[i][...] = acc_o[...].astype(BF16)
                dx_refs[i][:, :width] = acc_x[...].astype(BF16)
                dx_refs[i][:, width:] = tail
    else:
        out_ref[...] = acc_o[...].astype(BF16)
        dx_ref[...] = acc_x[...].astype(BF16)
        dgate_ref[...] = dgate


def expert_data(experts, xs, gs, rows, ws, carry, last):
    blocks = len(xs)
    width = xs[0][0].shape[1]
    tile = min(256, rows)
    tiles = rows // tile
    full = gs[0][0].shape[1]
    slots = experts.shape[0]
    pieces = len(ws) // slots
    hidden = ws[0].shape[2]
    first = carry is None
    total = blocks * rows

    def out_spec(columns):
        return pl.BlockSpec((tile, columns), lambda b, i: (b * tiles + i, 0))

    def in_spec(columns, offset):
        return pl.BlockSpec((tile, columns), lambda b, i: (offset * tiles + i, 0))

    def own_spec(columns, j):
        return pl.BlockSpec((tile, columns), lambda b, i: (jnp.clip((b - j) * tiles + i, 0, tiles - 1), 0))

    ins = [experts, *[x for x, _ in xs], *[g for g, _ in gs], *ws]
    specs = [pl.BlockSpec(memory_space=pltpu.SMEM)]
    specs += [in_spec(width, o) for _, o in xs] + [in_spec(full, o) for _, o in gs]
    specs += [pl.BlockSpec(memory_space=pl.ANY)] * len(ws)
    if not first:
        ins += list(carry)
        specs += [out_spec(width), out_spec(width), out_spec(LANES)]
    if last:
        out_specs = [own_spec(c, j) for c in (width, full) for j in range(blocks)]
        out_shape = [jax.ShapeDtypeStruct((rows, c), BF16) for c in (width, full) for _ in range(blocks)]
    else:
        out_specs = [out_spec(c) for c in (width, width, LANES)]
        out_shape = [jax.ShapeDtypeStruct((total, c), t) for c, t in ((width, BF16), (width, BF16), (LANES, F32))]
    n = len(out_specs)
    kept = [2 * pieces * hidden] * slots + [pieces * hidden] * slots
    single = pieces * hidden
    outs = pl.pallas_call(
        functools.partial(data_kernel, first, last, blocks, tiles, slots, pieces),
        grid=(blocks, tiles),
        in_specs=specs,
        out_specs=out_specs + [out_spec(c) for c in kept],
        out_shape=out_shape + [jax.ShapeDtypeStruct((total, c), BF16) for c in kept],
        scratch_shapes=[
            pltpu.VMEM((tile, width), F32),
            pltpu.VMEM((tile, width), F32),
            pltpu.VMEM((len(ws), 3, width, hidden), BF16),
            pltpu.SemaphoreType.DMA((len(ws), 3)),
        ],
        compiler_params=pltpu.CompilerParams(vmem_limit_bytes=60 * 2**20),
        cost_estimate=pl.CostEstimate(
            flops=3 * slots * total * width * single,
            bytes_accessed=total * width * 12 + slots * pieces * width * hidden * 6,
            transcendentals=slots * total * single,
        ),
        name="expert_data",
    )(*ins)
    result = (outs[:blocks], outs[blocks:n]) if last else outs[:n]
    return result, outs[n : n + slots], outs[n + slots :]


def weight_kernel(shape, pieces, *refs):
    xt = gt = None
    refs = list(refs)
    for blocks in shape:
        xs, gs, h, a = refs[:blocks], refs[blocks : 2 * blocks], refs[2 * blocks], refs[2 * blocks + 1]
        refs = refs[2 * blocks + 2 :]
        rows = xs[0].shape[0]
        for i in range(blocks):
            span = slice(i * rows, (i + 1) * rows)
            xp, gp = dot_tn(xs[i][...], h[span]), dot_tn(gs[i][...], a[span])
            xt, gt = (xp, gp) if xt is None else (xt + xp, gt + gp)
    outs = refs
    hid = outs[0].shape[2]
    for i in range(pieces):
        outs[i][0] = xt[:, 2 * i * hid : (2 * i + 1) * hid].astype(BF16)
        outs[i][1] = xt[:, (2 * i + 1) * hid : (2 * i + 2) * hid].astype(BF16)
        outs[i][2] = gt[:, i * hid : (i + 1) * hid].astype(BF16)


def expert_weight(parts, pieces, width):
    hidden = parts[0][4].shape[1] // pieces
    block = 256
    ins, specs, shape, total = [], [], [], 0
    for xs, gs, rows, h, a in parts:
        for v, o in [*xs, *gs]:
            ins.append(v)
            specs.append(pl.BlockSpec((rows, block), lambda i, o=o: (o, i)))
        for v in (h, a):
            ins.append(v)
            specs.append(pl.BlockSpec(v.shape, lambda i: (0, 0), pipeline_mode=pl.Buffered(1)))
        shape.append(len(xs))
        total += h.shape[0]
    return pl.pallas_call(
        functools.partial(weight_kernel, tuple(shape), pieces),
        grid=(width // block,),
        in_specs=specs,
        out_specs=[pl.BlockSpec((3, block, hidden), lambda i: (0, i, 0))] * pieces,
        out_shape=[jax.ShapeDtypeStruct((3, width, hidden), BF16)] * pieces,
        compiler_params=pltpu.CompilerParams(vmem_limit_bytes=60 * 2**20),
        cost_estimate=pl.CostEstimate(
            flops=total * width * hidden * pieces,
            bytes_accessed=total * (width * 4 + hidden * pieces * 6) + width * hidden * pieces * 6,
            transcendentals=0,
        ),
        name="expert_weight",
    )(*ins)


def rms_parts(v):
    inv = lax.rsqrt(jnp.mean(v * v, axis=1, keepdims=True) + EPS)
    return inv, v * inv


def join_kernel(pieces, at_ref, x_ref, gain_ref, *refs):
    os, ws = refs[:pieces], refs[pieces : 2 * pieces]
    mixed_ref, top_ref, low_ref = refs[2 * pieces :]
    mixed = x_ref[...].astype(F32)
    for o, w in zip(os, ws):
        mixed = mixed + dot_tn(o[...], w[...])
    mixed_ref[...] = mixed
    rows = (rms_parts(mixed)[1] * gain_ref[...]).astype(BF16)
    for i, ref in enumerate((top_ref, low_ref)):

        @pl.when(pl.program_id(0) == i)
        def _():
            ref[...] = rows


def join_heads(at, tokens, gain, own, far, ws, rows):
    width = tokens.shape[1]
    half = rows // 2
    heads = own[0].shape[0]
    n = len(ws)
    o_specs = [pl.BlockSpec((heads, half), lambda i, at: (0, at[0] * 2 + i))] * len(own)
    o_specs += [pl.BlockSpec((heads, half), lambda i, at: (0, i))] * len(far)
    os = [*own, *far]
    if half % LANES:
        os = [lax.dynamic_slice_in_dim(o, at[0] * rows, rows, 1) for o in own] + far
        os = [jnp.stack([o[:, :half], o[:, half:]]) for o in os]
        o_specs = [pl.BlockSpec((None, heads, half), lambda i, at: (i, 0, 0))] * n
    once = pl.BlockSpec((half, width), lambda i, at: (0, 0))
    return pl.pallas_call(
        functools.partial(join_kernel, n),
        grid_spec=pltpu.PrefetchScalarGridSpec(
            num_scalar_prefetch=1,
            grid=(2,),
            in_specs=[
                pl.BlockSpec((half, width), lambda i, at: (at[0] * 2 + i, 0)),
                pl.BlockSpec((1, width), lambda i, at: (0, 0)),
            ]
            + o_specs
            + [pl.BlockSpec((heads, width), lambda i, at, b=b: (b, 0)) for _, b in ws],
            out_specs=[pl.BlockSpec((half, width), lambda i, at: (i, 0)), once, once],
        ),
        out_shape=[
            jax.ShapeDtypeStruct((rows, width), F32),
            jax.ShapeDtypeStruct((half, width), BF16),
            jax.ShapeDtypeStruct((half, width), BF16),
        ],
        compiler_params=pltpu.CompilerParams(vmem_limit_bytes=48 * 2**20),
        cost_estimate=pl.CostEstimate(
            flops=2 * rows * heads * n * width, bytes_accessed=rows * width * 8, transcendentals=0
        ),
        name="join_heads",
    )(at, tokens, gain[None, :], *os, *[w for w, _ in ws])


def input_kernel(groups, n_tensor, at_ref, x_ref, gain_ref, *refs):
    ds, ws = refs[: 3 * groups], refs[3 * groups : 3 * groups + 3]
    own_ref, *fars, dots_ref, acc = refs[3 * groups + 3 :]
    total = None
    for j in range(3):
        d = jnp.concatenate([ds[3 * i + j][...] for i in range(groups)], axis=0)
        term = lax.dot_general(d, ws[j][...], (((0,), (1,)), ((), ())), preferred_element_type=F32)
        total = term if total is None else total + term
    acc[...] = total
    normed = rms_parts(x_ref[...].astype(F32))[1]
    dots_ref[...] = jnp.sum(total * gain_ref[...] * normed, axis=1, keepdims=True)
    cols = own_ref.shape[1]
    for s, ref in enumerate([own_ref, *fars]):
        who = lax.rem(at_ref[0] + s, n_tensor)
        ref[...] = acc[:, pl.ds(pl.multiple_of(who * cols, cols), cols)].astype(ref.dtype)


def input_terms(at, tokens, gain, ds, ws, n_tensor):
    n, width = tokens.shape
    cols = width // n_tensor
    tile = min(256, n)
    flat = [d for group in ds for d in group]
    return pl.pallas_call(
        functools.partial(input_kernel, len(ds), n_tensor),
        grid_spec=pltpu.PrefetchScalarGridSpec(
            num_scalar_prefetch=1,
            grid=(n // tile,),
            in_specs=[pl.BlockSpec((tile, width), lambda i, at: (i, 0)), pl.BlockSpec((1, width), lambda i, at: (0, 0))]
            + [pl.BlockSpec((d.shape[0], tile), lambda i, at: (0, i)) for d in flat]
            + [pl.BlockSpec(w.shape, lambda i, at: (0, 0)) for w in ws],
            out_specs=[pl.BlockSpec((tile, cols), lambda i, at: (i, 0))] * n_tensor
            + [pl.BlockSpec((tile, 1), lambda i, at: (i, 0))],
            scratch_shapes=[pltpu.VMEM((tile, width), F32)],
        ),
        out_shape=[jax.ShapeDtypeStruct((n, cols), F32)]
        + [jax.ShapeDtypeStruct((n, cols), BF16)] * (n_tensor - 1)
        + [jax.ShapeDtypeStruct((n, 1), F32)],
        compiler_params=pltpu.CompilerParams(vmem_limit_bytes=48 * 2**20),
        cost_estimate=pl.CostEstimate(
            flops=2 * n * width * sum(w.shape[1] for w in ws), bytes_accessed=n * width * 8, transcendentals=0
        ),
        name="input_terms",
    )(at, tokens, gain[None, :], *flat, *ws)


def turn_kernel(top_ref, low_ref, xt_ref, yl_ref, xl_ref, yt_ref, mixed_ref, grad_ref, gain_ref, dy_ref, gates_ref, sum_ref):
    step = pl.program_id(0)
    width = mixed_ref.shape[1]
    upper = step == 0
    back = jnp.where(upper, top_ref[...], low_ref[...]).astype(F32)
    back = back + jnp.where(upper, xt_ref[...], xl_ref[...]).astype(F32)
    back = back + jnp.where(upper, yt_ref[...], yl_ref[...]).astype(F32)
    gates_ref[...] = back[:, width:]
    d_in = back[:, :width]
    inv, normed = rms_parts(mixed_ref[...])
    scaled = d_in * gain_ref[...]
    dots = jnp.mean(scaled * normed, axis=1, keepdims=True)
    dy_ref[...] = (grad_ref[...].astype(F32) + inv * (scaled - normed * dots)).astype(BF16)
    part = jnp.sum(d_in * normed, axis=0, keepdims=True)

    @pl.when(upper)
    def _():
        sum_ref[...] = part

    @pl.when(jnp.logical_not(upper))
    def _():
        sum_ref[...] += part


def turn_back(near, halves, others, mixed, grad_wide, gain):
    rows, width = mixed.shape
    half, full = rows // 2, near[0].shape[1]

    def spec(c):
        return pl.BlockSpec((half, c), lambda i: (i, 0))

    const = pl.BlockSpec((half, full), lambda i: (0, 0))
    line = pl.BlockSpec((1, width), lambda i: (0, 0))
    return pl.pallas_call(
        turn_kernel,
        grid=(2,),
        in_specs=[const] * 6 + [spec(width), spec(width), line],
        out_specs=[spec(width), spec(LANES), line],
        out_shape=[
            jax.ShapeDtypeStruct((rows, width), BF16),
            jax.ShapeDtypeStruct((rows, LANES), F32),
            jax.ShapeDtypeStruct((1, width), F32),
        ],
        compiler_params=pltpu.CompilerParams(vmem_limit_bytes=48 * 2**20),
        cost_estimate=pl.CostEstimate(flops=0, bytes_accessed=rows * width * 16, transcendentals=0),
        name="turn_back",
    )(*near, *halves, *others, mixed, grad_wide, gain[None, :])


def lay_out_kernel(halves, cuts, at_ref, *refs):
    q_out, k_out, v_out, o_out = refs[2 * PLANE :]
    rows = q_out.shape[0]
    for m in range(PLANE):

        @pl.when(pl.program_id(0) == m)
        def _():
            first, second = refs[m], refs[PLANE + m]
            parts = [second] if halves == 1 else [first, second]
            for out, cut, left in zip((q_out, k_out, v_out), cuts, (0, cuts[0], cuts[0] + cuts[1])):
                for i, part in enumerate(parts):
                    out[:, i * cut : (i + 1) * cut] = part[:rows, left : left + cut].astype(F32)
            wide = 0 if halves == 1 else sum(cuts)
            o_out[...] = first[:, wide:].astype(F32).T


def lay_out(at, first, second, halves, cuts):
    rows = first[0].shape[0]
    out_width = first[0].shape[1] - (0 if halves == 1 else sum(cuts))
    shapes = [(PLANE * rows, halves * c) for c in cuts] + [(out_width, PLANE * rows)]
    specs = [pl.BlockSpec((rows, halves * c), lambda m, at: (at[0] ^ m, 0)) for c in cuts]
    return pl.pallas_call(
        functools.partial(lay_out_kernel, halves, cuts),
        grid_spec=pltpu.PrefetchScalarGridSpec(
            num_scalar_prefetch=1,
            grid=(PLANE,),
            in_specs=[pl.BlockSpec(v.shape, lambda m, at: (0, 0)) for v in [*first, *second]],
            out_specs=specs + [pl.BlockSpec((out_width, rows), lambda m, at: (0, at[0] ^ m))],
        ),
        out_shape=[jax.ShapeDtypeStruct(v, F32) for v in shapes],
        compiler_params=pltpu.CompilerParams(vmem_limit_bytes=48 * 2**20),
        cost_estimate=pl.CostEstimate(flops=0, bytes_accessed=24 * rows * out_width, transcendentals=0),
        name="lay_out",
    )(at, *first, *second)


def after(x, *others):
    leaves, tree = jax.tree.flatten(x)
    extra = jax.tree.leaves(others)
    held = lax.optimization_barrier(tuple(leaves) + tuple(extra))
    return jax.tree.unflatten(tree, held[: len(leaves)])


def body(
    tokens,
    segment_ids,
    router_logits,
    expert_ids,
    gain_attn,
    w_query,
    key_matrix,
    value_matrix,
    w_out,
    gain_mlp,
    w_gate,
    w_up,
    w_down,
    out_grad,
):
    n_tok, width = tokens.shape
    col_width = out_grad.shape[1]
    n_tensor = width // col_width
    n_expert = router_logits.shape[1]
    depth = n_expert // PLANE
    my_row = n_tok // n_tensor
    t_at = lax.axis_index("tensor")
    e_at = lax.axis_index("expert")

    def hop(x, step):
        pairs = [(i, (i + step) % n_tensor) for i in range(n_tensor)]
        return jax.tree.map(lambda a: lax.ppermute(a, "tensor", pairs), x)

    def plane(x, mask):
        pairs = [(i, i ^ mask) for i in range(n_expert)]
        return jax.tree.map(lambda a: lax.ppermute(a, "expert", pairs), x)

    def ring(x, step=1):
        pairs = [(i, (i + step * PLANE) % n_expert) for i in range(n_expert)]
        return jax.tree.map(lambda a: lax.ppermute(a, "expert", pairs), x)

    def peer(step):
        return lax.rem(t_at + step + n_tensor, n_tensor)

    def rows_of(x, who):
        return lax.dynamic_slice_in_dim(x, who * my_row, my_row, 0)

    def cols_of(x, who):
        return lax.dynamic_slice_in_dim(x, who * col_width, col_width, x.ndim - 1)

    def place(parts, axis):
        if n_tensor == 2:
            return jnp.where(t_at == 0, jnp.concatenate(parts, axis), jnp.concatenate(parts[::-1], axis))
        size = parts[0].shape[axis]
        shape = list(parts[0].shape)
        shape[axis] *= n_tensor
        out = jnp.zeros(shape, parts[0].dtype)
        for s, v in enumerate(parts):
            out = lax.dynamic_update_slice_in_dim(out, v, peer(-s) * size, axis)
        return out

    def to_rows(x):
        return place([rows_of(x, t_at)] + [hop(rows_of(x, peer(s)), s) for s in range(1, n_tensor)], 1)

    def to_cols(x):
        return place([cols_of(x, t_at)] + [hop(cols_of(x, peer(s)), s) for s in range(1, n_tensor)], 0)

    def gather_rows(x):
        return place([x] + [hop(x, s) for s in range(1, n_tensor)], 0)

    ids_rows = rows_of(expert_ids, t_at)
    logit_rows = rows_of(router_logits, t_at)
    expert_range = jnp.arange(n_expert, dtype=jnp.int32)
    used = jnp.any(ids_rows[:, :, None] == expert_range[None, None, :], axis=1)
    masked = jnp.where(used, logit_rows, NEG)
    weights = jnp.where(used, jnp.exp(masked - jnp.max(masked, axis=1, keepdims=True)), 0.0)
    gates = weights / jnp.sum(weights, axis=1, keepdims=True)
    pad = ((0, 0), (0, LANES // 2 - n_expert))
    high = lax.optimization_barrier(gates.astype(BF16))
    low = (gates - high.astype(F32)).astype(BF16)
    gate_pair = jnp.concatenate([jnp.pad(high, pad), jnp.pad(low, pad)], axis=1)
    grad_low = out_grad.astype(BF16)
    grad_cols = [rows_of(grad_low, peer(s)) for s in range(n_tensor)]
    grad_cols, w_up, gate_pair = after((grad_cols, w_up, gate_pair))
    grad_cols = [grad_cols[0]] + [hop(grad_cols[s], s) for s in range(1, n_tensor)]
    held = [jnp.stack([w_gate[0], w_up[0], w_down[0].T])]
    grad_cols, held[0] = after((grad_cols, held[0]))
    grad_wide = jnp.concatenate([place(grad_cols, 1), gate_pair], axis=1)
    half_row = my_row // 2

    start = jnp.sum((segment_ids[:, None] < segment_ids[None, :]).astype(jnp.int32), axis=0)
    places = jnp.arange(n_tok, dtype=jnp.int32) - start
    half = HEAD_SIZE // 2
    freq = jnp.power(THETA, -2.0 * jnp.arange(half, dtype=F32) / HEAD_SIZE)
    angles = freq[:, None] * places.astype(F32)[None, :]
    cos_t, sin_t = jnp.cos(angles), jnp.sin(angles)
    start = start[None, :]
    held.append(ring(held[0]))
    tokens, grad_wide = after((tokens, grad_wide))
    grad_x, grad_y = plane(grad_wide, 1), plane(grad_wide, 2)
    out_pieces = [w_out] + [hop(w_out, s) for s in range(1, n_tensor)]
    slots = [[held[0]] + [hop(held[0], s) for s in range(1, n_tensor)]]
    x_full = tokens.astype(F32)
    inv_one = lax.rsqrt(jnp.mean(x_full * x_full, axis=1, keepdims=True) + EPS)
    normed_one = x_full * inv_one
    attn_in = (normed_one * gain_attn).astype(BF16)

    def project(w):
        return jnp.einsum("td,dc->ct", attn_in, w, preferred_element_type=F32)

    v_t = project(value_matrix).astype(BF16)
    q_pre, k_pre = project(w_query), project(key_matrix)
    kv = k_pre.shape[0] // HEAD_SIZE
    parts = 2 if kv % 2 == 0 else 1
    count = kv // parts
    q_t, k_t, o_t, lse = ([None] * parts for _ in range(4))
    far_os = []

    def head_group(i):
        q_t[i], k_t[i], o_t[i], lse[i] = attn_forward(q_pre, k_pre, v_t, cos_t, sin_t, start, i * count, count)

    def far_heads(i):
        sent = [lax.dynamic_slice_in_dim(o_t[i], peer(s) * my_row, my_row, 1) for s in range(1, n_tensor)]
        return [hop(v, s) for s, v in enumerate(sent, 1)]

    for i in range(parts):
        head_group(i)
    o_t, grad_x, grad_y = after((o_t, grad_x, grad_y))
    grad_diag = [plane(grad_x[:half_row], 2), plane(grad_y[half_row:], 1)]
    far_os = [far_heads(i) for i in range(parts)]
    far = [far_os[i][s] for s in range(n_tensor - 1) for i in range(parts)]
    out_ws = [(w, i) for w in out_pieces for i in range(parts)]
    mixed, mlp_top, mlp_low = join_heads(t_at.reshape(1), tokens, gain_mlp, o_t, far, out_ws, my_row)
    mlp_top, mlp_low, grad_diag, held[1] = after((mlp_top, mlp_low, grad_diag, held[1]))
    held.append(ring(held[1]))

    group = 2 if depth % 2 == 0 else 1
    last = depth - group
    carry = dict.fromkeys(("near", "one", "two", "diag"))
    saved = [{} for _ in range(depth)]
    where = {
        "near": ([(mlp_top, 0), (mlp_low, 0)], [(grad_wide, 0), (grad_wide, 1)]),
    }

    def run(name, k, fence=()):
        ks = range(k, k + group)
        experts = jnp.stack([lax.rem(e_at - i * PLANE + n_expert, n_expert) for i in ks])
        experts = after(experts, *fence) if fence else experts
        flat = [w for i in ks for w in slots[i]]
        xs, gs = where[name]
        carry[name], hs, acts = expert_data(experts, xs, gs, half_row, flat, carry[name], k == last)
        for i, h, a in zip(ks, hs, acts):
            saved[i][name] = (xs, gs, half_row, h, a)

    def add_slot():
        k = len(slots)
        slots.append([held[k]] + [hop(held[k], s) for s in range(1, n_tensor)])

    def add(a, b):
        return (a.astype(F32) + b.astype(F32)).astype(BF16)

    def weight_pieces(k, fence=()):
        parts = list(saved[k].values())
        if fence:
            xs, gs, rows, h, a = parts[0]
            parts[0] = (xs, gs, rows, after(h, *fence), a)
        return expert_weight(parts, n_tensor, width)

    def hop_back(grads):
        return [hop(grads[s], n_tensor - s) for s in range(1, n_tensor)]

    def total_of(grads, got):
        return functools.reduce(jnp.add, [v.astype(F32) for v in [grads[0], *got]])

    def send_on(k, moving):
        total = totals[k]
        if moving is not None:
            total = add(total, moving)
        return ring(total)

    for _ in range(1, group):
        add_slot()
    slots, mlp_top, mlp_low = after((slots, mlp_top, mlp_low))
    x_top, y_low = plane(mlp_top, 1), plane(mlp_low, 2)
    run("near", 0)
    x_top, y_low, carry["near"] = after((x_top, y_low, carry["near"]))
    x_low, y_top = plane(mlp_low, 1), plane(mlp_top, 2)
    where["one"] = ([(x_top, 0), (y_low, 0)], [(grad_x, 0), (grad_y, 1)])
    run("one", 0)
    x_low, y_top, carry["one"], held[2] = after((x_low, y_top, carry["one"], held[2]))
    for _ in range(3, depth):
        held.append(ring(held[-1]))
    mlp_diag = [plane(x_top, 2), plane(y_low, 1)]
    where["two"] = ([(x_low, 0), (y_top, 0)], [(grad_x, 1), (grad_y, 0)])
    run("two", 0)
    mlp_diag, carry["two"] = after((mlp_diag, carry["two"]))
    add_slot()
    where["diag"] = ([(v, 0) for v in mlp_diag], [(v, 0) for v in grad_diag])
    run("diag", 0)
    slots, carry["diag"] = after((slots, carry["diag"]))
    for k in range(group, last, group):
        while len(slots) < k + group:
            add_slot()
        for name in ("near", "one", "two", "diag"):
            run(name, k)
    totals = {}
    order = list(range(1, depth)) + [0]
    early = order[: depth - group - 1]
    early_grads = {k: weight_pieces(k) for k in early}
    while len(slots) < depth:
        add_slot()
    slots[-1], early_grads = after((slots[-1], early_grads))
    rest = order[len(early) :]

    early_got = {k: hop_back(early_grads[k]) for k in early}
    run("diag", last)
    carry["diag"], early_grads, early_got = after((carry["diag"], early_grads, early_got))
    moving = None
    for k in early:
        totals[k] = total_of(early_grads[k], early_got[k]).astype(BF16)
        moving = send_on(k, moving)
    back_parts = [plane(v, m) for v, m in zip(carry["diag"][1], (1, 2))]
    run("one", last, [carry["diag"]])
    back_parts, carry["one"] = after((back_parts, carry["one"]))
    halves = [plane(v, m) for v, m in zip(carry["one"][1], (1, 2))]
    run("two", last, [carry["one"]])
    low_x, top_y = ((v.astype(F32) + p.astype(F32)).astype(BF16) for v, p in zip(carry["two"][1], back_parts[::-1]))
    halves, low_x, top_y = after((halves, low_x, top_y))
    others = [plane(low_x, 1), plane(top_y, 2)]
    run("near", last, [low_x, top_y])
    others, carry["near"], moving = after((others, carry["near"], moving))

    dy, d_gates, gain_two_all = turn_back(carry["near"][1], halves, others, mixed, grad_wide, gain_mlp)
    out_diag, dy = after((carry["diag"][0], dy))
    out_parts = [plane(v, m) for v, m in zip(out_diag, (1, 2))]
    dy_full = gather_rows(dy)
    late = {rest[0]: weight_pieces(rest[0], [dy])}
    dy_full, late, out_parts = after((dy_full, late, out_parts))
    d_gates = d_gates[:, :n_expert] + d_gates[:, LANES // 2 : LANES // 2 + n_expert]

    arrived = moving
    late_got = hop_back(late[rest[0]])
    out_halves = [plane(v, m) for v, m in zip(carry["one"][0], (1, 2))]
    do_t = jnp.einsum("td,cd->ct", dy_full, w_out, preferred_element_type=F32).astype(BF16)
    out_w_grad = [jnp.einsum("td,ct->dc", dy_full, o, preferred_element_type=F32).astype(BF16) for o in o_t]

    def backward(i, do_t):
        return attn_backward(q_t[i], k_t[i], v_t, do_t, lse[i], cos_t, sin_t, start, i * count, count)

    def weight_grads(ds):
        return [jnp.einsum("td,ct->dc", attn_in, d, preferred_element_type=F32).astype(BF16) for d in ds]

    def part(a, who, rows):
        return lax.dynamic_slice_in_dim(a, who * rows, rows, 0)

    p_at, z_at = lax.rem(e_at, PLANE), e_at // PLANE

    def plane_shares(a):
        quarter = a.shape[0] // PLANE
        return [plane(part(a, p_at ^ m, quarter), m) for m in range(1, PLANE)]

    def plane_sum(a, shares):
        total = part(a, p_at, a.shape[0] // PLANE).astype(F32)
        for v in shares:
            total = total + v.astype(F32)
        return total.astype(BF16)

    def swap(a, bit):
        pairs = [(i, i ^ (bit * PLANE)) for i in range(n_expert)]
        return lax.ppermute(a, "expert", pairs)

    bits = [1 << i for i in range(depth.bit_length() - 1)]

    def upper(bit):
        return (z_at // bit) % 2

    def z_cut(a, bit, tail=None):
        rows = a.shape[0] // 2
        stay, go = part(a, upper(bit), rows), part(a, 1 - upper(bit), rows)
        return stay, go if tail is None else jnp.concatenate([go, tail], axis=0)

    def z_join(a, got, bit):
        return jnp.where(upper(bit) == 0, jnp.concatenate([a, got], 0), jnp.concatenate([got, a], 0))

    first = jnp.concatenate(out_w_grad, axis=1)
    ds = []
    do_t, out_w_grad = after((do_t, out_w_grad))
    if parts == 2:
        ds.append(backward(0, do_t))
        ds[0], out_halves, do_t, late_got = after((ds[0], out_halves, do_t, late_got))
        first = jnp.concatenate(weight_grads(ds[0]) + out_w_grad, axis=1)

    def next_moving(k, got, arrived):
        total = total_of(late[k], got)
        if arrived is not None:
            total = total + arrived.astype(F32)
        return total.astype(BF16)

    moving = next_moving(rest[0], late_got, arrived)
    first, out_halves, moving, do_t = after((first, out_halves, moving, do_t))
    ring_on = [ring(moving[c]) for c in range(2)]
    first_sent = plane_shares(first)
    ds.append(backward(parts - 1, do_t))
    third = rest[1]
    late[third] = weight_pieces(third, [ds[-1]])
    first_sent, ring_on, ds, late = after((first_sent, ring_on, ds, late))

    second = jnp.concatenate(weight_grads(ds[-1]), axis=1)
    first = plane_sum(first, first_sent)
    stay, go = z_cut(first, bits[0])
    second, stay, go, ds = after((second, stay, go, ds))
    second_sent = plane_shares(second)
    got = swap(go, bits[0])
    ring_on.append(ring(moving[2]))
    late_got = hop_back(late[third])
    own_terms, *far_terms, dots = input_terms(
        t_at.reshape(1), tokens, gain_attn, ds, (w_query, key_matrix, value_matrix), n_tensor
    )
    dots = dots[:, 0]
    second_sent, got, ring_on, far_terms, dots, late_got = after((second_sent, got, ring_on, far_terms, dots, late_got))
    moving = next_moving(third, late_got, jnp.stack(ring_on))

    first = add(stay, got)
    out_two = [add(v, p) for v, p in zip(carry["two"][0], out_parts[::-1])]
    gain_two = cols_of(gain_two_all[0], t_at)
    far_gains = [cols_of(gain_two_all[0], peer(s)) for s in range(1, n_tensor)]
    cuts = [z_cut(first, bits[1])] if len(bits) > 1 else []
    cuts, far_terms, dots = after((cuts, far_terms, dots))
    far_terms = [hop(v, s) for s, v in enumerate(far_terms, 1)]
    far_dots = [hop(jnp.concatenate([dots, v]), s) for s, v in enumerate(far_gains, 1)]
    gots = [swap(go, bits[1]) for _, go in cuts]
    gots, far_terms, far_dots, out_two = after((gots, far_terms, far_dots, out_two))
    out_others = [plane(v, m) for v, m in zip(out_two, (1, 2))]
    second = plane_sum(second, second_sent)
    for (stay, _), got in zip(cuts, gots):
        first = add(stay, got)
    for bit in bits[2:]:
        stay, go = z_cut(first, bit)
        first = add(stay, swap(go, bit))
    gain_two = functools.reduce(jnp.add, [gain_two] + [v[n_tok:] for v in far_dots])
    far_dots = [v[:n_tok] for v in far_dots]

    d_attn_in = functools.reduce(jnp.add, [own_terms] + [v.astype(F32) for v in far_terms])
    all_dots = functools.reduce(jnp.add, [dots] + far_dots)
    normed_cols = cols_of(tokens, t_at).astype(F32) * inv_one
    scaled_one = d_attn_in * cols_of(gain_attn, t_at)
    d_norm_one = inv_one * (scaled_one - normed_cols * (all_dots / width)[:, None])
    grad_tokens = cols_of(dy_full, t_at).astype(F32) + d_norm_one
    gain_one = jnp.sum(d_attn_in * normed_cols, axis=0)
    wide = second.shape[1]
    gains = jnp.concatenate([gain_one, gain_two]).astype(BF16).reshape(-1, wide)
    gain_rows = gains.shape[0]
    gains = jnp.pad(gains, ((0, 16 - gain_rows), (0, 0)))
    grad_logits = gather_rows(gates * (d_gates - jnp.sum(gates * d_gates, axis=1, keepdims=True)))
    for i, bit in enumerate(bits):
        rows = second.shape[0] // 2
        stay, go = z_cut(second, bit, gains)
        back = bits[-1 - i]
        first, go = after((first, go))
        got, first_got = swap(go, bit), swap(first, back)
        got, first_got, out_others = after((got, first_got, out_others))
        second, gains = add(stay, got[:rows]), add(gains, got[rows:])
        first = z_join(first, first_got, back)
    first, second, moving = after((first, second, moving))
    first_all = [first] + [plane(first, m) for m in range(1, PLANE)]
    late[0] = weight_pieces(0, [first])
    for bit in bits[::-1]:
        second = z_join(second, swap(second, bit), bit)
    moving, second = after((moving, second))
    ring_on = [ring(moving[c]) for c in range(3)]
    rows = second.shape[0]
    second = jnp.concatenate([second, gains], axis=0)
    out_top, out_low = carry["near"][0]
    top_rows = out_top.astype(F32) + out_halves[0].astype(F32) + out_others[1].astype(F32)
    low_rows = out_low.astype(F32) + out_others[0].astype(F32) + out_halves[1].astype(F32)
    block_out = to_cols((mixed + jnp.concatenate([top_rows, low_rows], axis=0)).astype(BF16))
    second, block_out, first_all, ring_on[0], late[0] = after((second, block_out, first_all, ring_on[0], late[0]))
    late_got = hop_back(late[0])
    second_all = [second] + [plane(second, m) for m in range(1, PLANE)]
    own = total_of(late[0], late_got)
    final = [own[c] + ring_on[c].astype(F32) for c in range(2)]
    second_all, final = after((second_all, final))
    gains = functools.reduce(jnp.add, [v[rows : rows + gain_rows].astype(F32) for v in second_all]).reshape(-1)
    cuts = [w.shape[1] // parts for w in (w_query, key_matrix, value_matrix)]
    laid = lay_out(p_at.reshape(1), first_all, second_all, parts, cuts)
    grad_query, grad_key, grad_value, grad_out = laid
    grad_query, down_arrived = after((grad_query, ring_on[2]))
    final.append((own[2] + down_arrived.astype(F32)).T)
    return (
        block_out,
        grad_tokens,
        grad_logits,
        gains[:col_width],
        grad_query,
        grad_key,
        grad_value,
        grad_out,
        gains[col_width:],
        final[0][None],
        final[1][None],
        final[2][None],
    )


def solution(mesh):
    return jax.shard_map(
        body,
        mesh=mesh,
        in_specs=(
            P("expert", None),
            P("expert"),
            P("expert", None),
            P("expert", None),
            P(),
            P(None, "tensor"),
            P(None, "tensor"),
            P(None, "tensor"),
            P("tensor", None),
            P(),
            P("expert", None, "tensor"),
            P("expert", None, "tensor"),
            P("expert", "tensor", None),
            P("expert", "tensor"),
        ),
        out_specs=(
            P("expert", "tensor"),
            P("expert", "tensor"),
            P("expert", None),
            P("tensor"),
            P(None, "tensor"),
            P(None, "tensor"),
            P(None, "tensor"),
            P("tensor", None),
            P("tensor"),
            P("expert", None, "tensor"),
            P("expert", None, "tensor"),
            P("expert", "tensor", None),
        ),
        check_vma=False,
    )
```
